32 devices in a mesh: leaf: 32 (over z, y, x, core).
Axes of the slice: x: 2, y: 2, z: 4, core: 2. Of those that a mesh axis runs over, the one named last changes fastest.
Arguments:
- points: bfloat16 [64, 131072], P(None, 'leaf'), may hold values from -3 to 3
- charges: bfloat16 [16, 131072], P(None, 'leaf'), may hold values from -6 to 6
- leaf_order: int32 [131072], P('leaf'), may hold values from 0 to 4095, as said below
- near_owner: int32 [512, 8], P('leaf'), may hold values from 0 to 31, all different within a row; in each aligned block of 16 rows (0 to 15, 16 to 31, ...) at most 6 rows name the same one
- near_slot: int32 [512, 8], P('leaf'), may hold values from 0 to 15
- far_list: int32 [512, 16], P('leaf'), may hold values from 0 to 30
- far_count: int32 [512], P('leaf'), may hold values from 1 to 16
- leaf_interp: bfloat16 [512, 256, 128], P('leaf'), may hold values from -0.375 to 0.375
- leaf_skel: int32 [512, 128], P('leaf'), may hold values from 0 to 255, as said below
- inner_interp: bfloat16 [480, 256, 128], P('leaf'), may hold values from -0.375 to 0.375
- inner_skel: int32 [480, 128], P('leaf'), may hold values from 0 to 255, as said below
- top_interp: bfloat16 [30, 256, 128], replicated, may hold values from -0.375 to 0.375
- top_skel: int32 [30, 128], replicated, may hold values from 0 to 255, as said below
Outputs:
- potential: float32 [16, 131072], P(None, 'leaf')
The draws below stay inside these ranges and needn't reach their ends.
Inputs may be any that keep to these rules, and one draw needn't show every extreme that they name: `leaf_order`: each device's 4096 entries are a permutation of its point numbers. `near_owner`: a row names 8 different devices; over the rows of one device, no device is named more than 6 times. `leaf_skel`: the entries of a row are different. `inner_skel`: the entries of a row are different. `top_skel`: the entries of a row are different.
All inputs are finite; a program needn't handle non-finite values.
Results may differ from the reference program's by a relative error of at most 0.008.
Values may be sent and summed in bfloat16 or wider, within the bound.
No kernel may reach another device: no remote copies, remote signals or barrier semaphores. Data moves between devices by JAX's collectives and lax.ppermute only.
A program may use at most 128 MiB of HBM per device.

```python
import math
from functools import partial
import jax
import jax.numpy as jnp
import numpy as np
from jax import lax

DIM = 64
COLS = 16
LEAF = 256
SKEL = 128
NEAR = 8
FARL = 16
LEAVES_DEV = 16
PTS_DEV = 4096
NLEAVES = 512
NPTS = 131072
CAP = 6
INNER = 480
NTOP = 30
N_LEAF = 32


def one_row(row_key, pool_size, keep_count):
    return jax.random.permutation(row_key, pool_size)[:keep_count]


def distinct_rows(key, row_count, pool_size, keep_count):
    row_keys = jax.random.split(key, row_count)
    picked = jax.vmap(partial(one_row, pool_size=pool_size, keep_count=keep_count))(row_keys)
    return picked.astype(jnp.int32)


def draw_leaf_order(key, part):
    key = jax.random.fold_in(key, 5)
    return distinct_rows(key, NPTS // PTS_DEV, PTS_DEV, PTS_DEV).reshape(-1)


def draw_leaf_skel(key, part):
    key = jax.random.fold_in(key, 7)
    return distinct_rows(key, NLEAVES, LEAF, SKEL)


def draw_inner_skel(key, part):
    key = jax.random.fold_in(key, 9)
    return distinct_rows(key, INNER, 2 * SKEL, SKEL)


def draw_top_skel(key, part):
    key = jax.random.fold_in(key, 13)
    return distinct_rows(key, NTOP, 2 * SKEL, SKEL)


def with_ends(result, rng, low, top_value):
    shape = result.shape
    index_at = [jax.random.randint(jax.random.fold_in(rng, axis), (), 0, shape[axis]) for axis in range(len(shape))]
    result = result.at[tuple(index_at)].set(low)
    longest = shape.index(max(shape))
    index_at[longest] = (index_at[longest] + 1) % shape[longest]
    return result.at[tuple(index_at)].set(top_value)


def block_scale(rng, dims, pieces, least, top_value):
    gain, own = 1.0, jax.random.fold_in(rng, 6)
    for axis_at, parts in pieces:
        steps = jnp.exp(jax.random.uniform(jax.random.fold_in(own, axis_at), (parts,), jnp.float32, least / len(pieces), top_value / len(pieces)))
        gain = gain * jnp.repeat(steps, dims[axis_at] // parts).reshape([-1 if axis == axis_at else 1 for axis in range(len(dims))])
    return gain


def shared_out(rng, own, number, rows, count, top, reach, slope):
    sequence = jax.random.permutation(rng, count)
    heavy_load, usual = load_shares(count, rows * top, reach, slope, True), load_shares(count, rows * top, reach, slope, False)
    places = jnp.arange(count)

    def named(lengths, offset_by):
        used = int((lengths > 0).sum())
        fixed = max(1, used // 4)
        passed = fixed + (places - fixed + offset_by * (used - fixed)) % max(1, count - fixed)
        return jnp.zeros((count,), jnp.int32).at[sequence[jnp.where(places < fixed, places, passed)]].set(jnp.asarray(lengths, jnp.int32))

    lengths = jnp.where(number % 4 == 0, named(heavy_load, number // 4), named(usual, number - number // 4 - 1))
    mixed = jax.random.permutation(jax.random.fold_in(own, 3), count)
    donor, taker = mixed[0:count // 2 * 2:2], mixed[1:count // 2 * 2:2]
    room = jnp.minimum(lengths[donor] - 1, reach - lengths[taker]) // 2
    room = jnp.where((donor == sequence[0]) | (taker == sequence[0]) | (lengths[taker] == 0), 0, jnp.maximum(room, 0))
    passed = jax.random.randint(jax.random.fold_in(own, 4), (count // 2,), 0, 1 << 20) % (room + 1)
    lengths = lengths.at[donor].add(-passed).at[taker].add(passed)
    items = jnp.searchsorted(jnp.cumsum(lengths), jnp.arange(rows * top), side="right").astype(jnp.int32)
    table = items.reshape(top, rows).T
    table = table[jax.random.permutation(jax.random.fold_in(own, 1), rows)]
    offset_by = jax.random.randint(jax.random.fold_in(own, 2), (rows, 1), 0, top)
    return jnp.take_along_axis(table, (jnp.arange(top)[None, :] + offset_by) % top, axis=1)


def load_shares(amount, total, bound, skew, full):
    weights = [(1 << 20) // math.isqrt(rank ** skew) + 1 for rank in range(1, amount + 1)]
    largest = bound if full else min(bound, max(-(-total // amount), total * weights[0] // sum(weights)))
    least = 1 if total - largest >= amount - 1 else 0
    holding, spare = [largest] + [least] * (amount - 1), total - largest - least * (amount - 1)
    while spare > 0:
        candidates = [i for i in range(1, amount) if holding[i] < largest] or [i for i in range(1, amount) if holding[i] < bound]
        whole, left = sum([weights[i] for i in candidates]), spare
        for i in candidates:
            extra = min(bound - holding[i], max(1, left * weights[i] // whole), spare)
            holding[i] = holding[i] + extra
            spare = spare - extra
    return np.array(holding)


def noise(stream_key, dims, spread, reach, shards=(), held_as=jnp.bfloat16):
    drawn = jax.random.normal(stream_key, dims, jnp.float32) * spread
    if len(shards) > 0:
        drawn = block_scale(stream_key, dims, shards, -0.22, 0.18) * drawn
    return jnp.clip(drawn, min=-reach, max=reach).astype(held_as)


def setup_inputs(seed: int = 0) -> dict:
    streams_of = jax.random.split(jax.random.key(seed), 14)
    points = noise(streams_of[0], (DIM, NPTS), 0.5, 3.0, ((1, 32),))
    charges = noise(streams_of[1], (COLS, NPTS), 1.0, 6.0, ((1, 32),))
    leaf_order = draw_leaf_order(jax.random.fold_in(streams_of[13], 71), 0)
    near_owner_keys = jax.random.split(jax.random.fold_in(streams_of[3], 1), NLEAVES // LEAVES_DEV)
    near_owner_turns = jax.random.permutation(jax.random.fold_in(streams_of[3], 3), NLEAVES // LEAVES_DEV)
    near_owner = jax.vmap(lambda own, number: shared_out(jax.random.fold_in(streams_of[3], 2), own, number, LEAVES_DEV, N_LEAF, NEAR, CAP, 2))(near_owner_keys, near_owner_turns).reshape((NLEAVES, NEAR))
    near_slot = with_ends(jax.random.randint(streams_of[4], (NLEAVES, NEAR), 0, LEAVES_DEV), jax.random.fold_in(streams_of[4], 1), 0, LEAVES_DEV - 1).astype(jnp.int32)
    far_list = with_ends(jax.random.randint(streams_of[5], (NLEAVES, FARL), 0, 2 * LEAVES_DEV - 1), jax.random.fold_in(streams_of[5], 1), 0, (2 * LEAVES_DEV - 1) - 1).astype(jnp.int32)
    far_count = with_ends(jax.random.randint(streams_of[6], (NLEAVES,), 1, FARL + 1), jax.random.fold_in(streams_of[6], 1), 1, FARL).astype(jnp.int32)
    leaf_interp = noise(streams_of[7], (NLEAVES, LEAF, SKEL), LEAF ** -0.5, 0.375, ((0, 32),))
    leaf_skel = draw_leaf_skel(jax.random.fold_in(streams_of[13], 71), 0)
    inner_interp = noise(streams_of[9], (INNER, 2 * SKEL, SKEL), (2 * SKEL) ** -0.5, 0.375, ((0, 32),))
    inner_skel = draw_inner_skel(jax.random.fold_in(streams_of[13], 71), 0)
    top_interp = noise(streams_of[11], (NTOP, 2 * SKEL, SKEL), (2 * SKEL) ** -0.5, 0.375)
    top_skel = draw_top_skel(jax.random.fold_in(streams_of[13], 71), 0)
    return {"points": points, "charges": charges, "leaf_order": leaf_order, "near_owner": near_owner, "near_slot": near_slot, "far_list": far_list, "far_count": far_count, "leaf_interp": leaf_interp, "leaf_skel": leaf_skel, "inner_interp": inner_interp, "inner_skel": inner_skel, "top_interp": top_interp, "top_skel": top_skel}


width_sq = 8.0


def kernel_tile(sources, targets):
    source_norm = jnp.sum(jnp.square(sources.astype(jnp.float32)), axis=0)
    target_norm = jnp.sum(jnp.square(targets.astype(jnp.float32)), axis=0)
    cross = lax.dot_general(sources, targets, (((0,), (0,)), ((), ())), preferred_element_type=jnp.float32)
    distance = source_norm[:, None] + target_norm[None, :] - 2.0 * cross
    return jnp.exp(-distance / width_sq).astype(jnp.bfloat16)


def combine_pairs(child_coords, child_loads, skel_picks, interp_rows):
    half_count = child_coords.shape[0] // 2
    paired_coords = child_coords.reshape((half_count, 2) + child_coords.shape[1:])
    paired_loads = child_loads.reshape((half_count, 2) + child_loads.shape[1:])
    joined_coords = jnp.concatenate([paired_coords[:, 0], paired_coords[:, 1]], axis=2)
    joined_loads = jnp.concatenate([paired_loads[:, 0], paired_loads[:, 1]], axis=2)
    parent_coords = jnp.take_along_axis(joined_coords, skel_picks[:, None, :], axis=2)
    parent_loads = jnp.einsum("ncs,nsk->nck", joined_loads.astype(jnp.float32), interp_rows.astype(jnp.float32))
    return parent_coords, parent_loads.astype(jnp.bfloat16)


def reference(points, charges, leaf_order, near_owner, near_slot, far_list, far_count, leaf_interp, leaf_skel, inner_interp, inner_skel, top_interp, top_skel):
    block_start = (jnp.arange(NPTS, dtype=jnp.int32) // PTS_DEV) * PTS_DEV
    order = block_start + leaf_order
    coords = jnp.take(points, order, axis=1)
    charge_rows = jnp.take(charges, order, axis=1)
    leaf_coords = jnp.transpose(coords.reshape(DIM, NLEAVES, LEAF), (1, 0, 2))
    leaf_charges = jnp.transpose(charge_rows.reshape(COLS, NLEAVES, LEAF), (1, 0, 2))
    source_ids = near_owner * LEAVES_DEV + near_slot

    def near_leaf(index):
        target = leaf_coords[index]
        total = jnp.dot(leaf_charges[index], kernel_tile(target, target), preferred_element_type=jnp.float32)
        for near_index in range(NEAR):
            other = source_ids[index, near_index]
            total = total + jnp.dot(leaf_charges[other], kernel_tile(leaf_coords[other], target), preferred_element_type=jnp.float32)
        return total

    near_part = lax.map(near_leaf, jnp.arange(NLEAVES, dtype=jnp.int32))

    skel_coords = jnp.take_along_axis(leaf_coords, leaf_skel[:, None, :], axis=2)
    skel_loads = jnp.einsum("ncs,nsk->nck", leaf_charges.astype(jnp.float32), leaf_interp.astype(jnp.float32)).astype(jnp.bfloat16)
    coord_levels = [skel_coords.reshape(N_LEAF, LEAVES_DEV, DIM, SKEL)]
    load_levels = [skel_loads.reshape(N_LEAF, LEAVES_DEV, COLS, SKEL)]
    inner_picks = inner_skel.reshape(N_LEAF, LEAVES_DEV - 1, SKEL)
    inner_rows = inner_interp.reshape(N_LEAF, LEAVES_DEV - 1, 2 * SKEL, SKEL)
    here_coords = skel_coords
    here_loads = skel_loads
    node_count = LEAVES_DEV
    height = 1
    while node_count > 1:
        offset = LEAVES_DEV - (LEAVES_DEV >> (height - 1))
        half_count = node_count // 2
        picks_now = inner_picks[:, offset:offset + half_count].reshape(-1, SKEL)
        rows_now = inner_rows[:, offset:offset + half_count].reshape(-1, 2 * SKEL, SKEL)
        here_coords, here_loads = combine_pairs(here_coords, here_loads, picks_now, rows_now)
        coord_levels.append(here_coords.reshape(N_LEAF, half_count, DIM, SKEL))
        load_levels.append(here_loads.reshape(N_LEAF, half_count, COLS, SKEL))
        node_count = half_count
        height = height + 1
    node_coords = jnp.concatenate(coord_levels, axis=1)
    node_loads = jnp.concatenate(load_levels, axis=1)

    live = (jnp.arange(FARL, dtype=jnp.int32)[None, :] < far_count[:, None]).astype(jnp.bfloat16)

    def far_leaf(index):
        device_index = index // LEAVES_DEV
        node_ids = far_list[index]
        chosen_coords = node_coords[device_index][node_ids]
        chosen_loads = node_loads[device_index][node_ids] * live[index][:, None, None]
        kernel_block = jax.vmap(kernel_tile, in_axes=(0, None))(chosen_coords, leaf_coords[index])
        return jnp.einsum("fck,fkt->ct", chosen_loads.astype(jnp.float32), kernel_block.astype(jnp.float32))

    far_part = lax.map(far_leaf, jnp.arange(NLEAVES, dtype=jnp.int32))

    level_count = N_LEAF.bit_length() - 1
    device_coords = jnp.transpose(coords.reshape(DIM, N_LEAF, PTS_DEV), (1, 0, 2))
    here_coords = node_coords[:, -1]
    here_loads = node_loads[:, -1]
    top_part = jnp.zeros((N_LEAF, COLS, PTS_DEV), jnp.float32)

    def top_term(bundle):
        targets, sibling_coords, sibling_loads = bundle
        return jnp.dot(sibling_loads, kernel_tile(sibling_coords, targets), preferred_element_type=jnp.float32)

    for height in range(level_count):
        partner = (jnp.arange(N_LEAF, dtype=jnp.int32) >> height) ^ 1
        top_part = top_part + lax.map(top_term, (device_coords, here_coords[partner], here_loads[partner]))
        if height + 1 < level_count:
            offset = N_LEAF - (N_LEAF >> height)
            half_count = here_coords.shape[0] // 2
            here_coords, here_loads = combine_pairs(here_coords, here_loads, top_skel[offset:offset + half_count], top_interp[offset:offset + half_count])

    nearby = near_part + far_part
    potential = jnp.transpose(nearby, (1, 0, 2)).reshape(COLS, NPTS) + jnp.transpose(top_part, (1, 0, 2)).reshape(COLS, NPTS)
    return potential
```

```python
import functools

import jax
import jax.numpy as jnp
from jax import lax
from jax.experimental import pallas as pl
from jax.experimental.pallas import tpu as pltpu
from jax.sharding import PartitionSpec as P

TARGET_BITS = (1, 3)
FAR_UNROLL = 8
NEAR_STEPS = (8, 4, 2)
DUMMY = 1 << 30
PHASE_BIT = 24
CODE = (1 << PHASE_BIT) - 1
VMEM_LIMIT = 24 * 1024 * 1024
FIRST_LIMIT = 58 * 1024 * 1024
PHASES = 3
bf16 = jnp.bfloat16
f32 = jnp.float32

VMEM = pl.BlockSpec(memory_space=pltpu.VMEM)
SMEM = pl.BlockSpec(memory_space=pltpu.SMEM)
ANY = pl.BlockSpec(memory_space=pl.ANY)
HBM = pl.BlockSpec(memory_space=pltpu.HBM)


def params(limit=VMEM_LIMIT):
    return pltpu.CompilerParams(vmem_limit_bytes=limit)


def cost():
    return pl.CostEstimate(flops=1, bytes_accessed=1, transcendentals=0)


def dot(a, b):
    return lax.dot_general(a, b, (((1,), (0,)), ((), ())), preferred_element_type=f32)


def dot_nt(a, b):
    return lax.dot_general(a, b, (((1,), (1,)), ((), ())), preferred_element_type=f32)


def split3(value):
    hi = value.astype(bf16).astype(f32)
    rest = value - hi
    mid = rest.astype(bf16).astype(f32)
    return hi, mid, rest - mid


def norm_row(coords):
    wide = coords.astype(f32)
    return jnp.sum(wide * wide, axis=0, keepdims=True) * 0.125


def extra_rows(norms, first):
    hi, mid, lo = split3(-norms)
    row = lax.broadcasted_iota(jnp.int32, (16, norms.shape[1]), 0)
    one_at = 3 - first
    out = jnp.where((row >= one_at) & (row < one_at + 3), 1.0, 0.0)
    out = jnp.where(row == first, hi, out)
    out = jnp.where(row == first + 1, mid, out)
    return jnp.where(row == first + 2, lo, out)


def source_matrix(coords, norms):
    width = coords.shape[1]
    extra = extra_rows(norms, 0).astype(bf16)
    return jnp.concatenate([coords, extra, jnp.zeros((48, width), bf16)], axis=0)


def target_matrix(coords, norms):
    width = coords.shape[1]
    extra = extra_rows(norms, 3)
    wide = jnp.concatenate(
        [coords.astype(f32) * 0.25, extra, jnp.zeros((48, width), f32)], axis=0
    )
    return jnp.transpose(wide).astype(bf16)


def placed(loads, place):
    zero = jnp.zeros_like(loads)
    return jnp.concatenate(
        [jnp.where(place == k, loads, zero) for k in range(8)], axis=0
    )


def onehot(picks, size):
    row = lax.broadcasted_iota(jnp.int32, (size, picks.shape[1]), 0)
    return jnp.where(row == picks, 1.0, 0.0).astype(bf16)


def combine(left, right, picks, interp):
    both = jnp.concatenate([left, right], axis=1)
    coords = dot(both[:64], onehot(picks, 256)).astype(bf16)
    load = dot(both[64:], interp).astype(bf16)
    return jnp.concatenate([coords, load], axis=0)


def first_kernel(
    order, points_in, charges_in, owner_in, slot_in,
    leaf_interp_in, leaf_skel_in, inner_interp_in, inner_skel_in, top_interp, top_skel,
    src_out, tgt_out, cols_out, loads_out, rows_out, norms_out, mine_out, interps_out, skels_out,
    points, charges, owner, slot, unsorted, buffer0, buffer1, src, tgt, cols, loads, rows, norms,
    joined, root, leaf_interp, leaf_skel, inner_interp, inner_skel, sems,
):
    count = points.shape[1]
    chunks = 4
    width = count // chunks
    begun = []

    def begin(a, b):
        copy = pltpu.make_async_copy(a, b, sems.at[len(begun)])
        copy.start()
        begun.append(copy)
        return copy

    parts = [begin(charges_in, charges)]
    for c in range(chunks):
        at = pl.ds(c * width, width)
        parts.append(begin(points_in.at[:, at], points.at[:, at]))
    near_lists = [begin(owner_in, owner), begin(slot_in, slot)]
    needed = [
        begin(leaf_skel_in, leaf_skel),
        begin(leaf_interp_in, leaf_interp),
        begin(inner_skel_in, inner_skel),
        begin(inner_interp_in, inner_interp),
    ]
    rest = []
    path = path_rows()
    for k in range(interps_out.shape[0]):
        rest.append(begin(top_interp.at[path[k]], interps_out.at[k]))
        rest.append(begin(top_skel.at[pl.ds(path[k], 1)], skels_out.at[k]))

    parts[0].wait()
    for c in range(count // 128):
        at = slice(c * 128, (c + 1) * 128)
        if c * 128 % width == 0:
            parts[1 + c * 128 // width].wait()
        block = jnp.concatenate(
            [
                points[:, at].astype(f32),
                charges[:, at].astype(f32),
                jnp.zeros((48, 128), f32),
            ],
            axis=0,
        )
        unsorted[at, :] = jnp.transpose(block)

    leaves = src.shape[0]
    first_node = 2 * leaves
    lane = lax.broadcasted_iota(jnp.int32, (256, 128), 1)

    def finish(node, both):
        joined[node] = both
        cols[first_node + node] = source_matrix(both[:64], norm_row(both[:64]))
        loads[first_node + node] = both[64:]

    def copy_rows(pair, buffer):
        base = pl.multiple_of(pair * 512, 512)
        for u in range(512):
            buffer[u : u + 1, :] = unsorted[pl.ds(order[base + u], 1), :]

    def process(pair, buffer):
        even = buffer[:256]
        odd = buffer[256:]
        both = jnp.where(lane < 64, even, pltpu.roll(odd, 64, 1))
        tgt[pl.ds(pl.multiple_of(pair * 256, 256), 256), :] = (both * 0.25).astype(bf16)
        for k, mine in enumerate((even, odd)):
            i = 2 * pair + k
            both = jnp.transpose(mine)[:80].astype(bf16)
            src[i] = both
            coords, load = both[:64], both[64:]
            norm = norm_row(coords)
            norms[i] = norm
            rows[i] = target_matrix(coords, norm)
            matrix = source_matrix(coords, norm)
            for half in range(2):
                cols[2 * i + half] = matrix[:, half * 128 : half * 128 + 128]
                loads[2 * i + half] = load[:, half * 128 : half * 128 + 128]
            picked = dot(coords, onehot(leaf_skel[pl.ds(i, 1), :], 256)).astype(bf16)
            value = dot(load, leaf_interp[i]).astype(bf16)
            finish(i, jnp.concatenate([picked, value], axis=0))

    for copy in needed:
        copy.wait()

    def two_pairs(i, carry):
        copy_rows(2 * i, buffer0)
        process(jnp.maximum(2 * i - 1, 0), buffer1)
        copy_rows(2 * i + 1, buffer1)
        process(2 * i, buffer0)
        return carry

    lax.fori_loop(0, leaves // 4, two_pairs, 0)
    process(leaves // 2 - 1, buffer1)
    for copy in near_lists:
        copy.wait()
    near = jnp.concatenate([owner[...].astype(f32), slot[...].astype(f32)], axis=0)
    blank = jnp.zeros((near.shape[0], 128 - near.shape[1]), f32)
    tgt[count // 2 :, :] = jnp.concatenate([near, blank], axis=1).astype(bf16)
    rest += [begin(src, src_out), begin(tgt, tgt_out), begin(src, mine_out.at[pl.ds(0, leaves)])]
    rest += [begin(rows, rows_out), begin(norms, norms_out)]
    tiles = pl.ds(0, 3 * leaves)
    rest += [begin(cols.at[tiles], cols_out.at[tiles])]
    first, half = 0, leaves // 2
    number, row = leaves, 0
    while half > 0:
        for j in range(half):
            left = joined[first + 2 * j]
            right = joined[first + 2 * j + 1]
            finish(number, combine(left, right, inner_skel[row : row + 1, :], inner_interp[row]))
            number, row = number + 1, row + 1
        first = first + 2 * half
        half = half // 2
    node = joined[2 * leaves - 2]
    root[...] = jnp.concatenate([node, jnp.zeros_like(node)], axis=1)
    last = cols.shape[0] - 1
    cols[last] = jnp.zeros((128, 128), bf16)
    loads[last] = jnp.zeros((16, 128), bf16)
    inner_tiles = pl.ds(3 * leaves, leaves)
    rest += [begin(root, mine_out.at[leaves]), begin(loads, loads_out)]
    rest += [begin(cols.at[inner_tiles], cols_out.at[inner_tiles])]
    for copy in rest:
        copy.wait()


def path_rows():
    devices = lax.axis_size("leaf")
    device = lax.axis_index("leaf")
    bits = devices.bit_length() - 1
    return [devices - (devices >> (h - 1)) + (device >> h) for h in range(1, bits)]


def first_part(points, charges, order, owner, slot, *tables):
    count = points.shape[1]
    leaves = count // 256
    tiles = 4 * leaves
    steps = len(path_rows())
    leaf_interp, leaf_skel, inner_interp, inner_skel = tables[:4]
    src = (leaves, 80, 256)
    tgt = (count // 2 + 2 * owner.shape[0], 128)
    cols = (tiles, 128, 128)
    loads = (tiles, 16, 128)
    rows = (leaves, 256, 128)
    norms = (leaves, 1, 256)
    shapes = [
        (src, bf16),
        (tgt, bf16),
        (cols, bf16),
        (loads, bf16),
        (rows, bf16),
        (norms, f32),
        ((leaves + 1, 80, 256), bf16),
        ((steps, 256, 128), bf16),
        ((steps, 1, 128), jnp.int32),
    ]
    held = [
        (points.shape, bf16),
        (charges.shape, bf16),
        (owner.shape, jnp.int32),
        (slot.shape, jnp.int32),
        ((count, 128), f32),
        ((512, 128), f32),
        ((512, 128), f32),
    ]
    held += shapes[:6]
    held += [((2 * leaves - 1, 80, 128), bf16), ((80, 256), bf16)]
    held += [(table.shape, table.dtype) for table in tables[:4]]
    return pl.pallas_call(
        first_kernel,
        out_shape=tuple(jax.ShapeDtypeStruct(*shape) for shape in shapes),
        in_specs=[SMEM] + [ANY] * 10,
        out_specs=(ANY,) * 9,
        scratch_shapes=[pltpu.VMEM(*shape) for shape in held]
        + [pltpu.SemaphoreType.DMA((20 + 2 * steps,))],
        compiler_params=params(FIRST_LIMIT),
        cost_estimate=cost(),
        name="order_and_subtree",
    )(order, points, charges, owner, slot, *tables)


def far_kernel(*refs, first_leaf, n_leaves, n_ids):
    codes = refs[:n_ids]
    far_list, far_count, cols_in, loads_in, rows_in, acc = refs[n_ids : 6 + n_ids]
    lists = refs[6 + n_ids : -5]
    cols, loads, rows, tiles, sems = refs[-5:]
    leaves = rows.shape[0]
    width = far_list.shape[1]
    first_node = 2 * leaves
    empty = cols.shape[0] - 1
    mine = pl.ds(first_leaf, n_leaves)
    my_tiles = pl.ds(2 * first_leaf, 2 * n_leaves)
    nodes = pl.ds(first_node, cols.shape[0] - first_node)
    copies = [
        pltpu.make_async_copy(rows_in.at[mine], rows.at[mine], sems.at[0]),
        pltpu.make_async_copy(cols_in.at[my_tiles], cols.at[my_tiles], sems.at[1]),
        pltpu.make_async_copy(loads_in, loads, sems.at[2]),
        pltpu.make_async_copy(cols_in.at[nodes], cols.at[nodes], sems.at[3]),
    ]
    for copy in copies:
        copy.start()

    def list_leaf(k, count):
        i = first_leaf + k
        tiles[count] = (i << 16) | ((2 * i) << 8) | (2 * i + 1)
        count = count + 1
        used = far_count[i]
        for k in range(0, width, 2):
            first = far_list[i, k] + first_node
            second = jnp.where(k + 1 < used, far_list[i, k + 1] + first_node, empty)
            tiles[count] = (i << 16) | (first << 8) | second
            count = count + (k < used).astype(jnp.int32)
        return count

    count = lax.fori_loop(0, n_leaves, list_leaf, 0)
    for u in range(FAR_UNROLL):
        tiles[count + u] = (empty << 8) | empty

    def step(g, carry):
        values, weights = [], []
        for u in range(FAR_UNROLL):
            packed = tiles[g * FAR_UNROLL + u]
            leaf = packed >> 16
            first = (packed >> 8) & 255
            second = packed & 255
            matrix = jnp.concatenate([cols[first], cols[second]], axis=1)
            load = jnp.concatenate([loads[first], loads[second]], axis=1)
            values.append(jnp.exp(dot(rows[leaf], matrix)).astype(bf16))
            weights.append(placed(load, leaf & 7))
        acc[...] += dot_nt(jnp.concatenate(values, axis=1), jnp.concatenate(weights, axis=1))
        return carry

    acc[...] = jnp.zeros_like(acc)
    for k in range(n_ids):
        list_pairs(codes[k], lists[PHASES * k : PHASES * k + PHASES])
    for copy in copies:
        copy.wait()
    lax.fori_loop(0, lax.div(count + FAR_UNROLL - 1, FAR_UNROLL), step, 0)


def list_pairs(codes, tables):
    per_leaf, leaves = codes.shape
    for g in range(leaves // 8):
        counts = [jnp.int32(0)] * len(tables)
        for j in range(8):
            for u in range(per_leaf):
                value = codes[u, g * 8 + j]
                for p, table in enumerate(tables):
                    if table is None:
                        continue
                    table[g, 1 + counts[p]] = value & CODE
                    counts[p] = counts[p] + ((value >> (PHASE_BIT + p)) & 1)
        for p, table in enumerate(tables):
            if table is None:
                continue
            table[g, 1 + counts[p]] = DUMMY
            table[g, 0] = (counts[p] + 1) & ~1


def pair_table(leaves):
    return jax.ShapeDtypeStruct((leaves // 8, 128), jnp.int32)


def self_and_far(codes, far_list, far_count, cols, loads, rows, call, calls):
    leaves = rows.shape[0]
    width = far_list.shape[1]
    n_leaves = leaves // calls
    out = pl.pallas_call(
        functools.partial(
            far_kernel, first_leaf=call * n_leaves, n_leaves=n_leaves, n_ids=len(codes)
        ),
        out_shape=(jax.ShapeDtypeStruct((256, 128), f32),) + (pair_table(leaves),) * (PHASES * len(codes)),
        in_specs=[SMEM] * (2 + len(codes)) + [ANY] * 3,
        out_specs=(VMEM,) + (SMEM,) * (PHASES * len(codes)),
        scratch_shapes=[
            pltpu.VMEM(cols.shape, bf16),
            pltpu.VMEM(loads.shape, bf16),
            pltpu.VMEM(rows.shape, bf16),
            pltpu.SMEM((n_leaves * (1 + width // 2) + 1 + FAR_UNROLL,), jnp.int32),
            pltpu.SemaphoreType.DMA((4,)),
        ],
        compiler_params=params(FIRST_LIMIT),
        cost_estimate=cost(),
        name=f"self_and_far{call}",
    )(*codes, far_list, far_count, cols, loads, rows)
    return out[0], [out[1 + PHASES * k : 1 + PHASES * k + PHASES] for k in range(len(codes))]


def near_kernel(*refs, n_sources, n_targets, n_lists, phase):
    refs = list(refs)

    def take(n):
        taken = refs[:n]
        del refs[:n]
        return taken

    makes = phase < PHASES - 1
    (codes,) = take(1) if makes else (None,)
    lists = take(n_lists)
    target_parts = take(n_targets)
    source_parts = take(n_sources)
    before = take(phase > 0)
    outs = take(n_targets) if not makes else []
    (acc,) = take(1) if makes else (None,)
    tables = take(PHASES - 1 - phase) if makes else []
    sources, targets, sems, table, flat, steps = take(6)
    if not makes:
        (acc,) = refs
    leaves = source_parts[0].shape[0]
    size = leaves * 128
    copies = []

    def begin(part, place):
        copies.append(pltpu.make_async_copy(part, place, sems.at[len(copies)]))
        copies[-1].start()

    done = 0
    for part in before:
        done = part.shape[0]
        begin(part, acc.at[pl.ds(0, done)])
    for k, part in enumerate(target_parts):
        begin(part.at[pl.ds(0, size)], targets.at[pl.ds(k * size, size)])
    for k, part in enumerate(source_parts):
        begin(part.at[pl.ds(0, leaves)], sources.at[pl.ds(k * leaves, leaves)])
    if done < acc.shape[0]:
        acc[done:] = jnp.zeros((acc.shape[0] - done,) + acc.shape[1:], f32)
    if makes:
        if phase > 0:
            list_pairs(codes, [None] * phase + [table] + tables)
            lists = lists + [table]
        else:
            list_pairs(codes, [None] + tables)

    counts = [jnp.int32(0)] * len(NEAR_STEPS)
    base = jnp.int32(0)
    for number, pairs in enumerate(lists):
        for row in range(pairs.shape[0]):
            group = number * pairs.shape[0] + row
            used = pairs[row, 0]

            def copy_pair(i, at, pairs=pairs, row=row, group=group):
                flat[at + i] = pairs[row, 1 + i] | (group << 19)
                return at

            lax.fori_loop(0, used, copy_pair, base)
            start = base
            for k, size in enumerate(NEAR_STEPS):
                if k == 0:
                    whole = lax.div(used, size)

                    def note(i, count, start=start, size=size):
                        steps[0, count + i] = start + i * size
                        return count

                    lax.fori_loop(0, whole, note, counts[0])
                    counts[0] = counts[0] + whole
                    start = start + whole * size
                else:
                    steps[k, counts[k]] = start
                    has = jnp.where((used & size) > 0, 1, 0)
                    counts[k] = counts[k] + has
                    start = start + has * size
            base = base + used

    for copy in copies:
        copy.wait()

    for k, size in enumerate(NEAR_STEPS):

        def step(i, carry, k=k, size=size):
            start = steps[k, i]
            values, weights = [], []
            group = (flat[start] >> 19) & 31
            for u in range(size):
                packed = flat[start + u]
                target = (packed >> 16) & 7
                source = packed & 65535
                place = jnp.where(packed < DUMMY, target, 8)
                odd = target & 1
                both = sources[source]
                coords = both[:64]
                zero = jnp.zeros_like(coords)
                matrix = jnp.concatenate(
                    [jnp.where(odd == 0, coords, zero), jnp.where(odd == 1, coords, zero)],
                    axis=0,
                )
                at = pl.multiple_of(group * 1024 + (target >> 1) * 256, 256)
                value = dot(targets[pl.ds(at, 256), :], matrix) - norm_row(coords)
                values.append(jnp.exp(value).astype(bf16))
                weights.append(placed(both[64:], place))
            acc[group] += dot_nt(jnp.concatenate(values, axis=1), jnp.concatenate(weights, axis=1))
            return carry

        lax.fori_loop(0, counts[k], step, 0)

    each = acc.shape[0] // n_targets
    for k, out in enumerate(outs):
        out[...] = acc[k * each : (k + 1) * each].astype(bf16)


def near(phase, lists, targets, sources, codes=None, before=None):
    n_sources, n_targets = len(sources), len(targets)
    leaves = min(source.shape[0] for source in sources)
    sums = jax.ShapeDtypeStruct((n_targets * leaves // 8, 256, 128), f32)
    part = jax.ShapeDtypeStruct((leaves // 8, 256, 128), bf16)
    makes = phase < PHASES - 1
    args = ([codes] if makes else []) + list(lists) + list(targets) + list(sources)
    args += [] if before is None else [before]
    n_smem = len(lists) + makes
    n_tables = PHASES - 1 - phase
    if makes:
        out_shape = (sums,) + (pair_table(leaves),) * n_tables
        out_specs = (VMEM,) + (SMEM,) * n_tables
    else:
        out_shape, out_specs = (part,) * n_targets, (VMEM,) * n_targets
    scratch = [
        pltpu.VMEM((n_sources * leaves, 80, 256), bf16),
        pltpu.VMEM((n_targets * leaves * 128, 128), bf16),
        pltpu.SemaphoreType.DMA((n_sources + n_targets + 1,)),
        pltpu.SMEM(pair_table(leaves).shape, jnp.int32),
        pltpu.SMEM((n_targets * leaves * 8,), jnp.int32),
        pltpu.SMEM((len(NEAR_STEPS), n_targets * leaves), jnp.int32),
    ]
    if not makes:
        scratch.append(pltpu.VMEM(sums.shape, f32))
    return pl.pallas_call(
        functools.partial(
            near_kernel, n_sources=n_sources, n_targets=n_targets, n_lists=len(lists), phase=phase
        ),
        out_shape=out_shape,
        in_specs=[SMEM] * n_smem + [ANY] * (len(args) - n_smem),
        out_specs=out_specs,
        scratch_shapes=scratch,
        compiler_params=params(),
        cost_estimate=cost(),
        name=f"near{phase}",
    )(*args)


def ordered(first, second, test):
    return jnp.where(test, first, second), jnp.where(test, second, first)


def climb_kernel(me, own, other, skels, interps, parent, *, height, row):
    sibling = other[0, :, :128] if len(other.shape) == 3 else other[...]
    left, right = ordered(own[0, :, :128] if len(own.shape) == 3 else own[...], sibling, ((me[0] >> height) & 1) == 0)
    parent[...] = combine(left, right, skels[row], interps[row])


def last_block(value):
    if value.ndim == 2:
        return VMEM
    blocks = value.shape[0]
    return pl.BlockSpec((1,) + value.shape[1:], lambda i: (blocks - 1, 0, 0))


def climb(me, own, other, skels, interps, height, row):
    return pl.pallas_call(
        functools.partial(climb_kernel, height=height, row=row),
        grid=(1,),
        out_shape=jax.ShapeDtypeStruct((80, 128), bf16),
        in_specs=[SMEM, last_block(own), last_block(other), VMEM, VMEM],
        out_specs=VMEM,
        compiler_params=params(),
        cost_estimate=cost(),
        name=f"climb{height}",
    )(me, own, other, skels, interps)


def top_kernel(*refs):
    parts, (rows, acc, cols, loads) = refs[:-4], refs[-4:]
    for t, part in enumerate(parts):
        node = part[0, :, :128] if len(part.shape) == 3 else part[...]
        cols[:, t * 128 : (t + 1) * 128] = source_matrix(node[:64], norm_row(node[:64]))
        loads[:, t * 128 : (t + 1) * 128] = jnp.concatenate([node[64:]] * 8, axis=0)
    lane = lax.broadcasted_iota(jnp.int32, (256, 128), 1) >> 4

    def two_leaves(i, carry):
        both = rows[pl.ds(2 * i, 2)].reshape(512, 128)
        value = jnp.exp(dot(both, cols[...])).astype(bf16)
        result = dot_nt(value, loads[...])
        group = lax.div(i, 4)
        place = (2 * i) & 7
        acc[group] += jnp.where(lane == place, result[:256], 0.0) + jnp.where(
            lane == place + 1, result[256:], 0.0
        )
        return carry

    acc[...] = jnp.zeros_like(acc)
    lax.fori_loop(0, rows.shape[0] // 2, two_leaves, 0, unroll=2)


def top(parts, rows):
    levels = len(parts)
    return pl.pallas_call(
        top_kernel,
        out_shape=jax.ShapeDtypeStruct((rows.shape[0] // 8, 256, 128), f32),
        grid=(1,),
        in_specs=[last_block(part) for part in parts] + [VMEM],
        out_specs=VMEM,
        scratch_shapes=[
            pltpu.VMEM((128, levels * 128), bf16),
            pltpu.VMEM((128, levels * 128), bf16),
        ],
        compiler_params=params(),
        cost_estimate=cost(),
        name="top",
    )(*parts, rows)


def last_kernel(*refs, n_far):
    fars = refs[:n_far]
    above, norms = refs[n_far : n_far + 2]
    received, out = refs[n_far + 2 : -1], refs[-1]
    groups = above.shape[0]
    for group in range(groups):
        local = above[group]
        for far in fars[group * n_far // groups : (group + 1) * n_far // groups]:
            local = local + far[...]
        local = jnp.transpose(local)
        total = received[0][group].astype(f32)
        for part in received[1:]:
            total = total + part[group].astype(f32)
        total = jnp.transpose(total)
        for j in range(8):
            leaf = group * 8 + j
            rows = slice(16 * j, 16 * j + 16)
            out[:, leaf * 256 : (leaf + 1) * 256] = local[rows] + total[rows] * jnp.exp(-norms[leaf])


def last(fars, above, norms, received):
    return pl.pallas_call(
        functools.partial(last_kernel, n_far=len(fars)),
        out_shape=jax.ShapeDtypeStruct((16, norms.shape[0] * 256), f32),
        in_specs=[VMEM] * (2 + len(fars) + len(received)),
        out_specs=VMEM,
        compiler_params=params(),
        cost_estimate=cost(),
        name="last_sum",
    )(*fars, above, norms, *received)


def spread(number, bits):
    return sum(((number >> k) & 1) << b for k, b in enumerate(bits))


def compress(number, bits):
    return sum(((number >> b) & 1) << k for k, b in enumerate(bits))


def swap(value, mask):
    pairs = [(d, d ^ mask) for d in range(lax.axis_size("leaf"))]
    return lax.ppermute(value, "leaf", pairs)


def after(value, *others):
    return lax.optimization_barrier((value,) + others)[0]


def shards(
    points,
    charges,
    leaf_order,
    near_owner,
    near_slot,
    far_list,
    far_count,
    leaf_interp,
    leaf_skel,
    inner_interp,
    inner_skel,
    top_interp,
    top_skel,
):
    device_count = lax.axis_size("leaf")
    bits = device_count.bit_length() - 1
    source_bits = tuple(b for b in range(bits) if b not in TARGET_BITS)
    outer_bits = source_bits[1:]
    device = lax.axis_index("leaf")
    leaves = near_owner.shape[0]
    me = device.reshape(1).astype(jnp.int32)
    mates = range(1, 2 ** len(TARGET_BITS))
    early_bits = outer_bits[:-1]
    late = 2 ** outer_bits[-1]

    def codes_of(owner, slot, first):
        other = owner ^ device
        target_mask = sum(2**b for b in TARGET_BITS)
        place = compress(other, source_bits) * leaves + slot
        here = jnp.where((other & target_mask) == 0, 1, 0)
        near_half = leaves << (len(source_bits) - 1)
        is_late = place >= near_half
        place = place & (near_half - 1)
        is_last = is_late & (place >= 2 * leaves)
        piece = place // leaves
        is_first = ~is_late & (first == 0) & ((piece < 2) | (piece % 2 == 0))
        phase = jnp.where(is_last, 2, jnp.where(is_first, 0, 1))
        first_place = place - (piece - jnp.where(piece < 2, piece, piece // 2 + 1)) * leaves
        place = jnp.where(
            is_last,
            place - 2 * leaves,
            jnp.where(is_late, near_half + place, jnp.where(is_first, first_place, place)),
        )
        target = lax.broadcasted_iota(jnp.int32, owner.shape, 1) & 7
        return (here << (phase + PHASE_BIT)) | (target << 16) | place

    def payload_codes(payload, first):
        near = payload[-2 * near_owner.shape[1] :, :leaves].astype(jnp.int32)
        return codes_of(near[: near_owner.shape[1]], near[near_owner.shape[1] :], first)

    owner, slot = near_owner.T, near_slot.T
    src, tgt, cols, loads, rows, norms, mine, interps, skels = first_part(
        points, charges, leaf_order, owner, slot,
        leaf_interp, leaf_skel, inner_interp, inner_skel, top_interp, top_skel,
    )
    pieces = {0: src, late: swap(src, late)}
    for b in reversed(early_bits):
        pieces[2**b] = swap(src, 2**b)
    beside = swap(tgt, 2 ** TARGET_BITS[0])
    far_away = swap(tgt, 2 ** TARGET_BITS[1])
    pieces[1] = swap(mine, 1)

    def far(call, codes, token):
        return self_and_far(
            codes, after(far_list, token), far_count, cols, loads, rows, call, 2
        )

    far0, lists0 = far(0, [codes_of(owner, slot, 0)], norms)
    node = climb(me, after(mine, far0, beside), pieces[1], skels, interps, 0, 0)
    siblings = [pieces[1], swap(node, 2)]
    far1, lists1 = far(1, [payload_codes(after(beside, far0), 0)], node)
    last_targets = swap(after(far_away, far1), 2 ** TARGET_BITS[0])
    for n, b in enumerate(early_bits):
        for low in range(2**n):
            place = spread(low, early_bits[:n])
            if low:
                pieces[place | 2**b] = swap(pieces[place], 2**b)
    wanted = [spread(k, source_bits) for k in range(2 ** (len(source_bits) - 1))]
    targets = [tgt, beside, far_away, last_targets]
    lists = lists0 + lists1
    sums, far_tables1, far_tables2 = near(
        0,
        [tables[0] for tables in lists],
        targets[:2],
        [pieces[k] for k in wanted if k == 1 or not k & 1],
        codes=payload_codes(after(far_away, far1), 1),
    )
    node = climb(me, node, after(siblings[1], sums), skels, interps, 1, 1)
    for k in wanted[2::2]:
        pieces[k | 1] = swap(after(pieces[k], node), 1)
    pieces[late] = after(pieces[late], node)
    for n, b in enumerate(early_bits):
        for low in range(2**n):
            place = spread(low, early_bits[:n]) | late
            pieces[place | 2**b] = swap(pieces[place], 2**b)
    pieces[late | 1] = swap(pieces[late], 1)
    siblings.append(swap(node, 4))
    sums, last_table = near(
        1,
        [tables[1] for tables in lists] + [far_tables1],
        targets,
        [pieces[k] for k in wanted + [late, late | 1]],
        codes=payload_codes(after(last_targets, node), 1),
        before=sums,
    )
    node = climb(me, node, after(siblings[2], sums), skels, interps, 2, 2)
    siblings.append(swap(node, 8))
    for k in wanted[2::2]:
        pieces[k | late | 1] = swap(after(pieces[k | late], node), 1)
    parts = near(
        2,
        [tables[2] for tables in lists] + [far_tables2, last_table],
        targets,
        [pieces[k | late] for k in wanted[2:]],
        before=sums,
    )
    for height in range(3, bits - 1):
        node = climb(me, node, after(siblings[height], parts[0]), skels, interps, height, height)
        siblings.append(swap(node, 2 ** (height + 1)))
    received = [parts[0]] + [swap(after(parts[k], node), spread(k, TARGET_BITS)) for k in mates]
    above = top(siblings, after(rows, parts[0]))
    return last((far0, far1), above, norms, received)


def solution(mesh):
    in_specs = (
        P(None, "leaf"),
        P(None, "leaf"),
        P("leaf"),
        P("leaf", None),
        P("leaf", None),
        P("leaf", None),
        P("leaf"),
        P("leaf", None, None),
        P("leaf", None),
        P("leaf", None, None),
        P("leaf", None),
        P(),
        P(),
    )
    out_specs = P(None, "leaf")
    return jax.shard_map(shards, mesh=mesh, in_specs=in_specs, out_specs=out_specs, check_vma=False)
```

```python
import functools

import jax
import jax.numpy as jnp
from jax import lax
from jax.experimental import pallas as pl
from jax.experimental.pallas import tpu as pltpu
from jax.sharding import PartitionSpec as P

TARGET_BITS = (1, 3)
FAR_UNROLL = 8
NEAR_STEPS = (8, 4, 2)
DUMMY = 1 << 30
PHASE_BIT = 24
CODE = (1 << PHASE_BIT) - 1
VMEM_LIMIT = 24 * 1024 * 1024
FIRST_LIMIT = 58 * 1024 * 1024
PHASES = 3
bf16 = jnp.bfloat16
f32 = jnp.float32

VMEM = pl.BlockSpec(memory_space=pltpu.VMEM)
SMEM = pl.BlockSpec(memory_space=pltpu.SMEM)
ANY = pl.BlockSpec(memory_space=pl.ANY)
HBM = pl.BlockSpec(memory_space=pltpu.HBM)


def params(limit=VMEM_LIMIT):
    return pltpu.CompilerParams(vmem_limit_bytes=limit)


def cost():
    return pl.CostEstimate(flops=1, bytes_accessed=1, transcendentals=0)


def dot(a, b):
    return lax.dot_general(a, b, (((1,), (0,)), ((), ())), preferred_element_type=f32)


def dot_nt(a, b):
    return lax.dot_general(a, b, (((1,), (1,)), ((), ())), preferred_element_type=f32)


def split3(value):
    hi = value.astype(bf16).astype(f32)
    rest = value - hi
    mid = rest.astype(bf16).astype(f32)
    return hi, mid, rest - mid


def norm_row(coords):
    wide = coords.astype(f32)
    return jnp.sum(wide * wide, axis=0, keepdims=True) * 0.125


def extra_rows(norms, first):
    hi, mid, lo = split3(-norms)
    row = lax.broadcasted_iota(jnp.int32, (16, norms.shape[1]), 0)
    one_at = 3 - first
    out = jnp.where((row >= one_at) & (row < one_at + 3), 1.0, 0.0)
    out = jnp.where(row == first, hi, out)
    out = jnp.where(row == first + 1, mid, out)
    return jnp.where(row == first + 2, lo, out)


def source_matrix(coords, norms):
    width = coords.shape[1]
    extra = extra_rows(norms, 0).astype(bf16)
    return jnp.concatenate([coords, extra, jnp.zeros((48, width), bf16)], axis=0)


def target_matrix(coords, norms):
    width = coords.shape[1]
    extra = extra_rows(norms, 3)
    wide = jnp.concatenate(
        [coords.astype(f32) * 0.25, extra, jnp.zeros((48, width), f32)], axis=0
    )
    return jnp.transpose(wide).astype(bf16)


def tiles_sum(count, exponent, weight):
    total = None
    value = None
    ahead = exponent(0)
    for u in range(count):
        now = ahead
        if u + 1 < count:
            ahead = exponent(u + 1)
        if value is not None:
            part = dot_nt(value, weight(u - 1))
            total = part if total is None else total + part
        value = jnp.exp(now).astype(bf16)
    part = dot_nt(value, weight(count - 1))
    return part if total is None else total + part


def placed(loads, place):
    zero = jnp.zeros_like(loads)
    return jnp.concatenate(
        [jnp.where(place == k, loads, zero) for k in range(8)], axis=0
    )


def onehot(picks, size):
    row = lax.broadcasted_iota(jnp.int32, (size, picks.shape[1]), 0)
    return jnp.where(row == picks, 1.0, 0.0).astype(bf16)


def combine(left, right, picks, interp):
    both = jnp.concatenate([left, right], axis=1)
    coords = dot(both[:64], onehot(picks, 256)).astype(bf16)
    load = dot(both[64:], interp).astype(bf16)
    return jnp.concatenate([coords, load], axis=0)


def first_kernel(
    order, points_in, charges_in, owner_in, slot_in,
    leaf_interp_in, leaf_skel_in, inner_interp_in, inner_skel_in, top_interp, top_skel,
    src_out, tgt_out, cols_out, loads_out, rows_out, norms_out, mine_out, interps_out, skels_out,
    points, charges, owner, slot, unsorted, buffer0, buffer1, src, tgt, cols, loads, rows, norms,
    joined, root, leaf_interp, leaf_skel, inner_interp, inner_skel, sems,
):
    count = points.shape[1]
    chunks = 4
    width = count // chunks
    begun = []

    def begin(a, b):
        copy = pltpu.make_async_copy(a, b, sems.at[len(begun)])
        copy.start()
        begun.append(copy)
        return copy

    parts = [begin(charges_in, charges)]
    for c in range(chunks):
        at = pl.ds(c * width, width)
        parts.append(begin(points_in.at[:, at], points.at[:, at]))
    near_lists = [begin(owner_in, owner), begin(slot_in, slot)]
    needed = [
        begin(leaf_skel_in, leaf_skel),
        begin(leaf_interp_in, leaf_interp),
        begin(inner_skel_in, inner_skel),
        begin(inner_interp_in, inner_interp),
    ]
    rest = []
    path = path_rows()
    for k in range(interps_out.shape[0]):
        rest.append(begin(top_interp.at[path[k]], interps_out.at[k]))
        rest.append(begin(top_skel.at[pl.ds(path[k], 1)], skels_out.at[k]))

    parts[0].wait()
    for c in range(count // 128):
        at = slice(c * 128, (c + 1) * 128)
        if c * 128 % width == 0:
            parts[1 + c * 128 // width].wait()
        block = jnp.concatenate(
            [
                points[:, at].astype(f32),
                charges[:, at].astype(f32),
                jnp.zeros((48, 128), f32),
            ],
            axis=0,
        )
        unsorted[at, :] = jnp.transpose(block)

    leaves = src.shape[0]
    first_node = 2 * leaves
    lane = lax.broadcasted_iota(jnp.int32, (256, 128), 1)

    def finish(node, both):
        joined[node] = both
        cols[first_node + node] = source_matrix(both[:64], norm_row(both[:64]))
        loads[first_node + node] = both[64:]

    def copy_rows(pair, buffer):
        base = pl.multiple_of(pair * 512, 512)
        for u in range(512):
            buffer[u : u + 1, :] = unsorted[pl.ds(order[base + u], 1), :]

    def process(pair, buffer):
        even = buffer[:256]
        odd = buffer[256:]
        both = jnp.where(lane < 64, even, pltpu.roll(odd, 64, 1))
        tgt[pl.ds(pl.multiple_of(pair * 256, 256), 256), :] = (both * 0.25).astype(bf16)
        for k, mine in enumerate((even, odd)):
            i = 2 * pair + k
            both = jnp.transpose(mine)[:80].astype(bf16)
            src[i] = both
            coords, load = both[:64], both[64:]
            norm = norm_row(coords)
            norms[i] = norm
            rows[i] = target_matrix(coords, norm)
            matrix = source_matrix(coords, norm)
            for half in range(2):
                cols[2 * i + half] = matrix[:, half * 128 : half * 128 + 128]
                loads[2 * i + half] = load[:, half * 128 : half * 128 + 128]
            picked = dot(coords, onehot(leaf_skel[pl.ds(i, 1), :], 256)).astype(bf16)
            value = dot(load, leaf_interp[i]).astype(bf16)
            finish(i, jnp.concatenate([picked, value], axis=0))

    for copy in needed:
        copy.wait()

    def two_pairs(i, carry):
        copy_rows(2 * i, buffer0)
        process(jnp.maximum(2 * i - 1, 0), buffer1)
        copy_rows(2 * i + 1, buffer1)
        process(2 * i, buffer0)
        return carry

    lax.fori_loop(0, leaves // 4, two_pairs, 0)
    process(leaves // 2 - 1, buffer1)
    for copy in near_lists:
        copy.wait()
    near = jnp.concatenate([owner[...].astype(f32), slot[...].astype(f32)], axis=0)
    blank = jnp.zeros((near.shape[0], 128 - near.shape[1]), f32)
    tgt[count // 2 :, :] = jnp.concatenate([near, blank], axis=1).astype(bf16)
    rest += [begin(src, src_out), begin(tgt, tgt_out), begin(src, mine_out.at[pl.ds(0, leaves)])]
    rest += [begin(rows, rows_out), begin(norms, norms_out)]
    tiles = pl.ds(0, 3 * leaves)
    rest += [begin(cols.at[tiles], cols_out.at[tiles])]
    first, half = 0, leaves // 2
    number, row = leaves, 0
    while half > 0:
        for j in range(half):
            left = joined[first + 2 * j]
            right = joined[first + 2 * j + 1]
            finish(number, combine(left, right, inner_skel[row : row + 1, :], inner_interp[row]))
            number, row = number + 1, row + 1
        first = first + 2 * half
        half = half // 2
    node = joined[2 * leaves - 2]
    root[...] = jnp.concatenate([node, jnp.zeros_like(node)], axis=1)
    last = cols.shape[0] - 1
    cols[last] = jnp.zeros((128, 128), bf16)
    loads[last] = jnp.zeros((16, 128), bf16)
    inner_tiles = pl.ds(3 * leaves, leaves)
    rest += [begin(root, mine_out.at[leaves]), begin(loads, loads_out)]
    rest += [begin(cols.at[inner_tiles], cols_out.at[inner_tiles])]
    for copy in rest:
        copy.wait()


def path_rows():
    devices = lax.axis_size("leaf")
    device = lax.axis_index("leaf")
    bits = devices.bit_length() - 1

    def row_at(height, node):
        return devices - (devices >> (height - 1)) + node

    path = [row_at(1, device >> 1), row_at(2, device >> 2)]
    for height in range(2, bits - 1, 2):
        up = device >> (height + 1)
        path += [row_at(height + 1, up), row_at(height + 1, up ^ 1)]
        path.append(row_at(min(height + 2, bits - 1), up >> 1))
    return path


def first_part(points, charges, order, owner, slot, *tables):
    count = points.shape[1]
    leaves = count // 256
    tiles = 4 * leaves
    steps = len(path_rows())
    leaf_interp, leaf_skel, inner_interp, inner_skel = tables[:4]
    src = (leaves, 80, 256)
    tgt = (count // 2 + 2 * owner.shape[0], 128)
    cols = (tiles, 128, 128)
    loads = (tiles, 16, 128)
    rows = (leaves, 256, 128)
    norms = (leaves, 1, 256)
    shapes = [
        (src, bf16),
        (tgt, bf16),
        (cols, bf16),
        (loads, bf16),
        (rows, bf16),
        (norms, f32),
        ((leaves + 1, 80, 256), bf16),
        ((steps, 256, 128), bf16),
        ((steps, 1, 128), jnp.int32),
    ]
    held = [
        (points.shape, bf16),
        (charges.shape, bf16),
        (owner.shape, jnp.int32),
        (slot.shape, jnp.int32),
        ((count, 128), f32),
        ((512, 128), f32),
        ((512, 128), f32),
    ]
    held += shapes[:6]
    held += [((2 * leaves - 1, 80, 128), bf16), ((80, 256), bf16)]
    held += [(table.shape, table.dtype) for table in tables[:4]]
    return pl.pallas_call(
        first_kernel,
        out_shape=tuple(jax.ShapeDtypeStruct(*shape) for shape in shapes),
        in_specs=[SMEM] + [ANY] * 10,
        out_specs=(ANY,) * 9,
        scratch_shapes=[pltpu.VMEM(*shape) for shape in held]
        + [pltpu.SemaphoreType.DMA((20 + 2 * steps,))],
        compiler_params=params(FIRST_LIMIT),
        cost_estimate=cost(),
        name="order_and_subtree",
    )(order, points, charges, owner, slot, *tables)


def far_kernel(*refs, first_leaf, n_leaves, n_ids):
    codes = refs[:n_ids]
    far_list, far_count, cols_in, loads_in, rows_in, acc = refs[n_ids : 6 + n_ids]
    lists = refs[6 + n_ids : -5]
    cols, loads, rows, tiles, sems = refs[-5:]
    leaves = rows.shape[0]
    width = far_list.shape[1]
    first_node = 2 * leaves
    empty = cols.shape[0] - 1
    mine = pl.ds(first_leaf, n_leaves)
    my_tiles = pl.ds(2 * first_leaf, 2 * n_leaves)
    nodes = pl.ds(first_node, cols.shape[0] - first_node)
    copies = [
        pltpu.make_async_copy(rows_in.at[mine], rows.at[mine], sems.at[0]),
        pltpu.make_async_copy(cols_in.at[my_tiles], cols.at[my_tiles], sems.at[1]),
        pltpu.make_async_copy(loads_in, loads, sems.at[2]),
        pltpu.make_async_copy(cols_in.at[nodes], cols.at[nodes], sems.at[3]),
    ]
    for copy in copies:
        copy.start()

    def list_leaf(k, count):
        i = first_leaf + k
        tiles[count] = (i << 16) | ((2 * i) << 8) | (2 * i + 1)
        count = count + 1
        used = far_count[i]
        for k in range(0, width, 2):
            first = far_list[i, k] + first_node
            second = jnp.where(k + 1 < used, far_list[i, k + 1] + first_node, empty)
            tiles[count] = (i << 16) | (first << 8) | second
            count = count + (k < used).astype(jnp.int32)
        return count

    count = lax.fori_loop(0, n_leaves, list_leaf, 0)
    for u in range(FAR_UNROLL):
        tiles[count + u] = (empty << 8) | empty

    def step(g, carry):
        def entry(u):
            packed = tiles[g * FAR_UNROLL + u]
            return packed >> 16, (packed >> 8) & 255, packed & 255

        def exponent(u):
            leaf, first, second = entry(u)
            return dot(rows[leaf], jnp.concatenate([cols[first], cols[second]], axis=1))

        def weight(u):
            leaf, first, second = entry(u)
            return placed(jnp.concatenate([loads[first], loads[second]], axis=1), leaf & 7)

        acc[...] += tiles_sum(FAR_UNROLL, exponent, weight)
        return carry

    acc[...] = jnp.zeros_like(acc)
    for k in range(n_ids):
        list_pairs(codes[k], lists[PHASES * k : PHASES * k + PHASES])
    for copy in copies:
        copy.wait()
    lax.fori_loop(0, lax.div(count + FAR_UNROLL - 1, FAR_UNROLL), step, 0)


def list_pairs(codes, tables):
    per_leaf, leaves = codes.shape
    for g in range(leaves // 8):
        counts = [jnp.int32(0)] * len(tables)
        for j in range(8):
            for u in range(per_leaf):
                value = codes[u, g * 8 + j]
                for p, table in enumerate(tables):
                    if table is None:
                        continue
                    table[g, 1 + counts[p]] = value & CODE
                    counts[p] = counts[p] + ((value >> (PHASE_BIT + p)) & 1)
        for p, table in enumerate(tables):
            if table is None:
                continue
            table[g, 1 + counts[p]] = DUMMY
            table[g, 0] = (counts[p] + 1) & ~1


def pair_table(leaves):
    return jax.ShapeDtypeStruct((leaves // 8, 128), jnp.int32)


def self_and_far(codes, far_list, far_count, cols, loads, rows, call, calls):
    leaves = rows.shape[0]
    width = far_list.shape[1]
    n_leaves = leaves // calls
    out = pl.pallas_call(
        functools.partial(
            far_kernel, first_leaf=call * n_leaves, n_leaves=n_leaves, n_ids=len(codes)
        ),
        out_shape=(jax.ShapeDtypeStruct((256, 128), f32),) + (pair_table(leaves),) * (PHASES * len(codes)),
        in_specs=[SMEM] * (2 + len(codes)) + [ANY] * 3,
        out_specs=(VMEM,) + (SMEM,) * (PHASES * len(codes)),
        scratch_shapes=[
            pltpu.VMEM(cols.shape, bf16),
            pltpu.VMEM(loads.shape, bf16),
            pltpu.VMEM(rows.shape, bf16),
            pltpu.SMEM((n_leaves * (1 + width // 2) + 1 + FAR_UNROLL,), jnp.int32),
            pltpu.SemaphoreType.DMA((4,)),
        ],
        compiler_params=params(FIRST_LIMIT),
        cost_estimate=cost(),
        name=f"self_and_far{call}",
    )(*codes, far_list, far_count, cols, loads, rows)
    return out[0], [out[1 + PHASES * k : 1 + PHASES * k + PHASES] for k in range(len(codes))]


def near_kernel(*refs, n_sources, n_targets, n_lists, phase):
    refs = list(refs)

    def take(n):
        taken = refs[:n]
        del refs[:n]
        return taken

    makes = phase < PHASES - 1
    (codes,) = take(1) if makes else (None,)
    lists = take(n_lists)
    target_parts = take(n_targets)
    source_parts = take(n_sources)
    before = take(phase > 0)
    outs = take(n_targets) if not makes else []
    (acc,) = take(1) if makes else (None,)
    tables = take(PHASES - 1 - phase) if makes else []
    sources, targets, sems, table, flat, steps = take(6)
    if not makes:
        (acc,) = refs
    leaves = source_parts[0].shape[0]
    size = leaves * 128
    copies = []

    def begin(part, place):
        copies.append(pltpu.make_async_copy(part, place, sems.at[len(copies)]))
        copies[-1].start()

    done = 0
    for part in before:
        done = part.shape[0]
        begin(part, acc.at[pl.ds(0, done)])
    for k, part in enumerate(target_parts):
        begin(part.at[pl.ds(0, size)], targets.at[pl.ds(k * size, size)])
    for k, part in enumerate(source_parts):
        begin(part.at[pl.ds(0, leaves)], sources.at[pl.ds(k * leaves, leaves)])
    if done < acc.shape[0]:
        acc[done:] = jnp.zeros((acc.shape[0] - done,) + acc.shape[1:], f32)
    if makes:
        list_pairs(codes, [None] * phase + [table] + tables)
        lists = lists + [table]
    counts = [jnp.int32(0)] * len(NEAR_STEPS)
    base = jnp.int32(0)
    for number, pairs in enumerate(lists):
        for row in range(pairs.shape[0]):
            group = number * pairs.shape[0] + row
            used = pairs[row, 0]

            def copy_pair(i, at, pairs=pairs, row=row, group=group):
                flat[at + i] = pairs[row, 1 + i] | (group << 19)
                return at

            lax.fori_loop(0, used, copy_pair, base)
            start = base
            for k, size in enumerate(NEAR_STEPS):
                if k == 0:
                    whole = lax.div(used, size)

                    def note(i, count, start=start, size=size):
                        steps[0, count + i] = start + i * size
                        return count

                    lax.fori_loop(0, whole, note, counts[0])
                    counts[0] = counts[0] + whole
                    start = start + whole * size
                else:
                    steps[k, counts[k]] = start
                    has = jnp.where((used & size) > 0, 1, 0)
                    counts[k] = counts[k] + has
                    start = start + has * size
            base = base + used

    for copy in copies:
        copy.wait()

    for k, size in enumerate(NEAR_STEPS):

        def step(i, carry, k=k, size=size):
            start = steps[k, i]
            group = (flat[start] >> 19) & 31

            def exponent(u):
                packed = flat[start + u]
                target = (packed >> 16) & 7
                coords = sources[packed & 65535, :64, :]
                odd = target & 1
                zero = jnp.zeros_like(coords)
                matrix = jnp.concatenate(
                    [jnp.where(odd == 0, coords, zero), jnp.where(odd == 1, coords, zero)],
                    axis=0,
                )
                at = pl.multiple_of(group * 1024 + (target >> 1) * 256, 256)
                return dot(targets[pl.ds(at, 256), :], matrix) - norm_row(coords)

            def weight(u):
                packed = flat[start + u]
                place = jnp.where(packed < DUMMY, (packed >> 16) & 7, 8)
                return placed(sources[packed & 65535, 64:, :], place)

            acc[group] += tiles_sum(size, exponent, weight)
            return carry

        lax.fori_loop(0, counts[k], step, 0)

    each = acc.shape[0] // n_targets
    for k, out in enumerate(outs):
        out[...] = acc[k * each : (k + 1) * each].astype(bf16)


def near(phase, lists, targets, sources, codes=None, before=None):
    n_sources, n_targets = len(sources), len(targets)
    leaves = min(source.shape[0] for source in sources)
    sums = jax.ShapeDtypeStruct((n_targets * leaves // 8, 256, 128), f32)
    part = jax.ShapeDtypeStruct((leaves // 8, 256, 128), bf16)
    makes = phase < PHASES - 1
    args = ([codes] if makes else []) + list(lists) + list(targets) + list(sources)
    args += [] if before is None else [before]
    n_smem = len(lists) + makes
    n_tables = PHASES - 1 - phase
    if makes:
        out_shape = (sums,) + (pair_table(leaves),) * n_tables
        out_specs = (VMEM,) + (SMEM,) * n_tables
    else:
        out_shape, out_specs = (part,) * n_targets, (VMEM,) * n_targets
    scratch = [
        pltpu.VMEM((n_sources * leaves, 80, 256), bf16),
        pltpu.VMEM((n_targets * leaves * 128, 128), bf16),
        pltpu.SemaphoreType.DMA((n_sources + n_targets + 1,)),
        pltpu.SMEM(pair_table(leaves).shape, jnp.int32),
        pltpu.SMEM((n_targets * leaves * 8,), jnp.int32),
        pltpu.SMEM((len(NEAR_STEPS), n_targets * leaves), jnp.int32),
    ]
    if not makes:
        scratch.append(pltpu.VMEM(sums.shape, f32))
    return pl.pallas_call(
        functools.partial(
            near_kernel, n_sources=n_sources, n_targets=n_targets, n_lists=len(lists), phase=phase
        ),
        out_shape=out_shape,
        in_specs=[SMEM] * n_smem + [ANY] * (len(args) - n_smem),
        out_specs=out_specs,
        scratch_shapes=scratch,
        compiler_params=params(),
        cost_estimate=cost(),
        name=f"near{phase}",
    )(*args)


def ordered(first, second, test):
    return jnp.where(test, first, second), jnp.where(test, second, first)


def climb_kernel(me, own, other, skels, interps, parent, *, height, row):
    sibling = other[0, :, :128] if len(other.shape) == 3 else other[...]
    left, right = ordered(own[0, :, :128] if len(own.shape) == 3 else own[...], sibling, ((me[0] >> height) & 1) == 0)
    parent[...] = combine(left, right, skels[row], interps[row])


def last_block(value):
    if value.ndim == 2:
        return VMEM
    blocks = value.shape[0]
    return pl.BlockSpec((1,) + value.shape[1:], lambda i: (blocks - 1, 0, 0))


def climb(me, own, other, skels, interps, height, row):
    return pl.pallas_call(
        functools.partial(climb_kernel, height=height, row=row),
        grid=(1,),
        out_shape=jax.ShapeDtypeStruct((80, 128), bf16),
        in_specs=[SMEM, last_block(own), last_block(other), VMEM, VMEM],
        out_specs=VMEM,
        compiler_params=params(),
        cost_estimate=cost(),
        name=f"climb{height}",
    )(me, own, other, skels, interps)


def climb_two_kernel(me, own, one, two, three, skels, interps, sibling, parent, *, height, row):
    node = me[0] >> height
    is_left = (node & 1) == 0
    left, right = ordered(own[...], one[...], is_left)
    mine = combine(left, right, skels[row], interps[row])
    left, right = ordered(two[...], three[...], is_left)
    other = combine(left, right, skels[row + 1], interps[row + 1])
    sibling[...] = other
    left, right = ordered(mine, other, (node & 2) == 0)
    parent[...] = combine(left, right, skels[row + 2], interps[row + 2])


def climb_two(me, own, others, skels, interps, height, row):
    node = jax.ShapeDtypeStruct((80, 128), bf16)
    return pl.pallas_call(
        functools.partial(climb_two_kernel, height=height, row=row),
        out_shape=(node, node),
        in_specs=[SMEM] + [VMEM] * 6,
        out_specs=(VMEM, VMEM),
        compiler_params=params(),
        cost_estimate=cost(),
        name=f"climb{height}",
    )(me, own, *others, skels, interps)


def top_kernel(*refs):
    parts, (rows, acc, cols, loads) = refs[:-4], refs[-4:]
    for t, part in enumerate(parts):
        node = part[0, :, :128] if len(part.shape) == 3 else part[...]
        cols[:, t * 128 : (t + 1) * 128] = source_matrix(node[:64], norm_row(node[:64]))
        loads[:, t * 128 : (t + 1) * 128] = jnp.concatenate([node[64:]] * 8, axis=0)
    lane = lax.broadcasted_iota(jnp.int32, (256, 128), 1) >> 4

    levels = len(parts)
    spans = [slice(c * 128, min(c + 2, levels) * 128) for c in range(0, levels, 2)]

    def two_leaves(i, carry):
        both = rows[pl.ds(2 * i, 2)].reshape(512, 128)
        result = tiles_sum(
            len(spans),
            lambda u: dot(both, cols[:, spans[u]]),
            lambda u: loads[:, spans[u]],
        )
        group = lax.div(i, 4)
        place = (2 * i) & 7
        acc[group] += jnp.where(lane == place, result[:256], 0.0) + jnp.where(
            lane == place + 1, result[256:], 0.0
        )
        return carry

    acc[...] = jnp.zeros_like(acc)
    lax.fori_loop(0, rows.shape[0] // 2, two_leaves, 0, unroll=2)


def top(parts, rows):
    levels = len(parts)
    return pl.pallas_call(
        top_kernel,
        out_shape=jax.ShapeDtypeStruct((rows.shape[0] // 8, 256, 128), f32),
        grid=(1,),
        in_specs=[last_block(part) for part in parts] + [VMEM],
        out_specs=VMEM,
        scratch_shapes=[
            pltpu.VMEM((128, levels * 128), bf16),
            pltpu.VMEM((128, levels * 128), bf16),
        ],
        compiler_params=params(),
        cost_estimate=cost(),
        name="top",
    )(*parts, rows)


def last_kernel(*refs, n_far):
    fars = refs[:n_far]
    above, norms = refs[n_far : n_far + 2]
    received, out = refs[n_far + 2 : -1], refs[-1]
    groups = above.shape[0]
    for group in range(groups):
        local = above[group]
        for far in fars[group * n_far // groups : (group + 1) * n_far // groups]:
            local = local + far[...]
        local = jnp.transpose(local)
        total = received[0][group].astype(f32)
        for part in received[1:]:
            total = total + part[group].astype(f32)
        total = jnp.transpose(total)
        for j in range(8):
            leaf = group * 8 + j
            rows = slice(16 * j, 16 * j + 16)
            out[:, leaf * 256 : (leaf + 1) * 256] = local[rows] + total[rows] * jnp.exp(-norms[leaf])


def last(fars, above, norms, received):
    return pl.pallas_call(
        functools.partial(last_kernel, n_far=len(fars)),
        out_shape=jax.ShapeDtypeStruct((16, norms.shape[0] * 256), f32),
        in_specs=[VMEM] * (2 + len(fars) + len(received)),
        out_specs=VMEM,
        compiler_params=params(),
        cost_estimate=cost(),
        name="last_sum",
    )(*fars, above, norms, *received)


def spread(number, bits):
    return sum(((number >> k) & 1) << b for k, b in enumerate(bits))


def compress(number, bits):
    return sum(((number >> b) & 1) << k for k, b in enumerate(bits))


def swap(value, mask):
    pairs = [(d, d ^ mask) for d in range(lax.axis_size("leaf"))]
    return lax.ppermute(value, "leaf", pairs)


def after(value, *others):
    return lax.optimization_barrier((value,) + others)[0]


def shards(
    points,
    charges,
    leaf_order,
    near_owner,
    near_slot,
    far_list,
    far_count,
    leaf_interp,
    leaf_skel,
    inner_interp,
    inner_skel,
    top_interp,
    top_skel,
):
    device_count = lax.axis_size("leaf")
    bits = device_count.bit_length() - 1
    source_bits = tuple(b for b in range(bits) if b not in TARGET_BITS)
    outer_bits = source_bits[1:]
    device = lax.axis_index("leaf")
    leaves = near_owner.shape[0]
    me = device.reshape(1).astype(jnp.int32)
    mates = range(1, 2 ** len(TARGET_BITS))
    early_bits = outer_bits[:-1]
    late = 2 ** outer_bits[-1]

    def codes_of(owner, slot, first):
        other = owner ^ device
        target_mask = sum(2**b for b in TARGET_BITS)
        place = compress(other, source_bits) * leaves + slot
        here = jnp.where((other & target_mask) == 0, 1, 0)
        near_half = leaves << (len(source_bits) - 1)
        is_late = place >= near_half
        place = place & (near_half - 1)
        is_last = is_late & (place >= 2 * leaves)
        piece = place // leaves
        is_first = ~is_late & (first == 0) & ((piece < 2) | (piece % 2 == 0))
        phase = jnp.where(is_last, 2, jnp.where(is_first, 0, 1))
        first_place = place - (piece - jnp.where(piece < 2, piece, piece // 2 + 1)) * leaves
        place = jnp.where(
            is_last,
            place - 2 * leaves,
            jnp.where(is_late, near_half + place, jnp.where(is_first, first_place, place)),
        )
        target = lax.broadcasted_iota(jnp.int32, owner.shape, 1) & 7
        return (here << (phase + PHASE_BIT)) | (target << 16) | place

    def payload_codes(payload, first):
        near = payload[-2 * near_owner.shape[1] :, :leaves].astype(jnp.int32)
        return codes_of(near[: near_owner.shape[1]], near[near_owner.shape[1] :], first)

    owner, slot = near_owner.T, near_slot.T
    src, tgt, cols, loads, rows, norms, mine, interps, skels = first_part(
        points, charges, leaf_order, owner, slot,
        leaf_interp, leaf_skel, inner_interp, inner_skel, top_interp, top_skel,
    )
    pieces = {0: src, late: swap(src, late)}
    for b in reversed(early_bits):
        pieces[2**b] = swap(src, 2**b)
    beside = swap(tgt, 2 ** TARGET_BITS[0])
    far_away = swap(tgt, 2 ** TARGET_BITS[1])
    pieces[1] = swap(mine, 1)

    def far(call, codes, token):
        return self_and_far(
            codes, after(far_list, token), far_count, cols, loads, rows, call, 2
        )

    far0, lists0 = far(0, [codes_of(owner, slot, 0)], norms)
    node = climb(me, after(mine, far0, beside), pieces[1], skels, interps, 0, 0)
    siblings = [pieces[1], swap(node, 2)]
    far1, lists1 = far(1, [payload_codes(after(beside, far0), 0)], node)
    last_targets = swap(after(far_away, far1), 2 ** TARGET_BITS[0])
    for n, b in enumerate(early_bits):
        for low in range(2**n):
            place = spread(low, early_bits[:n])
            if low:
                pieces[place | 2**b] = swap(pieces[place], 2**b)
    wanted = [spread(k, source_bits) for k in range(2 ** (len(source_bits) - 1))]
    targets = [tgt, beside, far_away, last_targets]
    lists = lists0 + lists1
    sums, far_tables1, far_tables2 = near(
        0,
        [tables[0] for tables in lists],
        targets[:3],
        [pieces[k] for k in wanted if k == 1 or not k & 1],
        codes=payload_codes(after(far_away, far1), 0),
    )
    node = climb(me, node, after(siblings[1], sums), skels, interps, 1, 1)
    for k in wanted[2::2]:
        pieces[k | 1] = swap(after(pieces[k], node), 1)
    pieces[late] = after(pieces[late], node)
    for n, b in enumerate(early_bits):
        for low in range(2**n):
            place = spread(low, early_bits[:n]) | late
            pieces[place | 2**b] = swap(pieces[place], 2**b)
    pieces[late | 1] = swap(pieces[late], 1)
    height, row = 2, 2
    others = [swap(node, k * 2**height) for k in (1, 2, 3)]
    sums, last_table = near(
        1,
        [tables[1] for tables in lists] + [far_tables1],
        targets,
        [pieces[k] for k in wanted + [late, late | 1]],
        codes=payload_codes(after(last_targets, node), 1),
        before=sums,
    )
    others[0] = after(others[0], sums)
    while height + 1 < bits:
        if height > 2:
            others = [swap(node, k * 2**height) for k in (1, 2, 3)]
        sibling, node = climb_two(me, node, others, skels, interps, height, row)
        siblings += [others[0], sibling]
        height, row = height + 2, row + 3
    if height < bits:
        siblings.append(swap(node, 2**height))
    for k in wanted[2::2]:
        pieces[k | late | 1] = swap(after(pieces[k | late], node), 1)
    parts = near(
        2,
        [tables[2] for tables in lists] + [far_tables2, after(last_table, node)],
        targets,
        [pieces[k | late] for k in wanted[2:]],
        before=sums,
    )
    siblings[-1] = after(siblings[-1], parts[0])
    received = [parts[0]] + [
        swap(after(parts[k], siblings[-1]), spread(k, TARGET_BITS)) for k in mates
    ]
    above = top(siblings, after(rows, parts[0]))
    return last((far0, far1), above, norms, received)


def solution(mesh):
    in_specs = (
        P(None, "leaf"),
        P(None, "leaf"),
        P("leaf"),
        P("leaf", None),
        P("leaf", None),
        P("leaf", None),
        P("leaf"),
        P("leaf", None, None),
        P("leaf", None),
        P("leaf", None, None),
        P("leaf", None),
        P(),
        P(),
    )
    out_specs = P(None, "leaf")
    return jax.shard_map(shards, mesh=mesh, in_specs=in_specs, out_specs=out_specs, check_vma=False)
```

```python
import functools

import jax
import jax.numpy as jnp
from jax import lax
from jax.experimental import pallas as pl
from jax.experimental.pallas import tpu as pltpu
from jax.sharding import PartitionSpec as P

TARGET_BITS = (1, 3)
FAR_UNROLL = 8
NEAR_STEPS = (8, 4, 2)
DUMMY = 1 << 30
PHASE_BIT = 24
CODE = (1 << PHASE_BIT) - 1
VMEM_LIMIT = 24 * 1024 * 1024
FIRST_LIMIT = 58 * 1024 * 1024
PHASES = 3
bf16 = jnp.bfloat16
f32 = jnp.float32

VMEM = pl.BlockSpec(memory_space=pltpu.VMEM)
SMEM = pl.BlockSpec(memory_space=pltpu.SMEM)
ANY = pl.BlockSpec(memory_space=pl.ANY)
HBM = pl.BlockSpec(memory_space=pltpu.HBM)


def params(limit=VMEM_LIMIT):
    return pltpu.CompilerParams(vmem_limit_bytes=limit)


def cost():
    return pl.CostEstimate(flops=1, bytes_accessed=1, transcendentals=0)


def dot(a, b):
    return lax.dot_general(a, b, (((1,), (0,)), ((), ())), preferred_element_type=f32)


def dot_nt(a, b):
    return lax.dot_general(a, b, (((1,), (1,)), ((), ())), preferred_element_type=f32)


def split3(value):
    hi = value.astype(bf16).astype(f32)
    rest = value - hi
    mid = rest.astype(bf16).astype(f32)
    return hi, mid, rest - mid


def norm_row(coords):
    wide = coords.astype(f32)
    return jnp.sum(wide * wide, axis=0, keepdims=True) * 0.125


def extra_rows(norms, first):
    hi, mid, lo = split3(-norms)
    row = lax.broadcasted_iota(jnp.int32, (16, norms.shape[1]), 0)
    one_at = 3 - first
    out = jnp.where((row >= one_at) & (row < one_at + 3), 1.0, 0.0)
    out = jnp.where(row == first, hi, out)
    out = jnp.where(row == first + 1, mid, out)
    return jnp.where(row == first + 2, lo, out)


def source_matrix(coords, norms):
    width = coords.shape[1]
    extra = extra_rows(norms, 0).astype(bf16)
    return jnp.concatenate([coords, extra, jnp.zeros((48, width), bf16)], axis=0)


def target_matrix(coords, norms):
    width = coords.shape[1]
    extra = extra_rows(norms, 3)
    wide = jnp.concatenate(
        [coords.astype(f32) * 0.25, extra, jnp.zeros((48, width), f32)], axis=0
    )
    return jnp.transpose(wide).astype(bf16)


def tiles_sum(count, exponent, weight):
    total = None
    value = None
    ahead = exponent(0)
    for u in range(count):
        now = ahead
        if u + 1 < count:
            ahead = exponent(u + 1)
        if value is not None:
            part = dot_nt(value, weight(u - 1))
            total = part if total is None else total + part
        value = jnp.exp(now).astype(bf16)
    part = dot_nt(value, weight(count - 1))
    return part if total is None else total + part


def placed(loads, place):
    zero = jnp.zeros_like(loads)
    return jnp.concatenate(
        [jnp.where(place == k, loads, zero) for k in range(8)], axis=0
    )


def onehot(picks, size):
    row = lax.broadcasted_iota(jnp.int32, (size, picks.shape[1]), 0)
    return jnp.where(row == picks, 1.0, 0.0).astype(bf16)


def combine(left, right, picks, interp):
    both = jnp.concatenate([left, right], axis=1)
    coords = dot(both[:64], onehot(picks, 256)).astype(bf16)
    load = dot(both[64:], interp).astype(bf16)
    return jnp.concatenate([coords, load], axis=0)


def first_kernel(
    order, points_in, charges_in, owner_in, slot_in,
    leaf_interp_in, leaf_skel_in, inner_interp_in, inner_skel_in, top_interp, top_skel,
    src_out, tgt_out, cols_out, loads_out, rows_out, norms_out, mine_out, interps_out, skels_out,
    points, charges, owner, slot, unsorted, buffer0, buffer1, src, tgt, cols, loads, rows, norms,
    joined, root, interps, skels, leaf_interp, leaf_skel, inner_interp, inner_skel, sems,
):
    count = points.shape[1]
    chunks = 4
    width = count // chunks
    begun = []

    def begin(a, b):
        copy = pltpu.make_async_copy(a, b, sems.at[len(begun)])
        copy.start()
        begun.append(copy)
        return copy

    parts = [begin(charges_in, charges)]
    for c in range(chunks):
        at = pl.ds(c * width, width)
        parts.append(begin(points_in.at[:, at], points.at[:, at]))
    near_lists = [begin(owner_in, owner), begin(slot_in, slot)]
    needed = [
        begin(leaf_skel_in, leaf_skel),
        begin(leaf_interp_in, leaf_interp),
        begin(inner_skel_in, inner_skel),
        begin(inner_interp_in, inner_interp),
    ]
    rest = []
    path = path_rows()
    on_path = []
    for k in range(interps_out.shape[0]):
        on_path.append(begin(top_interp.at[path[k]], interps.at[k]))
        on_path.append(begin(top_skel.at[pl.ds(path[k], 1)], skels.at[k]))

    parts[0].wait()
    for c in range(count // 128):
        at = slice(c * 128, (c + 1) * 128)
        if c * 128 % width == 0:
            parts[1 + c * 128 // width].wait()
        block = jnp.concatenate(
            [
                points[:, at].astype(f32),
                charges[:, at].astype(f32),
                jnp.zeros((48, 128), f32),
            ],
            axis=0,
        )
        unsorted[at, :] = jnp.transpose(block)

    leaves = src.shape[0]
    first_node = 2 * leaves
    lane = lax.broadcasted_iota(jnp.int32, (256, 128), 1)

    def finish(node, both):
        joined[node] = both
        cols[first_node + node] = source_matrix(both[:64], norm_row(both[:64]))
        loads[first_node + node] = both[64:]

    def copy_rows(pair, buffer):
        base = pl.multiple_of(pair * 512, 512)
        for u in range(512):
            buffer[u : u + 1, :] = unsorted[pl.ds(order[base + u], 1), :]

    def process(pair, buffer):
        even = buffer[:256]
        odd = buffer[256:]
        both = jnp.where(lane < 64, even, pltpu.roll(odd, 64, 1))
        tgt[pl.ds(pl.multiple_of(pair * 256, 256), 256), :] = (both * 0.25).astype(bf16)
        for k, mine in enumerate((even, odd)):
            i = 2 * pair + k
            both = jnp.transpose(mine)[:80].astype(bf16)
            src[i] = both
            coords, load = both[:64], both[64:]
            norm = norm_row(coords)
            norms[i] = norm
            rows[i] = target_matrix(coords, norm)
            matrix = source_matrix(coords, norm)
            for half in range(2):
                cols[2 * i + half] = matrix[:, half * 128 : half * 128 + 128]
                loads[2 * i + half] = load[:, half * 128 : half * 128 + 128]
            picked = dot(coords, onehot(leaf_skel[pl.ds(i, 1), :], 256)).astype(bf16)
            value = dot(load, leaf_interp[i]).astype(bf16)
            finish(i, jnp.concatenate([picked, value], axis=0))

    for copy in needed:
        copy.wait()

    def two_pairs(i, carry):
        copy_rows(2 * i, buffer0)
        process(jnp.maximum(2 * i - 1, 0), buffer1)
        copy_rows(2 * i + 1, buffer1)
        process(2 * i, buffer0)
        return carry

    lax.fori_loop(0, leaves // 4, two_pairs, 0)
    process(leaves // 2 - 1, buffer1)
    for copy in near_lists + on_path:
        copy.wait()
    rest += [begin(interps, interps_out), begin(skels, skels_out)]
    near = jnp.concatenate([owner[...].astype(f32), slot[...].astype(f32)], axis=0)
    blank = jnp.zeros((near.shape[0], 128 - near.shape[1]), f32)
    tgt[count // 2 :, :] = jnp.concatenate([near, blank], axis=1).astype(bf16)
    rest += [begin(src, src_out), begin(tgt, tgt_out), begin(src, mine_out.at[pl.ds(0, leaves)])]
    rest += [begin(rows, rows_out), begin(norms, norms_out)]
    tiles = pl.ds(0, 3 * leaves)
    rest += [begin(cols.at[tiles], cols_out.at[tiles])]
    first, half = 0, leaves // 2
    number, row = leaves, 0
    while half > 0:
        for j in range(half):
            left = joined[first + 2 * j]
            right = joined[first + 2 * j + 1]
            finish(number, combine(left, right, inner_skel[row : row + 1, :], inner_interp[row]))
            number, row = number + 1, row + 1
        first = first + 2 * half
        half = half // 2
    node = joined[2 * leaves - 2]
    root[...] = jnp.concatenate([node, jnp.zeros_like(node)], axis=1)
    last = cols.shape[0] - 1
    cols[last] = jnp.zeros((128, 128), bf16)
    loads[last] = jnp.zeros((16, 128), bf16)
    inner_tiles = pl.ds(3 * leaves, leaves)
    rest += [begin(root, mine_out.at[leaves]), begin(loads, loads_out)]
    rest += [begin(cols.at[inner_tiles], cols_out.at[inner_tiles])]
    for copy in rest:
        copy.wait()


def path_rows():
    devices = lax.axis_size("leaf")
    device = lax.axis_index("leaf")
    bits = devices.bit_length() - 1

    def row_at(height, node):
        return devices - (devices >> (height - 1)) + node

    path = [row_at(1, device >> 1), row_at(2, device >> 2)]
    for height in range(2, bits - 1, 2):
        up = device >> (height + 1)
        path += [row_at(height + 1, up), row_at(height + 1, up ^ 1)]
        path.append(row_at(min(height + 2, bits - 1), up >> 1))
    return path


def first_part(points, charges, order, owner, slot, *tables):
    count = points.shape[1]
    leaves = count // 256
    tiles = 4 * leaves
    steps = len(path_rows())
    leaf_interp, leaf_skel, inner_interp, inner_skel = tables[:4]
    src = (leaves, 80, 256)
    tgt = (count // 2 + 2 * owner.shape[0], 128)
    cols = (tiles, 128, 128)
    loads = (tiles, 16, 128)
    rows = (leaves, 256, 128)
    norms = (leaves, 1, 256)
    shapes = [
        (src, bf16),
        (tgt, bf16),
        (cols, bf16),
        (loads, bf16),
        (rows, bf16),
        (norms, f32),
        ((leaves + 1, 80, 256), bf16),
        ((steps, 256, 128), bf16),
        ((steps, 1, 128), jnp.int32),
    ]
    held = [
        (points.shape, bf16),
        (charges.shape, bf16),
        (owner.shape, jnp.int32),
        (slot.shape, jnp.int32),
        ((count, 128), f32),
        ((512, 128), f32),
        ((512, 128), f32),
    ]
    held += shapes[:6]
    held += [((2 * leaves - 1, 80, 128), bf16), ((80, 256), bf16)]
    held += shapes[7:]
    held += [(table.shape, table.dtype) for table in tables[:4]]
    return pl.pallas_call(
        first_kernel,
        out_shape=tuple(jax.ShapeDtypeStruct(*shape) for shape in shapes),
        in_specs=[SMEM] + [ANY] * 10,
        out_specs=(ANY,) * 9,
        scratch_shapes=[pltpu.VMEM(*shape) for shape in held]
        + [pltpu.SemaphoreType.DMA((24 + 2 * steps,))],
        compiler_params=params(FIRST_LIMIT),
        cost_estimate=cost(),
        name="order_and_subtree",
    )(order, points, charges, owner, slot, *tables)


def far_kernel(*refs, first_leaf, n_leaves, n_ids):
    codes = refs[:n_ids]
    far_list, far_count, cols_in, loads_in, rows_in, acc = refs[n_ids : 6 + n_ids]
    lists = refs[6 + n_ids : -5]
    cols, loads, rows, tiles, sems = refs[-5:]
    leaves = rows.shape[0]
    width = far_list.shape[1]
    first_node = 2 * leaves
    empty = cols.shape[0] - 1
    mine = pl.ds(first_leaf, n_leaves)
    my_tiles = pl.ds(2 * first_leaf, 2 * n_leaves)
    nodes = pl.ds(first_node, cols.shape[0] - first_node)
    copies = [
        pltpu.make_async_copy(rows_in.at[mine], rows.at[mine], sems.at[0]),
        pltpu.make_async_copy(cols_in.at[my_tiles], cols.at[my_tiles], sems.at[1]),
        pltpu.make_async_copy(loads_in, loads, sems.at[2]),
        pltpu.make_async_copy(cols_in.at[nodes], cols.at[nodes], sems.at[3]),
    ]
    for copy in copies:
        copy.start()

    def list_leaf(k, count):
        i = first_leaf + k
        tiles[count] = (i << 16) | ((2 * i) << 8) | (2 * i + 1)
        count = count + 1
        used = far_count[i]
        for k in range(0, width, 2):
            first = far_list[i, k] + first_node
            second = jnp.where(k + 1 < used, far_list[i, k + 1] + first_node, empty)
            tiles[count] = (i << 16) | (first << 8) | second
            count = count + (k < used).astype(jnp.int32)
        return count

    count = lax.fori_loop(0, n_leaves, list_leaf, 0)
    for u in range(FAR_UNROLL):
        tiles[count + u] = (empty << 8) | empty

    def step(g, carry):
        values, weights = [], []
        for u in range(FAR_UNROLL):
            packed = tiles[g * FAR_UNROLL + u]
            leaf = packed >> 16
            first = (packed >> 8) & 255
            second = packed & 255
            matrix = jnp.concatenate([cols[first], cols[second]], axis=1)
            load = jnp.concatenate([loads[first], loads[second]], axis=1)
            values.append(jnp.exp(dot(rows[leaf], matrix)).astype(bf16))
            weights.append(placed(load, leaf & 7))
        acc[...] += dot_nt(jnp.concatenate(values, axis=1), jnp.concatenate(weights, axis=1))
        return carry

    acc[...] = jnp.zeros_like(acc)
    for k in range(n_ids):
        list_pairs(codes[k], lists[PHASES * k : PHASES * k + PHASES])
    for copy in copies:
        copy.wait()
    lax.fori_loop(0, lax.div(count + FAR_UNROLL - 1, FAR_UNROLL), step, 0)


def list_pairs(codes, tables):
    per_leaf, leaves = codes.shape
    for g in range(leaves // 8):
        counts = [jnp.int32(0)] * len(tables)
        for j in range(8):
            for u in range(per_leaf):
                value = codes[u, g * 8 + j]
                for p, table in enumerate(tables):
                    if table is None:
                        continue
                    table[g, 1 + counts[p]] = value & CODE
                    counts[p] = counts[p] + ((value >> (PHASE_BIT + p)) & 1)
        for p, table in enumerate(tables):
            if table is None:
                continue
            table[g, 1 + counts[p]] = DUMMY
            table[g, 0] = (counts[p] + 1) & ~1


def pair_table(leaves):
    return jax.ShapeDtypeStruct((leaves // 8, 128), jnp.int32)


def self_and_far(codes, far_list, far_count, cols, loads, rows, call, calls):
    leaves = rows.shape[0]
    width = far_list.shape[1]
    n_leaves = leaves // calls
    out = pl.pallas_call(
        functools.partial(
            far_kernel, first_leaf=call * n_leaves, n_leaves=n_leaves, n_ids=len(codes)
        ),
        out_shape=(jax.ShapeDtypeStruct((256, 128), f32),) + (pair_table(leaves),) * (PHASES * len(codes)),
        in_specs=[SMEM] * (2 + len(codes)) + [ANY] * 3,
        out_specs=(VMEM,) + (SMEM,) * (PHASES * len(codes)),
        scratch_shapes=[
            pltpu.VMEM(cols.shape, bf16),
            pltpu.VMEM(loads.shape, bf16),
            pltpu.VMEM(rows.shape, bf16),
            pltpu.SMEM((n_leaves * (1 + width // 2) + 1 + FAR_UNROLL,), jnp.int32),
            pltpu.SemaphoreType.DMA((4,)),
        ],
        compiler_params=params(FIRST_LIMIT),
        cost_estimate=cost(),
        name=f"self_and_far{call}",
    )(*codes, far_list, far_count, cols, loads, rows)
    return out[0], [out[1 + PHASES * k : 1 + PHASES * k + PHASES] for k in range(len(codes))]


def near_kernel(*refs, n_sources, n_targets, n_lists, phase):
    refs = list(refs)

    def take(n):
        taken = refs[:n]
        del refs[:n]
        return taken

    makes = phase < PHASES - 1
    (codes,) = take(1) if makes else (None,)
    lists = take(n_lists)
    target_parts = take(n_targets)
    source_parts = take(n_sources)
    before = take(phase > 0)
    outs = take(n_targets) if not makes else []
    (acc,) = take(1) if makes else (None,)
    tables = take(PHASES - 1 - phase) if makes else []
    sources, targets, sems, table, flat, steps = take(6)
    if not makes:
        (acc,) = refs
    leaves = source_parts[0].shape[0]
    size = leaves * 128
    copies = []

    def begin(part, place):
        copies.append(pltpu.make_async_copy(part, place, sems.at[len(copies)]))
        copies[-1].start()

    done = 0
    for part in before:
        done = part.shape[0]
        begin(part, acc.at[pl.ds(0, done)])
    for k, part in enumerate(target_parts):
        begin(part.at[pl.ds(0, size)], targets.at[pl.ds(k * size, size)])
    for k, part in enumerate(source_parts):
        begin(part.at[pl.ds(0, leaves)], sources.at[pl.ds(k * leaves, leaves)])
    if done < acc.shape[0]:
        acc[done:] = jnp.zeros((acc.shape[0] - done,) + acc.shape[1:], f32)
    if makes:
        list_pairs(codes, [None] * phase + [table] + tables)
        lists = lists + [table]
    counts = [jnp.int32(0)] * len(NEAR_STEPS)
    base = jnp.int32(0)
    for number, pairs in enumerate(lists):
        for row in range(pairs.shape[0]):
            group = number * pairs.shape[0] + row
            used = pairs[row, 0]

            def copy_pair(i, at, pairs=pairs, row=row, group=group):
                flat[at + i] = pairs[row, 1 + i] | (group << 19)
                return at

            lax.fori_loop(0, used, copy_pair, base)
            start = base
            for k, size in enumerate(NEAR_STEPS):
                if k == 0:
                    whole = lax.div(used, size)

                    def note(i, count, start=start, size=size):
                        steps[0, count + i] = start + i * size
                        return count

                    lax.fori_loop(0, whole, note, counts[0])
                    counts[0] = counts[0] + whole
                    start = start + whole * size
                else:
                    steps[k, counts[k]] = start
                    has = jnp.where((used & size) > 0, 1, 0)
                    counts[k] = counts[k] + has
                    start = start + has * size
            base = base + used

    for copy in copies:
        copy.wait()

    for k, size in enumerate(NEAR_STEPS):

        def step(i, carry, k=k, size=size):
            start = steps[k, i]
            group = (flat[start] >> 19) & 31

            def exponent(u):
                packed = flat[start + u]
                target = (packed >> 16) & 7
                coords = sources[packed & 65535, :64, :]
                odd = target & 1
                zero = jnp.zeros_like(coords)
                matrix = jnp.concatenate(
                    [jnp.where(odd == 0, coords, zero), jnp.where(odd == 1, coords, zero)],
                    axis=0,
                )
                at = pl.multiple_of(group * 1024 + (target >> 1) * 256, 256)
                return dot(targets[pl.ds(at, 256), :], matrix) - norm_row(coords)

            def weight(u):
                packed = flat[start + u]
                place = jnp.where(packed < DUMMY, (packed >> 16) & 7, 8)
                return placed(sources[packed & 65535, 64:, :], place)

            acc[group] += tiles_sum(size, exponent, weight)
            return carry

        lax.fori_loop(0, counts[k], step, 0)

    each = acc.shape[0] // n_targets
    for k, out in enumerate(outs):
        out[...] = acc[k * each : (k + 1) * each].astype(bf16)


def near(phase, lists, targets, sources, codes=None, before=None):
    n_sources, n_targets = len(sources), len(targets)
    leaves = min(source.shape[0] for source in sources)
    sums = jax.ShapeDtypeStruct((n_targets * leaves // 8, 256, 128), f32)
    part = jax.ShapeDtypeStruct((leaves // 8, 256, 128), bf16)
    makes = phase < PHASES - 1
    args = ([codes] if makes else []) + list(lists) + list(targets) + list(sources)
    args += [] if before is None else [before]
    n_smem = len(lists) + makes
    n_tables = PHASES - 1 - phase
    if makes:
        out_shape = (sums,) + (pair_table(leaves),) * n_tables
        out_specs = (VMEM,) + (SMEM,) * n_tables
    else:
        out_shape, out_specs = (part,) * n_targets, (VMEM,) * n_targets
    scratch = [
        pltpu.VMEM((n_sources * leaves, 80, 256), bf16),
        pltpu.VMEM((n_targets * leaves * 128, 128), bf16),
        pltpu.SemaphoreType.DMA((n_sources + n_targets + 1,)),
        pltpu.SMEM(pair_table(leaves).shape, jnp.int32),
        pltpu.SMEM((n_targets * leaves * 8,), jnp.int32),
        pltpu.SMEM((len(NEAR_STEPS), n_targets * leaves), jnp.int32),
    ]
    if not makes:
        scratch.append(pltpu.VMEM(sums.shape, f32))
    return pl.pallas_call(
        functools.partial(
            near_kernel, n_sources=n_sources, n_targets=n_targets, n_lists=len(lists), phase=phase
        ),
        out_shape=out_shape,
        in_specs=[SMEM] * n_smem + [ANY] * (len(args) - n_smem),
        out_specs=out_specs,
        scratch_shapes=scratch,
        compiler_params=params(),
        cost_estimate=cost(),
        name=f"near{phase}",
    )(*args)


def ordered(first, second, test):
    return jnp.where(test, first, second), jnp.where(test, second, first)


def climb_kernel(me, own, other, skels, interps, parent, *, height, row):
    sibling = other[0, :, :128] if len(other.shape) == 3 else other[...]
    left, right = ordered(own[0, :, :128] if len(own.shape) == 3 else own[...], sibling, ((me[0] >> height) & 1) == 0)
    parent[...] = combine(left, right, skels[row], interps[row])


def last_block(value):
    if value.ndim == 2:
        return VMEM
    blocks = value.shape[0]
    return pl.BlockSpec((1,) + value.shape[1:], lambda i: (blocks - 1, 0, 0))


def climb(me, own, other, skels, interps, height, row):
    return pl.pallas_call(
        functools.partial(climb_kernel, height=height, row=row),
        grid=(1,),
        out_shape=jax.ShapeDtypeStruct((80, 128), bf16),
        in_specs=[SMEM, last_block(own), last_block(other), VMEM, VMEM],
        out_specs=VMEM,
        compiler_params=params(),
        cost_estimate=cost(),
        name=f"climb{height}",
    )(me, own, other, skels, interps)


def climb_two_kernel(me, own, one, two, three, skels, interps, sibling, parent, *, height, row):
    node = me[0] >> height
    is_left = (node & 1) == 0
    left, right = ordered(own[...], one[...], is_left)
    mine = combine(left, right, skels[row], interps[row])
    left, right = ordered(two[...], three[...], is_left)
    other = combine(left, right, skels[row + 1], interps[row + 1])
    sibling[...] = other
    left, right = ordered(mine, other, (node & 2) == 0)
    parent[...] = combine(left, right, skels[row + 2], interps[row + 2])


def climb_two(me, own, others, skels, interps, height, row):
    node = jax.ShapeDtypeStruct((80, 128), bf16)
    return pl.pallas_call(
        functools.partial(climb_two_kernel, height=height, row=row),
        out_shape=(node, node),
        in_specs=[SMEM] + [VMEM] * 6,
        out_specs=(VMEM, VMEM),
        compiler_params=params(),
        cost_estimate=cost(),
        name=f"climb{height}",
    )(me, own, *others, skels, interps)


def top_kernel(*refs):
    parts, (rows, acc, cols, loads) = refs[:-4], refs[-4:]
    for t, part in enumerate(parts):
        node = part[0, :, :128] if len(part.shape) == 3 else part[...]
        cols[:, t * 128 : (t + 1) * 128] = source_matrix(node[:64], norm_row(node[:64]))
        loads[:, t * 128 : (t + 1) * 128] = jnp.concatenate([node[64:]] * 8, axis=0)
    lane = lax.broadcasted_iota(jnp.int32, (256, 128), 1) >> 4

    def two_leaves(i, carry):
        both = rows[pl.ds(2 * i, 2)].reshape(512, 128)
        value = jnp.exp(dot(both, cols[...])).astype(bf16)
        result = dot_nt(value, loads[...])
        group = lax.div(i, 4)
        place = (2 * i) & 7
        acc[group] += jnp.where(lane == place, result[:256], 0.0) + jnp.where(
            lane == place + 1, result[256:], 0.0
        )
        return carry

    acc[...] = jnp.zeros_like(acc)
    lax.fori_loop(0, rows.shape[0] // 2, two_leaves, 0, unroll=2)


def top(parts, rows):
    levels = len(parts)
    return pl.pallas_call(
        top_kernel,
        out_shape=jax.ShapeDtypeStruct((rows.shape[0] // 8, 256, 128), f32),
        grid=(1,),
        in_specs=[last_block(part) for part in parts] + [VMEM],
        out_specs=VMEM,
        scratch_shapes=[
            pltpu.VMEM((128, levels * 128), bf16),
            pltpu.VMEM((128, levels * 128), bf16),
        ],
        compiler_params=params(),
        cost_estimate=cost(),
        name="top",
    )(*parts, rows)


def last_kernel(*refs, n_far):
    fars = refs[:n_far]
    above, norms = refs[n_far : n_far + 2]
    received, out = refs[n_far + 2 : -1], refs[-1]
    groups = above.shape[0]
    for group in range(groups):
        local = above[group]
        for far in fars[group * n_far // groups : (group + 1) * n_far // groups]:
            local = local + far[...]
        local = jnp.transpose(local)
        total = received[0][group].astype(f32)
        for part in received[1:]:
            total = total + part[group].astype(f32)
        total = jnp.transpose(total)
        for j in range(8):
            leaf = group * 8 + j
            rows = slice(16 * j, 16 * j + 16)
            out[:, leaf * 256 : (leaf + 1) * 256] = local[rows] + total[rows] * jnp.exp(-norms[leaf])


def last(fars, above, norms, received):
    return pl.pallas_call(
        functools.partial(last_kernel, n_far=len(fars)),
        out_shape=jax.ShapeDtypeStruct((16, norms.shape[0] * 256), f32),
        in_specs=[VMEM] * (2 + len(fars) + len(received)),
        out_specs=VMEM,
        compiler_params=params(),
        cost_estimate=cost(),
        name="last_sum",
    )(*fars, above, norms, *received)


def spread(number, bits):
    return sum(((number >> k) & 1) << b for k, b in enumerate(bits))


def compress(number, bits):
    return sum(((number >> b) & 1) << k for k, b in enumerate(bits))


def swap(value, mask):
    pairs = [(d, d ^ mask) for d in range(lax.axis_size("leaf"))]
    return lax.ppermute(value, "leaf", pairs)


def after(value, *others):
    return lax.optimization_barrier((value,) + others)[0]


def shards(
    points,
    charges,
    leaf_order,
    near_owner,
    near_slot,
    far_list,
    far_count,
    leaf_interp,
    leaf_skel,
    inner_interp,
    inner_skel,
    top_interp,
    top_skel,
):
    device_count = lax.axis_size("leaf")
    bits = device_count.bit_length() - 1
    source_bits = tuple(b for b in range(bits) if b not in TARGET_BITS)
    outer_bits = source_bits[1:]
    device = lax.axis_index("leaf")
    leaves = near_owner.shape[0]
    me = device.reshape(1).astype(jnp.int32)
    mates = range(1, 2 ** len(TARGET_BITS))
    early_bits = outer_bits[:-1]
    late = 2 ** outer_bits[-1]

    def codes_of(owner, slot, first):
        other = owner ^ device
        target_mask = sum(2**b for b in TARGET_BITS)
        place = compress(other, source_bits) * leaves + slot
        here = jnp.where((other & target_mask) == 0, 1, 0)
        near_half = leaves << (len(source_bits) - 1)
        is_late = place >= near_half
        place = place & (near_half - 1)
        is_last = is_late & (place >= 2 * leaves)
        piece = place // leaves
        is_first = ~is_late & (first == 0) & ((piece < 2) | (piece % 2 == 0))
        phase = jnp.where(is_last, 2, jnp.where(is_first, 0, 1))
        first_place = place - (piece - jnp.where(piece < 2, piece, piece // 2 + 1)) * leaves
        place = jnp.where(
            is_last,
            place - 2 * leaves,
            jnp.where(is_late, near_half + place, jnp.where(is_first, first_place, place)),
        )
        target = lax.broadcasted_iota(jnp.int32, owner.shape, 1) & 7
        return (here << (phase + PHASE_BIT)) | (target << 16) | place

    def payload_codes(payload, first):
        near = payload[-2 * near_owner.shape[1] :, :leaves].astype(jnp.int32)
        return codes_of(near[: near_owner.shape[1]], near[near_owner.shape[1] :], first)

    owner, slot = near_owner.T, near_slot.T
    src, tgt, cols, loads, rows, norms, mine, interps, skels = first_part(
        points, charges, leaf_order, owner, slot,
        leaf_interp, leaf_skel, inner_interp, inner_skel, top_interp, top_skel,
    )
    pieces = {0: src, late: swap(src, late)}
    for b in reversed(early_bits):
        pieces[2**b] = swap(src, 2**b)
    beside = swap(tgt, 2 ** TARGET_BITS[0])
    far_away = swap(tgt, 2 ** TARGET_BITS[1])
    pieces[1] = swap(mine, 1)

    def far(call, codes, token):
        return self_and_far(
            codes, after(far_list, token), far_count, cols, loads, rows, call, 2
        )

    far0, lists0 = far(0, [codes_of(owner, slot, 0)], norms)
    node = climb(me, after(mine, far0, beside), pieces[1], skels, interps, 0, 0)
    siblings = [pieces[1], swap(node, 2)]
    far1, lists1 = far(1, [payload_codes(after(beside, far0), 0)], node)
    last_targets = swap(after(far_away, far1), 2 ** TARGET_BITS[0])
    for n, b in enumerate(early_bits):
        for low in range(2**n):
            place = spread(low, early_bits[:n])
            if low:
                pieces[place | 2**b] = swap(pieces[place], 2**b)
    wanted = [spread(k, source_bits) for k in range(2 ** (len(source_bits) - 1))]
    targets = [tgt, beside, far_away, last_targets]
    lists = lists0 + lists1
    sums, far_tables1, far_tables2 = near(
        0,
        [tables[0] for tables in lists],
        targets[:3],
        [pieces[k] for k in wanted if k == 1 or not k & 1],
        codes=payload_codes(after(far_away, far1), 0),
    )
    node = climb(me, node, after(siblings[1], sums), skels, interps, 1, 1)
    for k in wanted[2::2]:
        pieces[k | 1] = swap(after(pieces[k], node), 1)
    pieces[late] = after(pieces[late], node)
    for n, b in enumerate(early_bits):
        for low in range(2**n):
            place = spread(low, early_bits[:n]) | late
            pieces[place | 2**b] = swap(pieces[place], 2**b)
    pieces[late | 1] = swap(pieces[late], 1)
    height, row = 2, 2
    others = [swap(node, k * 2**height) for k in (1, 2, 3)]
    sums, last_table = near(
        1,
        [tables[1] for tables in lists] + [far_tables1],
        targets,
        [pieces[k] for k in wanted + [late, late | 1]],
        codes=payload_codes(after(last_targets, node), 1),
        before=sums,
    )
    others[0] = after(others[0], sums)
    while height + 1 < bits:
        if height > 2:
            others = [swap(node, k * 2**height) for k in (1, 2, 3)]
        sibling, node = climb_two(me, node, others, skels, interps, height, row)
        siblings += [others[0], sibling]
        height, row = height + 2, row + 3
    if height < bits:
        siblings.append(swap(node, 2**height))
    for k in wanted[2::2]:
        pieces[k | late | 1] = swap(after(pieces[k | late], node), 1)
    parts = near(
        2,
        [tables[2] for tables in lists] + [far_tables2, after(last_table, node)],
        targets,
        [pieces[k | late] for k in wanted[2:]],
        before=sums,
    )
    siblings[-1] = after(siblings[-1], parts[0])
    received = [parts[0]] + [
        swap(after(parts[k], siblings[-1]), spread(k, TARGET_BITS)) for k in mates
    ]
    above = top(siblings, after(rows, parts[0]))
    return last((far0, far1), above, norms, received)


def solution(mesh):
    in_specs = (
        P(None, "leaf"),
        P(None, "leaf"),
        P("leaf"),
        P("leaf", None),
        P("leaf", None),
        P("leaf", None),
        P("leaf"),
        P("leaf", None, None),
        P("leaf", None),
        P("leaf", None, None),
        P("leaf", None),
        P(),
        P(),
    )
    out_specs = P(None, "leaf")
    return jax.shard_map(shards, mesh=mesh, in_specs=in_specs, out_specs=out_specs, check_vma=False)
```

```python
import functools

import jax
import jax.numpy as jnp
from jax import lax
from jax.experimental import pallas as pl
from jax.experimental.pallas import tpu as pltpu
from jax.sharding import PartitionSpec as P

TARGET_BITS = (1, 3)
STEPS = (8, 4, 2)
DUMMY = 1 << 30
PHASE_BIT = 24
CODE = (1 << PHASE_BIT) - 1
VMEM_LIMIT = 24 * 1024 * 1024
FIRST_LIMIT = 58 * 1024 * 1024
PHASES = 3
bf16 = jnp.bfloat16
f32 = jnp.float32

VMEM = pl.BlockSpec(memory_space=pltpu.VMEM)
SMEM = pl.BlockSpec(memory_space=pltpu.SMEM)
ANY = pl.BlockSpec(memory_space=pl.ANY)
HBM = pl.BlockSpec(memory_space=pltpu.HBM)


def params(limit=VMEM_LIMIT):
    return pltpu.CompilerParams(vmem_limit_bytes=limit)


def cost():
    return pl.CostEstimate(flops=1, bytes_accessed=1, transcendentals=0)


def dot(a, b):
    return lax.dot_general(a, b, (((1,), (0,)), ((), ())), preferred_element_type=f32)


def dot_nt(a, b):
    return lax.dot_general(a, b, (((1,), (1,)), ((), ())), preferred_element_type=f32)


def split3(value):
    hi = value.astype(bf16).astype(f32)
    rest = value - hi
    mid = rest.astype(bf16).astype(f32)
    return hi, mid, rest - mid


def norm_row(coords):
    wide = coords.astype(f32)
    return jnp.sum(wide * wide, axis=0, keepdims=True) * 0.125


def extra_rows(norms, first):
    hi, mid, lo = split3(-norms)
    row = lax.broadcasted_iota(jnp.int32, (16, norms.shape[1]), 0)
    one_at = 3 - first
    out = jnp.where((row >= one_at) & (row < one_at + 3), 1.0, 0.0)
    out = jnp.where(row == first, hi, out)
    out = jnp.where(row == first + 1, mid, out)
    return jnp.where(row == first + 2, lo, out)


def source_matrix(coords, norms):
    width = coords.shape[1]
    extra = extra_rows(norms, 0).astype(bf16)
    return jnp.concatenate([coords, extra, jnp.zeros((48, width), bf16)], axis=0)


def target_matrix(coords, norms):
    width = coords.shape[1]
    extra = extra_rows(norms, 3)
    wide = jnp.concatenate(
        [coords.astype(f32) * 0.25, extra, jnp.zeros((48, width), f32)], axis=0
    )
    return jnp.transpose(wide).astype(bf16)


def tiles_sum(count, exponent, weight):
    total = None
    value = None
    ahead = exponent(0)
    for u in range(count):
        now = ahead
        if u + 1 < count:
            ahead = exponent(u + 1)
        if value is not None:
            part = dot_nt(value, weight(u - 1))
            total = part if total is None else total + part
        value = jnp.exp(now).astype(bf16)
    part = dot_nt(value, weight(count - 1))
    return part if total is None else total + part


def placed(loads, place):
    zero = jnp.zeros_like(loads)
    return jnp.concatenate(
        [jnp.where(place == k, loads, zero) for k in range(8)], axis=0
    )


def onehot(picks, size):
    row = lax.broadcasted_iota(jnp.int32, (size, picks.shape[1]), 0)
    return jnp.where(row == picks, 1.0, 0.0).astype(bf16)


def combine(left, right, picks, interp):
    both = jnp.concatenate([left, right], axis=1)
    coords = dot(both[:64], onehot(picks, 256)).astype(bf16)
    load = dot(both[64:], interp).astype(bf16)
    return jnp.concatenate([coords, load], axis=0)


def spread(number, bits):
    return sum(((number >> k) & 1) << b for k, b in enumerate(bits))


def compress(number, bits):
    return sum(((number >> b) & 1) << k for k, b in enumerate(bits))


def codes_of(owner, slot, first, leaves):
    bits = lax.axis_size("leaf").bit_length() - 1
    source_bits = [b for b in range(bits) if b not in TARGET_BITS]
    other = owner ^ lax.axis_index("leaf")
    place = compress(other, source_bits) * leaves + slot
    here = jnp.where((other & sum(2**b for b in TARGET_BITS)) == 0, 1, 0)
    half = 2 ** (len(source_bits) - 1)
    is_late = place >= half * leaves
    place = place & (half * leaves - 1)
    is_last = is_late & (place >= 2 * leaves)
    piece = place >> (leaves.bit_length() - 1)
    is_first = jnp.logical_not(is_late) & ((piece < 2) | ((piece & 1) == 0))
    if first != 0:
        is_first = is_first & (piece < 0)
    phase = jnp.where(is_last, 2, jnp.where(is_first, 0, 1))
    first_place = place - (piece - jnp.where(piece < 2, piece, (piece >> 1) + 1)) * leaves
    place = jnp.where(
        is_last,
        place - 2 * leaves,
        jnp.where(is_late, half * leaves + place, jnp.where(is_first, first_place, place)),
    )
    target = lax.broadcasted_iota(jnp.int32, owner.shape, 1) & 7
    return (here << (phase + PHASE_BIT)) | (target << 16) | place


def first_kernel(
    order, points_in, charges_in, owner_in, slot_in,
    leaf_interp_in, leaf_skel_in, inner_interp_in, inner_skel_in, top_interp, top_skel,
    src_out, tgt_out, cols_out, loads_out, rows_out, norms_out, mine_out, interps_out, skels_out, codes_out,
    points, charges, owner, slot, unsorted, buffer0, buffer1, src, tgt, cols, loads, rows, norms,
    joined, root, interps, skels, codes, leaf_interp, leaf_skel, inner_interp, inner_skel, sems,
):
    count = points.shape[1]
    chunks = 4
    width = count // chunks
    begun = []

    def begin(a, b):
        copy = pltpu.make_async_copy(a, b, sems.at[len(begun)])
        copy.start()
        begun.append(copy)
        return copy

    parts = [begin(charges_in, charges)]
    for c in range(chunks):
        at = pl.ds(c * width, width)
        parts.append(begin(points_in.at[:, at], points.at[:, at]))
    near_lists = [begin(owner_in, owner), begin(slot_in, slot)]
    needed = [
        begin(leaf_skel_in, leaf_skel),
        begin(leaf_interp_in, leaf_interp),
        begin(inner_skel_in, inner_skel),
        begin(inner_interp_in, inner_interp),
    ]
    rest = []
    path = path_rows()
    on_path = []
    for k in range(interps_out.shape[0]):
        on_path.append(begin(top_interp.at[path[k]], interps.at[k]))
        on_path.append(begin(top_skel.at[pl.ds(path[k], 1)], skels.at[k]))

    parts[0].wait()
    for c in range(count // 128):
        at = slice(c * 128, (c + 1) * 128)
        if c * 128 % width == 0:
            parts[1 + c * 128 // width].wait()
        block = jnp.concatenate(
            [
                points[:, at].astype(f32),
                charges[:, at].astype(f32),
                jnp.zeros((48, 128), f32),
            ],
            axis=0,
        )
        unsorted[at, :] = jnp.transpose(block)

    leaves = src.shape[0]
    first_node = 2 * leaves
    lane = lax.broadcasted_iota(jnp.int32, (256, 128), 1)

    def finish(node, both):
        joined[node] = both
        cols[first_node + node] = source_matrix(both[:64], norm_row(both[:64]))
        loads[first_node + node] = both[64:]

    def copy_rows(pair, buffer):
        base = pl.multiple_of(pair * 512, 512)
        for u in range(512):
            buffer[u : u + 1, :] = unsorted[pl.ds(order[base + u], 1), :]

    def process(pair, buffer):
        even = buffer[:256]
        odd = buffer[256:]
        both = jnp.where(lane < 64, even, pltpu.roll(odd, 64, 1))
        tgt[pl.ds(pl.multiple_of(pair * 256, 256), 256), :] = (both * 0.25).astype(bf16)
        for k, mine in enumerate((even, odd)):
            i = 2 * pair + k
            both = jnp.transpose(mine)[:80].astype(bf16)
            src[i] = both
            coords, load = both[:64], both[64:]
            norm = norm_row(coords)
            norms[i] = norm
            rows[i] = target_matrix(coords, norm)
            matrix = source_matrix(coords, norm)
            for half in range(2):
                cols[2 * i + half] = matrix[:, half * 128 : half * 128 + 128]
                loads[2 * i + half] = load[:, half * 128 : half * 128 + 128]
            picked = dot(coords, onehot(leaf_skel[pl.ds(i, 1), :], 256)).astype(bf16)
            value = dot(load, leaf_interp[i]).astype(bf16)
            finish(i, jnp.concatenate([picked, value], axis=0))

    for copy in needed:
        copy.wait()

    def two_pairs(i, carry):
        copy_rows(2 * i, buffer0)
        process(jnp.maximum(2 * i - 1, 0), buffer1)
        copy_rows(2 * i + 1, buffer1)
        process(2 * i, buffer0)
        return carry

    lax.fori_loop(0, leaves // 4, two_pairs, 0)
    process(leaves // 2 - 1, buffer1)
    for copy in near_lists + on_path:
        copy.wait()
    codes[...] = codes_of(owner[...], slot[...], 0, leaves)
    rest += [begin(interps, interps_out), begin(skels, skels_out), begin(codes, codes_out)]
    near = jnp.concatenate([owner[...].astype(f32), slot[...].astype(f32)], axis=0)
    blank = jnp.zeros((near.shape[0], 128 - near.shape[1]), f32)
    tgt[count // 2 :, :] = jnp.concatenate([near, blank], axis=1).astype(bf16)
    rest += [begin(src, src_out), begin(tgt, tgt_out), begin(src, mine_out.at[pl.ds(0, leaves)])]
    rest += [begin(rows, rows_out), begin(norms, norms_out)]
    tiles = pl.ds(0, 3 * leaves)
    rest += [begin(cols.at[tiles], cols_out.at[tiles])]
    first, half = 0, leaves // 2
    number, row = leaves, 0
    while half > 0:
        for j in range(half):
            left = joined[first + 2 * j]
            right = joined[first + 2 * j + 1]
            finish(number, combine(left, right, inner_skel[row : row + 1, :], inner_interp[row]))
            number, row = number + 1, row + 1
        first = first + 2 * half
        half = half // 2
    node = joined[2 * leaves - 2]
    root[...] = jnp.concatenate([node, jnp.zeros_like(node)], axis=1)
    last = cols.shape[0] - 1
    cols[last] = jnp.zeros((128, 128), bf16)
    loads[last] = jnp.zeros((16, 128), bf16)
    inner_tiles = pl.ds(3 * leaves, leaves)
    rest += [begin(root, mine_out.at[leaves]), begin(loads, loads_out)]
    rest += [begin(cols.at[inner_tiles], cols_out.at[inner_tiles])]
    for copy in rest:
        copy.wait()


def path_rows():
    devices = lax.axis_size("leaf")
    device = lax.axis_index("leaf")
    bits = devices.bit_length() - 1

    def row_at(height, node):
        return devices - (devices >> (height - 1)) + node

    path = [row_at(1, device >> 1), row_at(2, device >> 2)]
    for height in range(2, bits - 1, 2):
        up = device >> (height + 1)
        path += [row_at(height + 1, up), row_at(height + 1, up ^ 1)]
        path.append(row_at(min(height + 2, bits - 1), up >> 1))
    return path


def first_part(points, charges, order, owner, slot, *tables):
    count = points.shape[1]
    leaves = count // 256
    tiles = 4 * leaves
    steps = len(path_rows())
    leaf_interp, leaf_skel, inner_interp, inner_skel = tables[:4]
    src = (leaves, 80, 256)
    tgt = (count // 2 + 2 * owner.shape[0], 128)
    cols = (tiles, 128, 128)
    loads = (tiles, 16, 128)
    rows = (leaves, 256, 128)
    norms = (leaves, 1, 256)
    shapes = [
        (src, bf16),
        (tgt, bf16),
        (cols, bf16),
        (loads, bf16),
        (rows, bf16),
        (norms, f32),
        ((leaves + 1, 80, 256), bf16),
        ((steps, 256, 128), bf16),
        ((steps, 1, 128), jnp.int32),
        (owner.shape, jnp.int32),
    ]
    held = [
        (points.shape, bf16),
        (charges.shape, bf16),
        (owner.shape, jnp.int32),
        (slot.shape, jnp.int32),
        ((count, 128), f32),
        ((512, 128), f32),
        ((512, 128), f32),
    ]
    held += shapes[:6]
    held += [((2 * leaves - 1, 80, 128), bf16), ((80, 256), bf16)]
    held += shapes[7:]
    held += [(table.shape, table.dtype) for table in tables[:4]]
    return pl.pallas_call(
        first_kernel,
        out_shape=tuple(jax.ShapeDtypeStruct(*shape) for shape in shapes),
        in_specs=[SMEM] + [ANY] * 10,
        out_specs=(ANY,) * 10,
        scratch_shapes=[pltpu.VMEM(*shape) for shape in held]
        + [pltpu.SemaphoreType.DMA((24 + 2 * steps,))],
        compiler_params=params(FIRST_LIMIT),
        cost_estimate=cost(),
        name="order_and_subtree",
    )(order, points, charges, owner, slot, *tables)


def far_kernel(*refs, first_leaf, n_leaves, n_ids):
    codes = refs[:n_ids]
    far_list, far_count, cols_in, loads_in, rows_in, acc = refs[n_ids : 6 + n_ids]
    lists = refs[6 + n_ids : -5]
    cols, loads, rows, tiles, sems = refs[-5:]
    leaves = rows.shape[0]
    width = far_list.shape[1]
    first_node = 2 * leaves
    empty = cols.shape[0] - 1
    mine = pl.ds(first_leaf, n_leaves)
    my_tiles = pl.ds(2 * first_leaf, 2 * n_leaves)
    nodes = pl.ds(first_node, cols.shape[0] - first_node)
    copies = [
        pltpu.make_async_copy(rows_in.at[mine], rows.at[mine], sems.at[0]),
        pltpu.make_async_copy(cols_in.at[my_tiles], cols.at[my_tiles], sems.at[1]),
        pltpu.make_async_copy(loads_in, loads, sems.at[2]),
        pltpu.make_async_copy(cols_in.at[nodes], cols.at[nodes], sems.at[3]),
    ]
    for copy in copies:
        copy.start()

    def list_leaf(k, count):
        i = first_leaf + k
        tiles[count] = (i << 16) | ((2 * i) << 8) | (2 * i + 1)
        count = count + 1
        used = far_count[i]
        for k in range(0, width, 2):
            first = far_list[i, k] + first_node
            second = jnp.where(k + 1 < used, far_list[i, k + 1] + first_node, empty)
            tiles[count] = (i << 16) | (first << 8) | second
            count = count + (k < used).astype(jnp.int32)
        return count

    count = lax.fori_loop(0, n_leaves, list_leaf, 0)
    tiles[count] = (empty << 8) | empty
    count = (count + 1) & ~1

    def step(start, size):
        values, weights = [], []
        for u in range(size):
            packed = tiles[start + u]
            leaf = packed >> 16
            first = (packed >> 8) & 255
            second = packed & 255
            matrix = jnp.concatenate([cols[first], cols[second]], axis=1)
            load = jnp.concatenate([loads[first], loads[second]], axis=1)
            values.append(jnp.exp(dot(rows[leaf], matrix)).astype(bf16))
            weights.append(placed(load, leaf & 7))
        acc[...] += dot_nt(jnp.concatenate(values, axis=1), jnp.concatenate(weights, axis=1))

    acc[...] = jnp.zeros_like(acc)
    for k in range(n_ids):
        list_pairs(codes[k], lists[PHASES * k : PHASES * k + PHASES])
    for copy in copies:
        copy.wait()
    largest = STEPS[0]
    whole = lax.div(count, largest)

    def full_step(i, carry):
        step(i * largest, largest)
        return carry

    lax.fori_loop(0, whole, full_step, 0)
    for size in STEPS[1:]:

        @pl.when((count & size) > 0)
        def _(size=size):
            step(count & ~(2 * size - 1), size)


def list_pairs(codes, tables):
    per_leaf, leaves = codes.shape
    for g in range(leaves // 8):
        counts = [jnp.int32(0)] * len(tables)
        for j in range(8):
            for u in range(per_leaf):
                value = codes[u, g * 8 + j]
                for p, table in enumerate(tables):
                    if table is None:
                        continue
                    table[g, 1 + counts[p]] = value & CODE
                    counts[p] = counts[p] + ((value >> (PHASE_BIT + p)) & 1)
        for p, table in enumerate(tables):
            if table is None:
                continue
            table[g, 1 + counts[p]] = DUMMY
            table[g, 0] = (counts[p] + 1) & ~1


def pair_table(leaves):
    return jax.ShapeDtypeStruct((leaves // 8, 128), jnp.int32)


def self_and_far(codes, far_list, far_count, cols, loads, rows, call, calls):
    leaves = rows.shape[0]
    width = far_list.shape[1]
    n_leaves = leaves // calls
    out = pl.pallas_call(
        functools.partial(
            far_kernel, first_leaf=call * n_leaves, n_leaves=n_leaves, n_ids=len(codes)
        ),
        out_shape=(jax.ShapeDtypeStruct((256, 128), f32),) + (pair_table(leaves),) * (PHASES * len(codes)),
        in_specs=[SMEM] * (2 + len(codes)) + [ANY] * 3,
        out_specs=(VMEM,) + (SMEM,) * (PHASES * len(codes)),
        scratch_shapes=[
            pltpu.VMEM(cols.shape, bf16),
            pltpu.VMEM(loads.shape, bf16),
            pltpu.VMEM(rows.shape, bf16),
            pltpu.SMEM((n_leaves * (1 + width // 2) + 2,), jnp.int32),
            pltpu.SemaphoreType.DMA((4,)),
        ],
        compiler_params=params(FIRST_LIMIT),
        cost_estimate=cost(),
        name=f"self_and_far{call}",
    )(*codes, far_list, far_count, cols, loads, rows)
    return out[0], [out[1 + PHASES * k : 1 + PHASES * k + PHASES] for k in range(len(codes))]


def near_kernel(*refs, n_sources, n_targets, n_lists, phase):
    refs = list(refs)

    def take(n):
        taken = refs[:n]
        del refs[:n]
        return taken

    makes = phase < PHASES - 1
    (codes,) = take(1) if makes else (None,)
    lists = take(n_lists)
    target_parts = take(n_targets)
    source_parts = take(n_sources)
    before = take(phase > 0)
    outs = take(n_targets) if not makes else []
    (acc,) = take(1) if makes else (None,)
    tables = take(PHASES - 1 - phase) if makes else []
    sources, targets, sems, pairs, steps = take(5)
    if not makes:
        (acc,) = refs
    leaves = source_parts[0].shape[0]
    size = leaves * 128
    copies = []

    def begin(part, place):
        copies.append(pltpu.make_async_copy(part, place, sems.at[len(copies)]))
        copies[-1].start()

    own_rows = acc.shape[0] // n_targets
    for k, part in enumerate(lists):
        begin(part, pairs.at[pl.ds(k * own_rows, own_rows)])
    done = 0
    for part in before:
        done = part.shape[0]
        begin(part, acc.at[pl.ds(0, done)])
    for k, part in enumerate(target_parts):
        begin(part.at[pl.ds(0, size)], targets.at[pl.ds(k * size, size)])
    for k, part in enumerate(source_parts):
        begin(part.at[pl.ds(0, leaves)], sources.at[pl.ds(k * leaves, leaves)])
    if done < acc.shape[0]:
        acc[done:] = jnp.zeros((acc.shape[0] - done,) + acc.shape[1:], f32)
    if makes:
        table = pairs.at[pl.ds(n_lists * own_rows, own_rows)]
        list_pairs(codes, [None] * phase + [table] + tables)
    for copy in copies:
        copy.wait()

    counts = [jnp.int32(0)] * len(STEPS)
    for row in range(pairs.shape[0]):
        used = pairs[row, 0]
        whole = lax.div(used, STEPS[0])

        def note(i, count, row=row):
            steps[0, count + i] = row * 128 + 1 + i * STEPS[0]
            return count

        lax.fori_loop(0, whole, note, counts[0])
        counts[0] = counts[0] + whole
        for k, size in enumerate(STEPS[1:], 1):
            steps[k, counts[k]] = row * 128 + 1 + (used & ~(2 * size - 1))
            counts[k] = counts[k] + jnp.where((used & size) > 0, 1, 0)

    for k, size in enumerate(STEPS):

        def step(i, carry, k=k, size=size):
            group = steps[k, i] >> 7
            start = steps[k, i] & 127

            def exponent(u):
                packed = pairs[group, start + u]
                target = (packed >> 16) & 7
                coords = sources[packed & 65535, :64, :]
                odd = target & 1
                zero = jnp.zeros_like(coords)
                matrix = jnp.concatenate(
                    [jnp.where(odd == 0, coords, zero), jnp.where(odd == 1, coords, zero)],
                    axis=0,
                )
                at = pl.multiple_of(group * 1024 + (target >> 1) * 256, 256)
                return dot(targets[pl.ds(at, 256), :], matrix) - norm_row(coords)

            def weight(u):
                packed = pairs[group, start + u]
                place = jnp.where(packed < DUMMY, (packed >> 16) & 7, 8)
                return placed(sources[packed & 65535, 64:, :], place)

            acc[group] += tiles_sum(size, exponent, weight)
            return carry

        lax.fori_loop(0, counts[k], step, 0)

    each = acc.shape[0] // n_targets
    for k, out in enumerate(outs):
        out[...] = acc[k * each : (k + 1) * each].astype(bf16)


def near(phase, lists, targets, sources, codes=None, before=None):
    n_sources, n_targets = len(sources), len(targets)
    leaves = min(source.shape[0] for source in sources)
    sums = jax.ShapeDtypeStruct((n_targets * leaves // 8, 256, 128), f32)
    part = jax.ShapeDtypeStruct((leaves // 8, 256, 128), bf16)
    makes = phase < PHASES - 1
    args = ([codes] if makes else []) + list(lists) + list(targets) + list(sources)
    args += [] if before is None else [before]
    n_smem = int(makes)
    n_tables = PHASES - 1 - phase
    if makes:
        out_shape = (sums,) + (pair_table(leaves),) * n_tables
        out_specs = (VMEM,) + (SMEM,) * n_tables
    else:
        out_shape, out_specs = (part,) * n_targets, (VMEM,) * n_targets
    scratch = [
        pltpu.VMEM((n_sources * leaves, 80, 256), bf16),
        pltpu.VMEM((n_targets * leaves * 128, 128), bf16),
        pltpu.SemaphoreType.DMA((n_sources + n_targets + len(lists) + 1,)),
        pltpu.SMEM((n_targets * leaves // 8, 128), jnp.int32),
        pltpu.SMEM((len(STEPS), n_targets * leaves), jnp.int32),
    ]
    if not makes:
        scratch.append(pltpu.VMEM(sums.shape, f32))
    return pl.pallas_call(
        functools.partial(
            near_kernel, n_sources=n_sources, n_targets=n_targets, n_lists=len(lists), phase=phase
        ),
        out_shape=out_shape,
        in_specs=[SMEM] * n_smem + [ANY] * (len(args) - n_smem),
        out_specs=out_specs,
        scratch_shapes=scratch,
        compiler_params=params(),
        cost_estimate=cost(),
        name=f"near{phase}",
    )(*args)


def ordered(first, second, test):
    return jnp.where(test, first, second), jnp.where(test, second, first)


def climb_kernel(me, own, other, skels, interps, parent, *, height, row):
    sibling = other[0, :, :128] if len(other.shape) == 3 else other[...]
    left, right = ordered(own[0, :, :128] if len(own.shape) == 3 else own[...], sibling, ((me[0] >> height) & 1) == 0)
    parent[...] = combine(left, right, skels[row], interps[row])


def last_block(value):
    if value.ndim == 2:
        return VMEM
    blocks = value.shape[0]
    return pl.BlockSpec((1,) + value.shape[1:], lambda i: (blocks - 1, 0, 0))


def climb(me, own, other, skels, interps, height, row):
    return pl.pallas_call(
        functools.partial(climb_kernel, height=height, row=row),
        grid=(1,),
        out_shape=jax.ShapeDtypeStruct((80, 128), bf16),
        in_specs=[SMEM, last_block(own), last_block(other), VMEM, VMEM],
        out_specs=VMEM,
        compiler_params=params(),
        cost_estimate=cost(),
        name=f"climb{height}",
    )(me, own, other, skels, interps)


def climb_two_kernel(me, own, one, two, three, skels, interps, sibling, parent, *, height, row):
    node = me[0] >> height
    is_left = (node & 1) == 0
    left, right = ordered(own[...], one[...], is_left)
    mine = combine(left, right, skels[row], interps[row])
    left, right = ordered(two[...], three[...], is_left)
    other = combine(left, right, skels[row + 1], interps[row + 1])
    sibling[...] = other
    left, right = ordered(mine, other, (node & 2) == 0)
    parent[...] = combine(left, right, skels[row + 2], interps[row + 2])


def climb_two(me, own, others, skels, interps, height, row):
    node = jax.ShapeDtypeStruct((80, 128), bf16)
    return pl.pallas_call(
        functools.partial(climb_two_kernel, height=height, row=row),
        out_shape=(node, node),
        in_specs=[SMEM] + [VMEM] * 6,
        out_specs=(VMEM, VMEM),
        compiler_params=params(),
        cost_estimate=cost(),
        name=f"climb{height}",
    )(me, own, *others, skels, interps)


def top_kernel(*refs):
    parts, (rows, acc, cols, loads) = refs[:-4], refs[-4:]
    for t, part in enumerate(parts):
        node = part[0, :, :128] if len(part.shape) == 3 else part[...]
        cols[:, t * 128 : (t + 1) * 128] = source_matrix(node[:64], norm_row(node[:64]))
        loads[:, t * 128 : (t + 1) * 128] = jnp.concatenate([node[64:]] * 8, axis=0)
    lane = lax.broadcasted_iota(jnp.int32, (256, 128), 1) >> 4

    def two_leaves(i, carry):
        both = rows[pl.ds(2 * i, 2)].reshape(512, 128)
        value = jnp.exp(dot(both, cols[...])).astype(bf16)
        result = dot_nt(value, loads[...])
        group = lax.div(i, 4)
        place = (2 * i) & 7
        acc[group] += jnp.where(lane == place, result[:256], 0.0) + jnp.where(
            lane == place + 1, result[256:], 0.0
        )
        return carry

    acc[...] = jnp.zeros_like(acc)
    lax.fori_loop(0, rows.shape[0] // 2, two_leaves, 0, unroll=2)


def top(parts, rows):
    levels = len(parts)
    return pl.pallas_call(
        top_kernel,
        out_shape=jax.ShapeDtypeStruct((rows.shape[0] // 8, 256, 128), f32),
        grid=(1,),
        in_specs=[last_block(part) for part in parts] + [VMEM],
        out_specs=VMEM,
        scratch_shapes=[
            pltpu.VMEM((128, levels * 128), bf16),
            pltpu.VMEM((128, levels * 128), bf16),
        ],
        compiler_params=params(),
        cost_estimate=cost(),
        name="top",
    )(*parts, rows)


def last_kernel(*refs, n_far):
    fars = refs[:n_far]
    above, norms = refs[n_far : n_far + 2]
    received, out = refs[n_far + 2 : -1], refs[-1]
    groups = above.shape[0]
    for group in range(groups):
        local = above[group]
        for far in fars[group * n_far // groups : (group + 1) * n_far // groups]:
            local = local + far[...]
        local = jnp.transpose(local)
        total = received[0][group].astype(f32)
        for part in received[1:]:
            total = total + part[group].astype(f32)
        total = jnp.transpose(total)
        for j in range(8):
            leaf = group * 8 + j
            rows = slice(16 * j, 16 * j + 16)
            out[:, leaf * 256 : (leaf + 1) * 256] = local[rows] + total[rows] * jnp.exp(-norms[leaf])


def last(fars, above, norms, received):
    return pl.pallas_call(
        functools.partial(last_kernel, n_far=len(fars)),
        out_shape=jax.ShapeDtypeStruct((16, norms.shape[0] * 256), f32),
        in_specs=[VMEM] * (2 + len(fars) + len(received)),
        out_specs=VMEM,
        compiler_params=params(),
        cost_estimate=cost(),
        name="last_sum",
    )(*fars, above, norms, *received)


def swap(value, mask):
    pairs = [(d, d ^ mask) for d in range(lax.axis_size("leaf"))]
    return lax.ppermute(value, "leaf", pairs)


def after(value, *others):
    return lax.optimization_barrier((value,) + others)[0]


def shards(
    points,
    charges,
    leaf_order,
    near_owner,
    near_slot,
    far_list,
    far_count,
    leaf_interp,
    leaf_skel,
    inner_interp,
    inner_skel,
    top_interp,
    top_skel,
):
    device_count = lax.axis_size("leaf")
    bits = device_count.bit_length() - 1
    source_bits = tuple(b for b in range(bits) if b not in TARGET_BITS)
    outer_bits = source_bits[1:]
    device = lax.axis_index("leaf")
    leaves = near_owner.shape[0]
    me = device.reshape(1).astype(jnp.int32)
    mates = range(1, 2 ** len(TARGET_BITS))
    early_bits = outer_bits[:-1]
    late = 2 ** outer_bits[-1]

    def payload_codes(payload, first):
        near = payload[-2 * near_owner.shape[1] :, :leaves].astype(jnp.int32)
        return codes_of(near[: near_owner.shape[1]], near[near_owner.shape[1] :], first, leaves)

    owner, slot = near_owner.T, near_slot.T
    src, tgt, cols, loads, rows, norms, mine, interps, skels, codes = first_part(
        points, charges, leaf_order, owner, slot,
        leaf_interp, leaf_skel, inner_interp, inner_skel, top_interp, top_skel,
    )
    pieces = {0: src, late: swap(src, late)}
    for b in reversed(early_bits):
        pieces[2**b] = swap(src, 2**b)
    beside = swap(tgt, 2 ** TARGET_BITS[0])
    far_away = swap(tgt, 2 ** TARGET_BITS[1])
    pieces[1] = swap(mine, 1)

    def far(call, codes, token):
        return self_and_far(
            codes, after(far_list, token), far_count, cols, loads, rows, call, 2
        )

    far0, lists0 = far(0, [codes], norms)
    node = climb(me, after(mine, far0, beside), pieces[1], skels, interps, 0, 0)
    siblings = [pieces[1], swap(node, 2)]
    far1, lists1 = far(1, [payload_codes(after(beside, far0), 0)], node)
    last_targets = swap(after(far_away, far1), 2 ** TARGET_BITS[0])
    for n, b in enumerate(early_bits):
        for low in range(2**n):
            place = spread(low, early_bits[:n])
            if low:
                pieces[place | 2**b] = swap(pieces[place], 2**b)
    wanted = [spread(k, source_bits) for k in range(2 ** (len(source_bits) - 1))]
    targets = [tgt, beside, far_away, last_targets]
    lists = lists0 + lists1
    sums, far_tables1, far_tables2 = near(
        0,
        [tables[0] for tables in lists],
        targets[:3],
        [pieces[k] for k in wanted if k == 1 or not k & 1],
        codes=payload_codes(after(far_away, far1), 0),
    )
    node = climb(me, node, after(siblings[1], sums), skels, interps, 1, 1)
    for k in wanted[2::2]:
        pieces[k | 1] = swap(after(pieces[k], node), 1)
    pieces[late] = after(pieces[late], node)
    for n, b in enumerate(early_bits):
        for low in range(2**n):
            place = spread(low, early_bits[:n]) | late
            pieces[place | 2**b] = swap(pieces[place], 2**b)
    pieces[late | 1] = swap(pieces[late], 1)
    height, row = 2, 2
    others = [swap(node, k * 2**height) for k in (1, 2, 3)]
    sums, last_table = near(
        1,
        [tables[1] for tables in lists] + [far_tables1],
        targets,
        [pieces[k] for k in wanted + [late, late | 1]],
        codes=payload_codes(after(last_targets, node), 1),
        before=sums,
    )
    others[0] = after(others[0], sums)
    while height + 1 < bits:
        if height > 2:
            others = [swap(node, k * 2**height) for k in (1, 2, 3)]
        sibling, node = climb_two(me, node, others, skels, interps, height, row)
        siblings += [others[0], sibling]
        height, row = height + 2, row + 3
    if height < bits:
        siblings.append(swap(node, 2**height))
    for k in wanted[2::2]:
        pieces[k | late | 1] = swap(after(pieces[k | late], node), 1)
    parts = near(
        2,
        [tables[2] for tables in lists] + [far_tables2, after(last_table, node)],
        targets,
        [pieces[k | late] for k in wanted[2:]],
        before=sums,
    )
    siblings[-1] = after(siblings[-1], parts[0])
    received = [parts[0]] + [
        swap(after(parts[k], siblings[-1]), spread(k, TARGET_BITS)) for k in mates
    ]
    above = top(siblings, after(rows, parts[0]))
    return last((far0, far1), above, norms, received)


def solution(mesh):
    in_specs = (
        P(None, "leaf"),
        P(None, "leaf"),
        P("leaf"),
        P("leaf", None),
        P("leaf", None),
        P("leaf", None),
        P("leaf"),
        P("leaf", None, None),
        P("leaf", None),
        P("leaf", None, None),
        P("leaf", None),
        P(),
        P(),
    )
    out_specs = P(None, "leaf")
    return jax.shard_map(shards, mesh=mesh, in_specs=in_specs, out_specs=out_specs, check_vma=False)
```

```python
import functools

import jax
import jax.numpy as jnp
from jax import lax
from jax.experimental import pallas as pl
from jax.experimental.pallas import tpu as pltpu
from jax.sharding import PartitionSpec as P

TARGET_BITS = (1, 3)
STEPS = (8, 4, 2)
DUMMY = 1 << 30
PHASE_BIT = 24
CODE = (1 << PHASE_BIT) - 1
VMEM_LIMIT = 24 * 1024 * 1024
FIRST_LIMIT = 58 * 1024 * 1024
PHASES = 3
bf16 = jnp.bfloat16
f32 = jnp.float32

VMEM = pl.BlockSpec(memory_space=pltpu.VMEM)
SMEM = pl.BlockSpec(memory_space=pltpu.SMEM)
ANY = pl.BlockSpec(memory_space=pl.ANY)
HBM = pl.BlockSpec(memory_space=pltpu.HBM)


def params(limit=VMEM_LIMIT):
    return pltpu.CompilerParams(vmem_limit_bytes=limit)


def cost():
    return pl.CostEstimate(flops=1, bytes_accessed=1, transcendentals=0)


def dot(a, b):
    return lax.dot_general(a, b, (((1,), (0,)), ((), ())), preferred_element_type=f32)


def dot_nt(a, b):
    return lax.dot_general(a, b, (((1,), (1,)), ((), ())), preferred_element_type=f32)


def split3(value):
    hi = value.astype(bf16).astype(f32)
    rest = value - hi
    mid = rest.astype(bf16).astype(f32)
    return hi, mid, rest - mid


def norm_row(coords):
    wide = coords.astype(f32)
    return jnp.sum(wide * wide, axis=0, keepdims=True) * 0.125


def extra_rows(norms, first):
    hi, mid, lo = split3(-norms)
    row = lax.broadcasted_iota(jnp.int32, (16, norms.shape[1]), 0)
    one_at = 3 - first
    out = jnp.where((row >= one_at) & (row < one_at + 3), 1.0, 0.0)
    out = jnp.where(row == first, hi, out)
    out = jnp.where(row == first + 1, mid, out)
    return jnp.where(row == first + 2, lo, out)


def source_matrix(coords, norms):
    width = coords.shape[1]
    extra = extra_rows(norms, 0).astype(bf16)
    return jnp.concatenate([coords, extra, jnp.zeros((48, width), bf16)], axis=0)


def target_matrix(coords, norms):
    width = coords.shape[1]
    extra = extra_rows(norms, 3)
    wide = jnp.concatenate(
        [coords.astype(f32) * 0.25, extra, jnp.zeros((48, width), f32)], axis=0
    )
    return jnp.transpose(wide).astype(bf16)


def tiles_sum(count, exponent, weight):
    total = None
    value = None
    ahead = exponent(0)
    for u in range(count):
        now = ahead
        if u + 1 < count:
            ahead = exponent(u + 1)
        if value is not None:
            part = dot_nt(value, weight(u - 1))
            total = part if total is None else total + part
        value = jnp.exp(now).astype(bf16)
    part = dot_nt(value, weight(count - 1))
    return part if total is None else total + part


def placed(loads, place):
    zero = jnp.zeros_like(loads)
    return jnp.concatenate(
        [jnp.where(place == k, loads, zero) for k in range(8)], axis=0
    )


def onehot(picks, size):
    row = lax.broadcasted_iota(jnp.int32, (size, picks.shape[1]), 0)
    return jnp.where(row == picks, 1.0, 0.0).astype(bf16)


def combine(left, right, picks, interp):
    both = jnp.concatenate([left, right], axis=1)
    coords = dot(both[:64], onehot(picks, 256)).astype(bf16)
    load = dot(both[64:], interp).astype(bf16)
    return jnp.concatenate([coords, load], axis=0)


def spread(number, bits):
    return sum(((number >> k) & 1) << b for k, b in enumerate(bits))


def compress(number, bits):
    return sum(((number >> b) & 1) << k for k, b in enumerate(bits))


def codes_of(owner, slot, first, leaves):
    bits = lax.axis_size("leaf").bit_length() - 1
    source_bits = [b for b in range(bits) if b not in TARGET_BITS]
    other = owner ^ lax.axis_index("leaf")
    place = compress(other, source_bits) * leaves + slot
    here = jnp.where((other & sum(2**b for b in TARGET_BITS)) == 0, 1, 0)
    half = 2 ** (len(source_bits) - 1)
    is_late = place >= half * leaves
    place = place & (half * leaves - 1)
    is_last = is_late & (place >= 2 * leaves)
    piece = place >> (leaves.bit_length() - 1)
    is_first = jnp.logical_not(is_late) & ((piece < 2) | ((piece & 1) == 0))
    if first != 0:
        is_first = is_first & (piece < 0)
    phase = jnp.where(is_last, 2, jnp.where(is_first, 0, 1))
    first_place = place - (piece - jnp.where(piece < 2, piece, (piece >> 1) + 1)) * leaves
    place = jnp.where(
        is_last,
        place - 2 * leaves,
        jnp.where(is_late, half * leaves + place, jnp.where(is_first, first_place, place)),
    )
    target = lax.broadcasted_iota(jnp.int32, owner.shape, 1) & 7
    return (here << (phase + PHASE_BIT)) | (target << 16) | place


def first_kernel(
    order_in, points_in, charges_in, owner_in, slot_in,
    leaf_interp_in, leaf_skel_in, inner_interp_in, inner_skel_in, top_interp, top_skel,
    src_out, tgt_out, cols_out, loads_out, rows_out, norms_out, mine_out, interps_out, skels_out, codes_out,
    points, charges, owner, slot, unsorted, buffer0, buffer1, src, tgt, cols, loads, rows, norms,
    joined, root, interps, skels, codes, order, leaf_interp, leaf_skel, inner_interp, inner_skel, sems,
):
    count = points.shape[1]
    chunks = 4
    width = count // chunks
    begun = []

    def begin(a, b):
        copy = pltpu.make_async_copy(a, b, sems.at[len(begun)])
        copy.start()
        begun.append(copy)
        return copy

    parts = [begin(charges_in, charges)]
    for c in range(chunks):
        at = pl.ds(c * width, width)
        parts.append(begin(points_in.at[:, at], points.at[:, at]))
    order_copy = begin(order_in, order)
    near_lists = [begin(owner_in, owner), begin(slot_in, slot)]
    needed = [
        begin(leaf_skel_in, leaf_skel),
        begin(leaf_interp_in, leaf_interp),
        begin(inner_skel_in, inner_skel),
        begin(inner_interp_in, inner_interp),
    ]
    rest = []
    path = path_rows()
    on_path = []
    for k in range(interps_out.shape[0]):
        on_path.append(begin(top_interp.at[path[k]], interps.at[k]))
        on_path.append(begin(top_skel.at[pl.ds(path[k], 1)], skels.at[k]))

    parts[0].wait()
    for c in range(count // 128):
        at = slice(c * 128, (c + 1) * 128)
        if c * 128 % width == 0:
            parts[1 + c * 128 // width].wait()
        block = jnp.concatenate(
            [
                points[:, at].astype(f32),
                charges[:, at].astype(f32),
                jnp.zeros((48, 128), f32),
            ],
            axis=0,
        )
        unsorted[at, :] = jnp.transpose(block)

    leaves = src.shape[0]
    first_node = 2 * leaves
    lane = lax.broadcasted_iota(jnp.int32, (256, 128), 1)

    def finish(node, both):
        joined[node] = both
        cols[first_node + node] = source_matrix(both[:64], norm_row(both[:64]))
        loads[first_node + node] = both[64:]

    def copy_rows(pair, buffer):
        base = pl.multiple_of(pair * 512, 512)
        for u in range(512):
            buffer[u : u + 1, :] = unsorted[pl.ds(order[base + u], 1), :]

    def process(pair, buffer):
        even = buffer[:256]
        odd = buffer[256:]
        both = jnp.where(lane < 64, even, pltpu.roll(odd, 64, 1))
        tgt[pl.ds(pl.multiple_of(pair * 256, 256), 256), :] = (both * 0.25).astype(bf16)
        for k, mine in enumerate((even, odd)):
            i = 2 * pair + k
            both = jnp.transpose(mine)[:80].astype(bf16)
            src[i] = both
            coords, load = both[:64], both[64:]
            norm = norm_row(coords)
            norms[i] = norm
            rows[i] = target_matrix(coords, norm)
            matrix = source_matrix(coords, norm)
            for half in range(2):
                cols[2 * i + half] = matrix[:, half * 128 : half * 128 + 128]
                loads[2 * i + half] = load[:, half * 128 : half * 128 + 128]
            picked = dot(coords, onehot(leaf_skel[pl.ds(i, 1), :], 256)).astype(bf16)
            value = dot(load, leaf_interp[i]).astype(bf16)
            finish(i, jnp.concatenate([picked, value], axis=0))
        node = combine(
            joined[2 * pair],
            joined[2 * pair + 1],
            inner_skel[pl.ds(pair, 1), :],
            inner_interp[pair],
        )
        finish(leaves + pair, node)

    for copy in needed + [order_copy]:
        copy.wait()

    def two_pairs(i, carry):
        copy_rows(2 * i, buffer0)
        process(jnp.maximum(2 * i - 1, 0), buffer1)
        copy_rows(2 * i + 1, buffer1)
        process(2 * i, buffer0)
        return carry

    lax.fori_loop(0, leaves // 4, two_pairs, 0)
    process(leaves // 2 - 1, buffer1)
    for copy in near_lists + on_path:
        copy.wait()
    codes[...] = codes_of(owner[...], slot[...], 0, leaves)
    rest += [begin(interps, interps_out), begin(skels, skels_out), begin(codes, codes_out)]
    near = jnp.concatenate([owner[...].astype(f32), slot[...].astype(f32)], axis=0)
    blank = jnp.zeros((near.shape[0], 128 - near.shape[1]), f32)
    tgt[count // 2 :, :] = jnp.concatenate([near, blank], axis=1).astype(bf16)
    rest += [begin(src, src_out), begin(tgt, tgt_out), begin(src, mine_out.at[pl.ds(0, leaves)])]
    rest += [begin(rows, rows_out), begin(norms, norms_out)]
    tiles = pl.ds(0, 3 * leaves + leaves // 2)
    rest += [begin(cols.at[tiles], cols_out.at[tiles])]
    first, half = leaves, leaves // 4
    number, row = leaves + leaves // 2, leaves // 2
    while half > 0:
        for j in range(half):
            left = joined[first + 2 * j]
            right = joined[first + 2 * j + 1]
            finish(number, combine(left, right, inner_skel[row : row + 1, :], inner_interp[row]))
            number, row = number + 1, row + 1
        first = first + 2 * half
        half = half // 2
    node = joined[2 * leaves - 2]
    root[...] = jnp.concatenate([node, jnp.zeros_like(node)], axis=1)
    last = cols.shape[0] - 1
    cols[last] = jnp.zeros((128, 128), bf16)
    loads[last] = jnp.zeros((16, 128), bf16)
    inner_tiles = pl.ds(3 * leaves + leaves // 2, leaves // 2)
    rest += [begin(root, mine_out.at[leaves]), begin(loads, loads_out)]
    rest += [begin(cols.at[inner_tiles], cols_out.at[inner_tiles])]
    for copy in rest:
        copy.wait()


def path_rows():
    devices = lax.axis_size("leaf")
    device = lax.axis_index("leaf")
    bits = devices.bit_length() - 1

    def row_at(height, node):
        return devices - (devices >> (height - 1)) + node

    path = [row_at(1, device >> 1), row_at(2, device >> 2)]
    for height in range(2, bits - 1, 2):
        up = device >> (height + 1)
        path += [row_at(height + 1, up), row_at(height + 1, up ^ 1)]
        path.append(row_at(min(height + 2, bits - 1), up >> 1))
    return path


def first_part(points, charges, order, owner, slot, *tables):
    count = points.shape[1]
    leaves = count // 256
    tiles = 4 * leaves
    steps = len(path_rows())
    leaf_interp, leaf_skel, inner_interp, inner_skel = tables[:4]
    src = (leaves, 80, 256)
    tgt = (count // 2 + 2 * owner.shape[0], 128)
    cols = (tiles, 128, 128)
    loads = (tiles, 16, 128)
    rows = (leaves, 256, 128)
    norms = (leaves, 1, 256)
    shapes = [
        (src, bf16),
        (tgt, bf16),
        (cols, bf16),
        (loads, bf16),
        (rows, bf16),
        (norms, f32),
        ((leaves + 1, 80, 256), bf16),
        ((steps, 256, 128), bf16),
        ((steps, 1, 128), jnp.int32),
        (owner.shape, jnp.int32),
    ]
    held = [
        (points.shape, bf16),
        (charges.shape, bf16),
        (owner.shape, jnp.int32),
        (slot.shape, jnp.int32),
        ((count, 128), f32),
        ((512, 128), f32),
        ((512, 128), f32),
    ]
    held += shapes[:6]
    held += [((2 * leaves - 1, 80, 128), bf16), ((80, 256), bf16)]
    held += shapes[7:]
    n_before = len(held)
    held += [(table.shape, table.dtype) for table in tables[:4]]
    return pl.pallas_call(
        first_kernel,
        out_shape=tuple(jax.ShapeDtypeStruct(*shape) for shape in shapes),
        in_specs=[ANY] * 11,
        out_specs=(ANY,) * 10,
        scratch_shapes=[pltpu.VMEM(*shape) for shape in held[:n_before]]
        + [pltpu.SMEM(order.shape, jnp.int32)]
        + [pltpu.VMEM(*shape) for shape in held[n_before:]]
        + [pltpu.SemaphoreType.DMA((24 + 2 * steps,))],
        compiler_params=params(FIRST_LIMIT),
        cost_estimate=cost(),
        name="order_and_subtree",
    )(order, points, charges, owner, slot, *tables)


def far_kernel(*refs, first_leaf, n_leaves, n_ids):
    codes = refs[:n_ids]
    far_list, far_count, cols_in, loads_in, rows_in, acc = refs[n_ids : 6 + n_ids]
    lists = refs[6 + n_ids : -5]
    cols, loads, rows, tiles, sems = refs[-5:]
    leaves = rows.shape[0]
    width = far_list.shape[1]
    first_node = 2 * leaves
    empty = cols.shape[0] - 1
    mine = pl.ds(first_leaf, n_leaves)
    my_tiles = pl.ds(2 * first_leaf, 2 * n_leaves)
    nodes = pl.ds(first_node, cols.shape[0] - first_node)
    copies = [
        pltpu.make_async_copy(rows_in.at[mine], rows.at[mine], sems.at[0]),
        pltpu.make_async_copy(cols_in.at[my_tiles], cols.at[my_tiles], sems.at[1]),
        pltpu.make_async_copy(loads_in, loads, sems.at[2]),
        pltpu.make_async_copy(cols_in.at[nodes], cols.at[nodes], sems.at[3]),
    ]
    for copy in copies:
        copy.start()

    def list_leaf(k, count):
        i = first_leaf + k
        tiles[count] = (i << 16) | ((2 * i) << 8) | (2 * i + 1)
        count = count + 1
        used = far_count[i]
        for k in range(0, width, 2):
            first = far_list[i, k] + first_node
            second = jnp.where(k + 1 < used, far_list[i, k + 1] + first_node, empty)
            tiles[count] = (i << 16) | (first << 8) | second
            count = count + (k < used).astype(jnp.int32)
        return count

    count = lax.fori_loop(0, n_leaves, list_leaf, 0)
    tiles[count] = (empty << 8) | empty
    count = (count + 1) & ~1

    def step(start, size):
        values, weights = [], []
        for u in range(size):
            packed = tiles[start + u]
            leaf = packed >> 16
            first = (packed >> 8) & 255
            second = packed & 255
            matrix = jnp.concatenate([cols[first], cols[second]], axis=1)
            load = jnp.concatenate([loads[first], loads[second]], axis=1)
            values.append(jnp.exp(dot(rows[leaf], matrix)).astype(bf16))
            weights.append(placed(load, leaf & 7))
        acc[...] += dot_nt(jnp.concatenate(values, axis=1), jnp.concatenate(weights, axis=1))

    acc[...] = jnp.zeros_like(acc)
    for k in range(n_ids):
        list_pairs(codes[k], lists[PHASES * k : PHASES * k + PHASES])
    for copy in copies:
        copy.wait()
    largest = STEPS[0]
    whole = lax.div(count, largest)

    def full_step(i, carry):
        step(i * largest, largest)
        return carry

    lax.fori_loop(0, whole, full_step, 0)
    for size in STEPS[1:]:

        @pl.when((count & size) > 0)
        def _(size=size):
            step(count & ~(2 * size - 1), size)


def list_pairs(codes, tables):
    per_leaf, leaves = codes.shape
    for g in range(leaves // 8):
        counts = [jnp.int32(0)] * len(tables)
        for j in range(8):
            for u in range(per_leaf):
                value = codes[u, g * 8 + j]
                for p, table in enumerate(tables):
                    if table is None:
                        continue
                    table[g, 1 + counts[p]] = value & CODE
                    counts[p] = counts[p] + ((value >> (PHASE_BIT + p)) & 1)
        for p, table in enumerate(tables):
            if table is None:
                continue
            table[g, 1 + counts[p]] = DUMMY
            table[g, 0] = (counts[p] + 1) & ~1


def pair_table(leaves):
    return jax.ShapeDtypeStruct((leaves // 8, 128), jnp.int32)


def self_and_far(codes, far_list, far_count, cols, loads, rows, call, calls):
    leaves = rows.shape[0]
    width = far_list.shape[1]
    n_leaves = leaves // calls
    out = pl.pallas_call(
        functools.partial(
            far_kernel, first_leaf=call * n_leaves, n_leaves=n_leaves, n_ids=len(codes)
        ),
        out_shape=(jax.ShapeDtypeStruct((256, 128), f32),) + (pair_table(leaves),) * (PHASES * len(codes)),
        in_specs=[SMEM] * (2 + len(codes)) + [ANY] * 3,
        out_specs=(VMEM,) + (SMEM,) * (PHASES * len(codes)),
        scratch_shapes=[
            pltpu.VMEM(cols.shape, bf16),
            pltpu.VMEM(loads.shape, bf16),
            pltpu.VMEM(rows.shape, bf16),
            pltpu.SMEM((n_leaves * (1 + width // 2) + 2,), jnp.int32),
            pltpu.SemaphoreType.DMA((4,)),
        ],
        compiler_params=params(FIRST_LIMIT),
        cost_estimate=cost(),
        name=f"self_and_far{call}",
    )(*codes, far_list, far_count, cols, loads, rows)
    return out[0], [out[1 + PHASES * k : 1 + PHASES * k + PHASES] for k in range(len(codes))]


def near_kernel(*refs, n_sources, n_targets, n_lists, phase):
    refs = list(refs)

    def take(n):
        taken = refs[:n]
        del refs[:n]
        return taken

    makes = phase < PHASES - 1
    (codes,) = take(1) if makes else (None,)
    lists = take(n_lists)
    target_parts = take(n_targets if makes else 1)
    source_parts = take(n_sources)
    before = take(phase > 0)
    outs = take(n_targets) if not makes else []
    (acc,) = take(1) if makes else (None,)
    tables = take(PHASES - 1 - phase) if makes else []
    if phase == 1:
        (targets,) = take(1)
    elif phase == 2:
        (targets,) = target_parts
        target_parts = []
    sources, sems, pairs, steps = take(4)
    if phase == 0:
        (targets,) = take(1)
    if not makes:
        (acc,) = take(1)
    leaves = source_parts[0].shape[0]
    size = leaves * 128
    copies = []

    def begin(part, place):
        copies.append(pltpu.make_async_copy(part, place, sems.at[len(copies)]))
        copies[-1].start()

    own_rows = acc.shape[0] // n_targets
    for k, part in enumerate(lists):
        begin(part, pairs.at[pl.ds(k * own_rows, own_rows)])
    for k, part in enumerate(target_parts):
        begin(part.at[pl.ds(0, size)], targets.at[pl.ds(k * size, size)])
    for k, part in enumerate(source_parts):
        begin(part.at[pl.ds(0, leaves)], sources.at[pl.ds(k * leaves, leaves)])
    acc[...] = jnp.zeros_like(acc)
    if makes:
        table = pairs.at[pl.ds(n_lists * own_rows, own_rows)]
        list_pairs(codes, [None] * phase + [table] + tables)
    for copy in copies:
        copy.wait()

    counts = [jnp.int32(0)] * len(STEPS)
    for row in range(pairs.shape[0]):
        used = pairs[row, 0]
        whole = lax.div(used, STEPS[0])

        def note(i, count, row=row):
            steps[0, count + i] = row * 128 + 1 + i * STEPS[0]
            return count

        lax.fori_loop(0, whole, note, counts[0])
        counts[0] = counts[0] + whole
        for k, size in enumerate(STEPS[1:], 1):
            steps[k, counts[k]] = row * 128 + 1 + (used & ~(2 * size - 1))
            counts[k] = counts[k] + jnp.where((used & size) > 0, 1, 0)

    for k, size in enumerate(STEPS):

        def step(i, carry, k=k, size=size):
            group = steps[k, i] >> 7
            start = steps[k, i] & 127

            def exponent(u):
                packed = pairs[group, start + u]
                target = (packed >> 16) & 7
                coords = sources[packed & 65535, :64, :]
                odd = target & 1
                zero = jnp.zeros_like(coords)
                matrix = jnp.concatenate(
                    [jnp.where(odd == 0, coords, zero), jnp.where(odd == 1, coords, zero)],
                    axis=0,
                )
                at = pl.multiple_of(group * 1024 + (target >> 1) * 256, 256)
                return dot(targets[pl.ds(at, 256), :], matrix) - norm_row(coords)

            def weight(u):
                packed = pairs[group, start + u]
                place = jnp.where(packed < DUMMY, (packed >> 16) & 7, 8)
                return placed(sources[packed & 65535, 64:, :], place)

            acc[group] += tiles_sum(size, exponent, weight)
            return carry

        lax.fori_loop(0, counts[k], step, 0)

    if makes:
        for part in before:
            acc[: part.shape[0]] += part[...]
    for k, out in enumerate(outs):
        mine = slice(k * own_rows, (k + 1) * own_rows)
        out[...] = (acc[mine] + before[0][mine]).astype(bf16)


def near(phase, lists, targets, sources, codes=None, before=None):
    n_sources = len(sources)
    makes = phase < PHASES - 1
    n_targets = len(targets) if makes else len(lists)
    leaves = min(source.shape[0] for source in sources)
    sums = jax.ShapeDtypeStruct((n_targets * leaves // 8, 256, 128), f32)
    part = jax.ShapeDtypeStruct((leaves // 8, 256, 128), bf16)
    held_targets = jax.ShapeDtypeStruct((n_targets * leaves * 128, 128), bf16)
    args = ([codes] if makes else []) + list(lists) + list(targets) + list(sources)
    in_specs = [SMEM] * int(makes) + [ANY] * (len(args) - int(makes))
    if not makes:
        in_specs[len(lists)] = VMEM
    if before is not None:
        args.append(before)
        in_specs.append(VMEM)
    if makes:
        n_tables = PHASES - 1 - phase
        out_shape = (sums,) + (pair_table(leaves),) * n_tables
        out_specs = (VMEM,) + (SMEM,) * n_tables
        if phase == 1:
            out_shape, out_specs = out_shape + (held_targets,), out_specs + (VMEM,)
    else:
        out_shape, out_specs = (part,) * n_targets, (VMEM,) * n_targets
    scratch = [
        pltpu.VMEM((n_sources * leaves, 80, 256), bf16),
        pltpu.SemaphoreType.DMA((n_sources + n_targets + len(lists),)),
        pltpu.SMEM((n_targets * leaves // 8, 128), jnp.int32),
        pltpu.SMEM((len(STEPS), n_targets * leaves), jnp.int32),
    ]
    if phase == 0:
        scratch.append(pltpu.VMEM(held_targets.shape, bf16))
    if not makes:
        scratch.append(pltpu.VMEM(sums.shape, f32))
    return pl.pallas_call(
        functools.partial(
            near_kernel, n_sources=n_sources, n_targets=n_targets, n_lists=len(lists), phase=phase
        ),
        out_shape=out_shape,
        in_specs=in_specs,
        out_specs=out_specs,
        scratch_shapes=scratch,
        compiler_params=params(),
        cost_estimate=cost(),
        name=f"near{phase}",
    )(*args)


def ordered(first, second, test):
    return jnp.where(test, first, second), jnp.where(test, second, first)


def climb_kernel(me, own, other, skels, interps, parent, *, height, row):
    sibling = other[0, :, :128] if len(other.shape) == 3 else other[...]
    left, right = ordered(own[0, :, :128] if len(own.shape) == 3 else own[...], sibling, ((me[0] >> height) & 1) == 0)
    parent[...] = combine(left, right, skels[row], interps[row])


def last_block(value):
    if value.ndim == 2:
        return VMEM
    blocks = value.shape[0]
    return pl.BlockSpec((1,) + value.shape[1:], lambda i: (blocks - 1, 0, 0))


def climb(me, own, other, skels, interps, height, row):
    return pl.pallas_call(
        functools.partial(climb_kernel, height=height, row=row),
        grid=(1,),
        out_shape=jax.ShapeDtypeStruct((80, 128), bf16),
        in_specs=[SMEM, last_block(own), last_block(other), VMEM, VMEM],
        out_specs=VMEM,
        compiler_params=params(),
        cost_estimate=cost(),
        name=f"climb{height}",
    )(me, own, other, skels, interps)


def climb_two_kernel(me, own, one, two, three, skels, interps, sibling, parent, *, height, row):
    node = me[0] >> height
    is_left = (node & 1) == 0
    left, right = ordered(own[...], one[...], is_left)
    mine = combine(left, right, skels[row], interps[row])
    left, right = ordered(two[...], three[...], is_left)
    other = combine(left, right, skels[row + 1], interps[row + 1])
    sibling[...] = other
    left, right = ordered(mine, other, (node & 2) == 0)
    parent[...] = combine(left, right, skels[row + 2], interps[row + 2])


def climb_two(me, own, others, skels, interps, height, row):
    node = jax.ShapeDtypeStruct((80, 128), bf16)
    return pl.pallas_call(
        functools.partial(climb_two_kernel, height=height, row=row),
        out_shape=(node, node),
        in_specs=[SMEM] + [VMEM] * 6,
        out_specs=(VMEM, VMEM),
        compiler_params=params(),
        cost_estimate=cost(),
        name=f"climb{height}",
    )(me, own, *others, skels, interps)


def top_kernel(*refs):
    parts, (rows, acc, cols, loads) = refs[:-4], refs[-4:]
    for t, part in enumerate(parts):
        node = part[0, :, :128] if len(part.shape) == 3 else part[...]
        cols[:, t * 128 : (t + 1) * 128] = source_matrix(node[:64], norm_row(node[:64]))
        loads[:, t * 128 : (t + 1) * 128] = jnp.concatenate([node[64:]] * 8, axis=0)
    lane = lax.broadcasted_iota(jnp.int32, (256, 128), 1) >> 4

    def two_leaves(i, carry):
        both = rows[pl.ds(2 * i, 2)].reshape(512, 128)
        value = jnp.exp(dot(both, cols[...])).astype(bf16)
        result = dot_nt(value, loads[...])
        group = lax.div(i, 4)
        place = (2 * i) & 7
        acc[group] += jnp.where(lane == place, result[:256], 0.0) + jnp.where(
            lane == place + 1, result[256:], 0.0
        )
        return carry

    acc[...] = jnp.zeros_like(acc)
    lax.fori_loop(0, rows.shape[0] // 2, two_leaves, 0, unroll=2)


def top(parts, rows):
    levels = len(parts)
    return pl.pallas_call(
        top_kernel,
        out_shape=jax.ShapeDtypeStruct((rows.shape[0] // 8, 256, 128), f32),
        grid=(1,),
        in_specs=[last_block(part) for part in parts] + [VMEM],
        out_specs=VMEM,
        scratch_shapes=[
            pltpu.VMEM((128, levels * 128), bf16),
            pltpu.VMEM((128, levels * 128), bf16),
        ],
        compiler_params=params(),
        cost_estimate=cost(),
        name="top",
    )(*parts, rows)


def last_kernel(*refs, n_far):
    fars = refs[:n_far]
    above, norms = refs[n_far : n_far + 2]
    received, out = refs[n_far + 2 : -1], refs[-1]
    groups = above.shape[0]
    for group in range(groups):
        local = above[group]
        for far in fars[group * n_far // groups : (group + 1) * n_far // groups]:
            local = local + far[...]
        local = jnp.transpose(local)
        total = received[0][group].astype(f32)
        for part in received[1:]:
            total = total + part[group].astype(f32)
        total = jnp.transpose(total)
        for j in range(8):
            leaf = group * 8 + j
            rows = slice(16 * j, 16 * j + 16)
            out[:, leaf * 256 : (leaf + 1) * 256] = local[rows] + total[rows] * jnp.exp(-norms[leaf])


def last(fars, above, norms, received):
    return pl.pallas_call(
        functools.partial(last_kernel, n_far=len(fars)),
        out_shape=jax.ShapeDtypeStruct((16, norms.shape[0] * 256), f32),
        in_specs=[VMEM] * (2 + len(fars) + len(received)),
        out_specs=VMEM,
        compiler_params=params(),
        cost_estimate=cost(),
        name="last_sum",
    )(*fars, above, norms, *received)


def swap(value, mask):
    pairs = [(d, d ^ mask) for d in range(lax.axis_size("leaf"))]
    return lax.ppermute(value, "leaf", pairs)


def after(value, *others):
    return lax.optimization_barrier((value,) + others)[0]


def shards(
    points,
    charges,
    leaf_order,
    near_owner,
    near_slot,
    far_list,
    far_count,
    leaf_interp,
    leaf_skel,
    inner_interp,
    inner_skel,
    top_interp,
    top_skel,
):
    device_count = lax.axis_size("leaf")
    bits = device_count.bit_length() - 1
    source_bits = tuple(b for b in range(bits) if b not in TARGET_BITS)
    outer_bits = source_bits[1:]
    device = lax.axis_index("leaf")
    leaves = near_owner.shape[0]
    me = device.reshape(1).astype(jnp.int32)
    mates = range(1, 2 ** len(TARGET_BITS))
    early_bits = outer_bits[:-1]
    late = 2 ** outer_bits[-1]

    def payload_codes(payload, first):
        near = payload[-2 * near_owner.shape[1] :, :leaves].astype(jnp.int32)
        return codes_of(near[: near_owner.shape[1]], near[near_owner.shape[1] :], first, leaves)

    owner, slot = near_owner.T, near_slot.T
    src, tgt, cols, loads, rows, norms, mine, interps, skels, codes = first_part(
        points, charges, leaf_order, owner, slot,
        leaf_interp, leaf_skel, inner_interp, inner_skel, top_interp, top_skel,
    )
    pieces = {0: src, late: swap(src, late)}
    for b in reversed(early_bits):
        pieces[2**b] = swap(src, 2**b)
    beside = swap(tgt, 2 ** TARGET_BITS[0])
    far_away = swap(tgt, 2 ** TARGET_BITS[1])
    pieces[1] = swap(mine, 1)

    def far(call, codes, token):
        return self_and_far(
            codes, after(far_list, token), far_count, cols, loads, rows, call, 2
        )

    far0, lists0 = far(0, [codes], norms)
    node = climb(me, after(mine, far0, beside), pieces[1], skels, interps, 0, 0)
    siblings = [pieces[1], swap(node, 2)]
    far1, lists1 = far(1, [payload_codes(after(beside, far0), 0)], node)
    last_targets = swap(after(far_away, far1), 2 ** TARGET_BITS[0])
    for n, b in enumerate(early_bits):
        for low in range(2**n):
            place = spread(low, early_bits[:n])
            if low:
                pieces[place | 2**b] = swap(pieces[place], 2**b)
    wanted = [spread(k, source_bits) for k in range(2 ** (len(source_bits) - 1))]
    targets = [tgt, beside, far_away, last_targets]
    lists = lists0 + lists1
    sums, far_tables1, far_tables2 = near(
        0,
        [tables[0] for tables in lists],
        targets[:3],
        [pieces[k] for k in wanted if k == 1 or not k & 1],
        codes=payload_codes(after(far_away, far1), 0),
    )
    node = climb(me, node, after(siblings[1], sums), skels, interps, 1, 1)
    for k in wanted[2::2]:
        pieces[k | 1] = swap(after(pieces[k], node), 1)
    pieces[late] = after(pieces[late], node)
    for n, b in enumerate(early_bits):
        for low in range(2**n):
            place = spread(low, early_bits[:n]) | late
            pieces[place | 2**b] = swap(pieces[place], 2**b)
    pieces[late | 1] = swap(pieces[late], 1)
    height, row = 2, 2
    others = [swap(node, k * 2**height) for k in (1, 2, 3)]
    sums, last_table, all_targets = near(
        1,
        [tables[1] for tables in lists] + [far_tables1],
        targets,
        [pieces[k] for k in wanted + [late, late | 1]],
        codes=payload_codes(after(last_targets, node), 1),
        before=sums,
    )
    others[0] = after(others[0], sums)
    while height + 1 < bits:
        if height > 2:
            others = [swap(node, k * 2**height) for k in (1, 2, 3)]
        sibling, node = climb_two(me, node, others, skels, interps, height, row)
        siblings += [others[0], sibling]
        height, row = height + 2, row + 3
    if height < bits:
        siblings.append(swap(node, 2**height))
    for k in wanted[2::2]:
        pieces[k | late | 1] = swap(after(pieces[k | late], node), 1)
    parts = near(
        2,
        [tables[2] for tables in lists] + [far_tables2, after(last_table, node)],
        [all_targets],
        [pieces[k | late] for k in wanted[2:]],
        before=sums,
    )
    siblings[-1] = after(siblings[-1], parts[0])
    received = [parts[0]] + [
        swap(after(parts[k], siblings[-1]), spread(k, TARGET_BITS)) for k in mates
    ]
    above = top(siblings, after(rows, parts[0]))
    return last((far0, far1), above, norms, received)


def solution(mesh):
    in_specs = (
        P(None, "leaf"),
        P(None, "leaf"),
        P("leaf"),
        P("leaf", None),
        P("leaf", None),
        P("leaf", None),
        P("leaf"),
        P("leaf", None, None),
        P("leaf", None),
        P("leaf", None, None),
        P("leaf", None),
        P(),
        P(),
    )
    out_specs = P(None, "leaf")
    return jax.shard_map(shards, mesh=mesh, in_specs=in_specs, out_specs=out_specs, check_vma=False)
```

```python
import functools

import jax
import jax.numpy as jnp
from jax import lax
from jax.experimental import pallas as pl
from jax.experimental.pallas import tpu as pltpu
from jax.sharding import PartitionSpec as P

TARGET_BITS = (1, 3)
STEPS = (8, 4, 2)
DUMMY = 1 << 30
PHASE_BIT = 24
CODE = (1 << PHASE_BIT) - 1
VMEM_LIMIT = 24 * 1024 * 1024
FIRST_LIMIT = 58 * 1024 * 1024
PHASES = 3
bf16 = jnp.bfloat16
f32 = jnp.float32

VMEM = pl.BlockSpec(memory_space=pltpu.VMEM)
SMEM = pl.BlockSpec(memory_space=pltpu.SMEM)
ANY = pl.BlockSpec(memory_space=pl.ANY)
HBM = pl.BlockSpec(memory_space=pltpu.HBM)


def params(limit=VMEM_LIMIT):
    return pltpu.CompilerParams(vmem_limit_bytes=limit)


def cost():
    return pl.CostEstimate(flops=1, bytes_accessed=1, transcendentals=0)


def dot(a, b):
    return lax.dot_general(a, b, (((1,), (0,)), ((), ())), preferred_element_type=f32)


def dot_nt(a, b):
    return lax.dot_general(a, b, (((1,), (1,)), ((), ())), preferred_element_type=f32)


def split3(value):
    hi = value.astype(bf16).astype(f32)
    rest = value - hi
    mid = rest.astype(bf16).astype(f32)
    return hi, mid, rest - mid


def norm_row(coords):
    wide = coords.astype(f32)
    return jnp.sum(wide * wide, axis=0, keepdims=True) * 0.125


def extra_rows(norms, first):
    hi, mid, lo = split3(-norms)
    row = lax.broadcasted_iota(jnp.int32, (16, norms.shape[1]), 0)
    one_at = 3 - first
    out = jnp.where((row >= one_at) & (row < one_at + 3), 1.0, 0.0)
    out = jnp.where(row == first, hi, out)
    out = jnp.where(row == first + 1, mid, out)
    return jnp.where(row == first + 2, lo, out)


def source_matrix(coords, norms):
    width = coords.shape[1]
    extra = extra_rows(norms, 0).astype(bf16)
    return jnp.concatenate([coords, extra, jnp.zeros((48, width), bf16)], axis=0)


def target_matrix(coords, norms):
    width = coords.shape[1]
    extra = extra_rows(norms, 3)
    wide = jnp.concatenate(
        [coords.astype(f32) * 0.25, extra, jnp.zeros((48, width), f32)], axis=0
    )
    return jnp.transpose(wide).astype(bf16)


def tiles_sum(count, exponent, weight):
    total = None
    value = None
    ahead = exponent(0)
    for u in range(count):
        now = ahead
        if u + 1 < count:
            ahead = exponent(u + 1)
        if value is not None:
            part = dot_nt(value, weight(u - 1))
            total = part if total is None else total + part
        value = jnp.exp(now).astype(bf16)
    part = dot_nt(value, weight(count - 1))
    return part if total is None else total + part


def placed(loads, place):
    zero = jnp.zeros_like(loads)
    return jnp.concatenate(
        [jnp.where(place == k, loads, zero) for k in range(8)], axis=0
    )


def onehot(picks, size):
    row = lax.broadcasted_iota(jnp.int32, (size, picks.shape[1]), 0)
    return jnp.where(row == picks, 1.0, 0.0).astype(bf16)


def combine(left, right, picks, interp):
    both = jnp.concatenate([left, right], axis=1)
    coords = dot(both[:64], onehot(picks, 256)).astype(bf16)
    load = dot(both[64:], interp).astype(bf16)
    return jnp.concatenate([coords, load], axis=0)


def spread(number, bits):
    return sum(((number >> k) & 1) << b for k, b in enumerate(bits))


def compress(number, bits):
    return sum(((number >> b) & 1) << k for k, b in enumerate(bits))


def codes_of(owner, slot, first, leaves):
    bits = lax.axis_size("leaf").bit_length() - 1
    source_bits = [b for b in range(bits) if b not in TARGET_BITS]
    other = owner ^ lax.axis_index("leaf")
    place = compress(other, source_bits) * leaves + slot
    here = jnp.where((other & sum(2**b for b in TARGET_BITS)) == 0, 1, 0)
    half = 2 ** (len(source_bits) - 1)
    is_late = place >= half * leaves
    place = place & (half * leaves - 1)
    is_last = is_late & (place >= 2 * leaves)
    piece = place >> (leaves.bit_length() - 1)
    is_first = jnp.logical_not(is_late) & ((piece < 2) | ((piece & 1) == 0))
    if first != 0:
        is_first = is_first & (piece < 0)
    phase = jnp.where(is_last, 2, jnp.where(is_first, 0, 1))
    first_place = place - (piece - jnp.where(piece < 2, piece, (piece >> 1) + 1)) * leaves
    place = jnp.where(
        is_last,
        place - 2 * leaves,
        jnp.where(is_late, half * leaves + place, jnp.where(is_first, first_place, place)),
    )
    target = lax.broadcasted_iota(jnp.int32, owner.shape, 1) & 7
    return (here << (phase + PHASE_BIT)) | (target << 16) | place


def first_kernel(
    order_in, points_in, charges_in, owner_in, slot_in,
    leaf_interp_in, leaf_skel_in, inner_interp_in, inner_skel_in, top_interp, top_skel,
    src_out, tgt_out, cols_out, loads_out, rows_out, norms_out, mine_out, interps_out, skels_out, codes_out,
    points, charges, owner, slot, unsorted, buffer0, buffer1, src, tgt, cols, loads, rows, norms,
    joined, root, interps, skels, codes, order, leaf_interp, leaf_skel, inner_interp, inner_skel, sems,
):
    count = points.shape[1]
    chunks = 4
    width = count // chunks
    begun = []

    def begin(a, b):
        copy = pltpu.make_async_copy(a, b, sems.at[len(begun)])
        copy.start()
        begun.append(copy)
        return copy

    parts = [begin(charges_in, charges)]
    for c in range(chunks):
        at = pl.ds(c * width, width)
        parts.append(begin(points_in.at[:, at], points.at[:, at]))
    order_copy = begin(order_in, order)
    near_lists = [begin(owner_in, owner), begin(slot_in, slot)]
    needed = [
        begin(leaf_skel_in, leaf_skel),
        begin(leaf_interp_in, leaf_interp),
        begin(inner_skel_in, inner_skel),
        begin(inner_interp_in, inner_interp),
    ]
    rest = []
    path = path_rows()
    on_path = []
    for k in range(interps_out.shape[0]):
        on_path.append(begin(top_interp.at[path[k]], interps.at[k]))
        on_path.append(begin(top_skel.at[pl.ds(path[k], 1)], skels.at[k]))

    parts[0].wait()
    for c in range(count // 128):
        at = slice(c * 128, (c + 1) * 128)
        if c * 128 % width == 0:
            parts[1 + c * 128 // width].wait()
        block = jnp.concatenate(
            [
                points[:, at].astype(f32),
                charges[:, at].astype(f32),
                jnp.zeros((48, 128), f32),
            ],
            axis=0,
        )
        unsorted[at, :] = jnp.transpose(block)

    leaves = src.shape[0]
    first_node = 2 * leaves
    lane = lax.broadcasted_iota(jnp.int32, (256, 128), 1)

    def finish(node, both):
        joined[node] = both
        cols[first_node + node] = source_matrix(both[:64], norm_row(both[:64]))
        loads[first_node + node] = both[64:]

    def copy_rows(pair, buffer):
        base = pl.multiple_of(pair * 512, 512)
        for u in range(512):
            buffer[u : u + 1, :] = unsorted[pl.ds(order[base + u], 1), :]

    def process(pair, buffer):
        even = buffer[:256]
        odd = buffer[256:]
        both = jnp.where(lane < 64, even, pltpu.roll(odd, 64, 1))
        tgt[pl.ds(pl.multiple_of(pair * 256, 256), 256), :] = (both * 0.25).astype(bf16)
        for k, mine in enumerate((even, odd)):
            i = 2 * pair + k
            both = jnp.transpose(mine)[:80].astype(bf16)
            src[i] = both
            coords, load = both[:64], both[64:]
            norm = norm_row(coords)
            norms[i] = norm
            rows[i] = target_matrix(coords, norm)
            matrix = source_matrix(coords, norm)
            for half in range(2):
                cols[2 * i + half] = matrix[:, half * 128 : half * 128 + 128]
                loads[2 * i + half] = load[:, half * 128 : half * 128 + 128]
            picked = dot(coords, onehot(leaf_skel[pl.ds(i, 1), :], 256)).astype(bf16)
            value = dot(load, leaf_interp[i]).astype(bf16)
            finish(i, jnp.concatenate([picked, value], axis=0))
        node = combine(
            joined[2 * pair],
            joined[2 * pair + 1],
            inner_skel[pl.ds(pair, 1), :],
            inner_interp[pair],
        )
        finish(leaves + pair, node)

    for copy in needed + [order_copy]:
        copy.wait()

    def two_pairs(i, carry):
        copy_rows(2 * i, buffer0)
        process(jnp.maximum(2 * i - 1, 0), buffer1)
        copy_rows(2 * i + 1, buffer1)
        process(2 * i, buffer0)
        return carry

    lax.fori_loop(0, leaves // 4, two_pairs, 0)
    process(leaves // 2 - 1, buffer1)
    for copy in near_lists + on_path:
        copy.wait()
    codes[...] = codes_of(owner[...], slot[...], 0, leaves)
    rest += [begin(interps, interps_out), begin(skels, skels_out), begin(codes, codes_out)]
    near = jnp.concatenate([owner[...].astype(f32), slot[...].astype(f32)], axis=0)
    blank = jnp.zeros((near.shape[0], 128 - near.shape[1]), f32)
    tgt[count // 2 :, :] = jnp.concatenate([near, blank], axis=1).astype(bf16)
    rest += [begin(src, src_out), begin(tgt, tgt_out), begin(src, mine_out.at[pl.ds(0, leaves)])]
    rest += [begin(rows, rows_out), begin(norms, norms_out)]
    tiles = pl.ds(0, 3 * leaves + leaves // 2)
    rest += [begin(cols.at[tiles], cols_out.at[tiles])]
    first, half = leaves, leaves // 4
    number, row = leaves + leaves // 2, leaves // 2
    while half > 0:
        for j in range(half):
            left = joined[first + 2 * j]
            right = joined[first + 2 * j + 1]
            finish(number, combine(left, right, inner_skel[row : row + 1, :], inner_interp[row]))
            number, row = number + 1, row + 1
        first = first + 2 * half
        half = half // 2
    node = joined[2 * leaves - 2]
    root[...] = jnp.concatenate([node, jnp.zeros_like(node)], axis=1)
    last = cols.shape[0] - 1
    cols[last] = jnp.zeros((128, 128), bf16)
    loads[last] = jnp.zeros((16, 128), bf16)
    inner_tiles = pl.ds(3 * leaves + leaves // 2, leaves // 2)
    rest += [begin(root, mine_out.at[leaves]), begin(loads, loads_out)]
    rest += [begin(cols.at[inner_tiles], cols_out.at[inner_tiles])]
    for copy in rest:
        copy.wait()


def path_rows():
    devices = lax.axis_size("leaf")
    device = lax.axis_index("leaf")
    bits = devices.bit_length() - 1

    def row_at(height, node):
        return devices - (devices >> (height - 1)) + node

    path = [row_at(1, device >> 1), row_at(2, device >> 2)]
    for height in range(2, bits - 1, 2):
        up = device >> (height + 1)
        path += [row_at(height + 1, up), row_at(height + 1, up ^ 1)]
        path.append(row_at(min(height + 2, bits - 1), up >> 1))
    return path


def first_part(points, charges, order, owner, slot, *tables):
    count = points.shape[1]
    leaves = count // 256
    tiles = 4 * leaves
    steps = len(path_rows())
    leaf_interp, leaf_skel, inner_interp, inner_skel = tables[:4]
    src = (leaves, 80, 256)
    tgt = (count // 2 + 2 * owner.shape[0], 128)
    cols = (tiles, 128, 128)
    loads = (tiles, 16, 128)
    rows = (leaves, 256, 128)
    norms = (leaves, 1, 256)
    shapes = [
        (src, bf16),
        (tgt, bf16),
        (cols, bf16),
        (loads, bf16),
        (rows, bf16),
        (norms, f32),
        ((leaves + 1, 80, 256), bf16),
        ((steps, 256, 128), bf16),
        ((steps, 1, 128), jnp.int32),
        (owner.shape, jnp.int32),
    ]
    held = [
        (points.shape, bf16),
        (charges.shape, bf16),
        (owner.shape, jnp.int32),
        (slot.shape, jnp.int32),
        ((count, 128), f32),
        ((512, 128), f32),
        ((512, 128), f32),
    ]
    held += shapes[:6]
    held += [((2 * leaves - 1, 80, 128), bf16), ((80, 256), bf16)]
    held += shapes[7:]
    n_before = len(held)
    held += [(table.shape, table.dtype) for table in tables[:4]]
    return pl.pallas_call(
        first_kernel,
        out_shape=tuple(jax.ShapeDtypeStruct(*shape) for shape in shapes),
        in_specs=[ANY] * 11,
        out_specs=(ANY,) * 10,
        scratch_shapes=[pltpu.VMEM(*shape) for shape in held[:n_before]]
        + [pltpu.SMEM(order.shape, jnp.int32)]
        + [pltpu.VMEM(*shape) for shape in held[n_before:]]
        + [pltpu.SemaphoreType.DMA((24 + 2 * steps,))],
        compiler_params=params(FIRST_LIMIT),
        cost_estimate=cost(),
        name="order_and_subtree",
    )(order, points, charges, owner, slot, *tables)


def far_kernel(*refs, first_leaf, n_leaves, n_ids):
    codes = refs[:n_ids]
    far_list, far_count, cols_in, loads_in, rows_in, acc = refs[n_ids : 6 + n_ids]
    lists = refs[6 + n_ids : -5]
    cols, loads, rows, tiles, sems = refs[-5:]
    leaves = rows.shape[0]
    width = far_list.shape[1]
    first_node = 2 * leaves
    empty = cols.shape[0] - 1
    mine = pl.ds(first_leaf, n_leaves)
    my_tiles = pl.ds(2 * first_leaf, 2 * n_leaves)
    nodes = pl.ds(first_node, cols.shape[0] - first_node)
    copies = [
        pltpu.make_async_copy(rows_in.at[mine], rows.at[mine], sems.at[0]),
        pltpu.make_async_copy(cols_in.at[my_tiles], cols.at[my_tiles], sems.at[1]),
        pltpu.make_async_copy(loads_in, loads, sems.at[2]),
        pltpu.make_async_copy(cols_in.at[nodes], cols.at[nodes], sems.at[3]),
    ]
    for copy in copies:
        copy.start()

    def list_leaf(k, count):
        i = first_leaf + k
        tiles[count] = (i << 16) | ((2 * i) << 8) | (2 * i + 1)
        count = count + 1
        used = far_count[i]
        for k in range(0, width, 2):
            first = far_list[i, k] + first_node
            second = jnp.where(k + 1 < used, far_list[i, k + 1] + first_node, empty)
            tiles[count] = (i << 16) | (first << 8) | second
            count = count + (k < used).astype(jnp.int32)
        return count

    count = lax.fori_loop(0, n_leaves, list_leaf, 0)
    tiles[count] = (empty << 8) | empty
    count = (count + 1) & ~1

    def step(start, size):
        values, weights = [], []
        for u in range(size):
            packed = tiles[start + u]
            leaf = packed >> 16
            first = (packed >> 8) & 255
            second = packed & 255
            matrix = jnp.concatenate([cols[first], cols[second]], axis=1)
            load = jnp.concatenate([loads[first], loads[second]], axis=1)
            values.append(jnp.exp(dot(rows[leaf], matrix)).astype(bf16))
            weights.append(placed(load, leaf & 7))
        acc[...] += dot_nt(jnp.concatenate(values, axis=1), jnp.concatenate(weights, axis=1))

    acc[...] = jnp.zeros_like(acc)
    for k in range(n_ids):
        list_pairs(codes[k], lists[PHASES * k : PHASES * k + PHASES])
    for copy in copies:
        copy.wait()
    largest = STEPS[0]
    whole = lax.div(count, largest)

    def full_step(i, carry):
        step(i * largest, largest)
        return carry

    lax.fori_loop(0, whole, full_step, 0)
    for size in STEPS[1:]:

        @pl.when((count & size) > 0)
        def _(size=size):
            step(count & ~(2 * size - 1), size)


def list_pairs(codes, tables):
    per_leaf, leaves = codes.shape
    for g in range(leaves // 8):
        counts = [jnp.int32(0)] * len(tables)
        for j in range(8):
            for u in range(per_leaf):
                value = codes[u, g * 8 + j]
                for p, table in enumerate(tables):
                    if table is None:
                        continue
                    table[g, 1 + counts[p]] = value & CODE
                    counts[p] = counts[p] + ((value >> (PHASE_BIT + p)) & 1)
        for p, table in enumerate(tables):
            if table is None:
                continue
            table[g, 1 + counts[p]] = DUMMY
            table[g, 0] = (counts[p] + 1) & ~1


def pair_table(leaves):
    return jax.ShapeDtypeStruct((leaves // 8, 128), jnp.int32)


def self_and_far(codes, far_list, far_count, cols, loads, rows, call, calls):
    leaves = rows.shape[0]
    width = far_list.shape[1]
    n_leaves = leaves // calls
    out = pl.pallas_call(
        functools.partial(
            far_kernel, first_leaf=call * n_leaves, n_leaves=n_leaves, n_ids=len(codes)
        ),
        out_shape=(jax.ShapeDtypeStruct((256, 128), f32),) + (pair_table(leaves),) * (PHASES * len(codes)),
        in_specs=[SMEM] * (2 + len(codes)) + [ANY] * 3,
        out_specs=(VMEM,) + (SMEM,) * (PHASES * len(codes)),
        scratch_shapes=[
            pltpu.VMEM(cols.shape, bf16),
            pltpu.VMEM(loads.shape, bf16),
            pltpu.VMEM(rows.shape, bf16),
            pltpu.SMEM((n_leaves * (1 + width // 2) + 2,), jnp.int32),
            pltpu.SemaphoreType.DMA((4,)),
        ],
        compiler_params=params(FIRST_LIMIT),
        cost_estimate=cost(),
        name=f"self_and_far{call}",
    )(*codes, far_list, far_count, cols, loads, rows)
    return out[0], [out[1 + PHASES * k : 1 + PHASES * k + PHASES] for k in range(len(codes))]


def near_kernel(*refs, n_sources, n_targets, n_lists, n_codes, phase):
    refs = list(refs)

    def take(n):
        taken = refs[:n]
        del refs[:n]
        return taken

    makes = phase < PHASES - 1
    codes = take(n_codes)
    lists = take(n_lists)
    target_parts = take(n_targets if makes else 1)
    source_parts = take(n_sources)
    before = take(phase > 0)
    outs = take(n_targets) if not makes else []
    (acc,) = take(1) if makes else (None,)
    tables = [take(PHASES - 1 - phase) for _ in range(n_codes)]
    if phase == 1:
        (targets,) = take(1)
    elif phase == 2:
        (targets,) = target_parts
        target_parts = []
    sources, sems, pairs, steps = take(4)
    if phase == 0:
        (targets,) = take(1)
    if not makes:
        (acc,) = take(1)
    leaves = source_parts[0].shape[0]
    size = leaves * 128
    copies = []

    def begin(part, place):
        copies.append(pltpu.make_async_copy(part, place, sems.at[len(copies)]))
        copies[-1].start()

    own_rows = acc.shape[0] // n_targets
    for k, part in enumerate(lists):
        begin(part, pairs.at[pl.ds(k * own_rows, own_rows)])
    for k, part in enumerate(target_parts):
        begin(part.at[pl.ds(0, size)], targets.at[pl.ds(k * size, size)])
    for k, part in enumerate(source_parts):
        begin(part.at[pl.ds(0, leaves)], sources.at[pl.ds(k * leaves, leaves)])
    acc[...] = jnp.zeros_like(acc)
    for k in range(n_codes):
        table = pairs.at[pl.ds((n_lists + k) * own_rows, own_rows)]
        list_pairs(codes[k], [None] * phase + [table] + tables[k])
    for copy in copies:
        copy.wait()

    counts = [jnp.int32(0)] * len(STEPS)
    for row in range(pairs.shape[0]):
        used = pairs[row, 0]
        whole = lax.div(used, STEPS[0])

        def note(i, count, row=row):
            steps[0, count + i] = row * 128 + 1 + i * STEPS[0]
            return count

        lax.fori_loop(0, whole, note, counts[0])
        counts[0] = counts[0] + whole
        for k, size in enumerate(STEPS[1:], 1):
            steps[k, counts[k]] = row * 128 + 1 + (used & ~(2 * size - 1))
            counts[k] = counts[k] + jnp.where((used & size) > 0, 1, 0)

    for k, size in enumerate(STEPS):

        def step(i, carry, k=k, size=size):
            group = steps[k, i] >> 7
            start = steps[k, i] & 127

            def exponent(u):
                packed = pairs[group, start + u]
                target = (packed >> 16) & 7
                coords = sources[packed & 65535, :64, :]
                odd = target & 1
                zero = jnp.zeros_like(coords)
                matrix = jnp.concatenate(
                    [jnp.where(odd == 0, coords, zero), jnp.where(odd == 1, coords, zero)],
                    axis=0,
                )
                at = pl.multiple_of(group * 1024 + (target >> 1) * 256, 256)
                return dot(targets[pl.ds(at, 256), :], matrix) - norm_row(coords)

            def weight(u):
                packed = pairs[group, start + u]
                place = jnp.where(packed < DUMMY, (packed >> 16) & 7, 8)
                return placed(sources[packed & 65535, 64:, :], place)

            acc[group] += tiles_sum(size, exponent, weight)
            return carry

        lax.fori_loop(0, counts[k], step, 0)

    if makes:
        for part in before:
            acc[: part.shape[0]] += part[...]
    for k, out in enumerate(outs):
        mine = slice(k * own_rows, (k + 1) * own_rows)
        out[...] = (acc[mine] + before[0][mine]).astype(bf16)


def near(phase, lists, targets, sources, codes=(), before=None):
    n_sources, n_codes = len(sources), len(codes)
    makes = phase < PHASES - 1
    n_targets = len(targets) if makes else len(lists)
    leaves = min(source.shape[0] for source in sources)
    sums = jax.ShapeDtypeStruct((n_targets * leaves // 8, 256, 128), f32)
    part = jax.ShapeDtypeStruct((leaves // 8, 256, 128), bf16)
    held_targets = jax.ShapeDtypeStruct((n_targets * leaves * 128, 128), bf16)
    args = list(codes) + list(lists) + list(targets) + list(sources)
    in_specs = [SMEM] * n_codes + [ANY] * (len(args) - n_codes)
    if not makes:
        in_specs[len(lists)] = VMEM
    if before is not None:
        args.append(before)
        in_specs.append(VMEM)
    if makes:
        n_tables = n_codes * (PHASES - 1 - phase)
        out_shape = (sums,) + (pair_table(leaves),) * n_tables
        out_specs = (VMEM,) + (SMEM,) * n_tables
        if phase == 1:
            out_shape, out_specs = out_shape + (held_targets,), out_specs + (VMEM,)
    else:
        out_shape, out_specs = (part,) * n_targets, (VMEM,) * n_targets
    scratch = [
        pltpu.VMEM((n_sources * leaves, 80, 256), bf16),
        pltpu.SemaphoreType.DMA((n_sources + n_targets + len(lists),)),
        pltpu.SMEM((n_targets * leaves // 8, 128), jnp.int32),
        pltpu.SMEM((len(STEPS), n_targets * leaves), jnp.int32),
    ]
    if phase == 0:
        scratch.append(pltpu.VMEM(held_targets.shape, bf16))
    if not makes:
        scratch.append(pltpu.VMEM(sums.shape, f32))
    return pl.pallas_call(
        functools.partial(
            near_kernel,
            n_sources=n_sources,
            n_targets=n_targets,
            n_lists=len(lists),
            n_codes=n_codes,
            phase=phase,
        ),
        out_shape=out_shape,
        in_specs=in_specs,
        out_specs=out_specs,
        scratch_shapes=scratch,
        compiler_params=params(),
        cost_estimate=cost(),
        name=f"near{phase}",
    )(*args)


def ordered(first, second, test):
    return jnp.where(test, first, second), jnp.where(test, second, first)


def climb_kernel(me, own, other, skels, interps, parent, *, height, row):
    sibling = other[0, :, :128] if len(other.shape) == 3 else other[...]
    left, right = ordered(own[0, :, :128] if len(own.shape) == 3 else own[...], sibling, ((me[0] >> height) & 1) == 0)
    parent[...] = combine(left, right, skels[row], interps[row])


def last_block(value):
    if value.ndim == 2:
        return VMEM
    blocks = value.shape[0]
    return pl.BlockSpec((1,) + value.shape[1:], lambda i: (blocks - 1, 0, 0))


def climb(me, own, other, skels, interps, height, row):
    return pl.pallas_call(
        functools.partial(climb_kernel, height=height, row=row),
        grid=(1,),
        out_shape=jax.ShapeDtypeStruct((80, 128), bf16),
        in_specs=[SMEM, last_block(own), last_block(other), VMEM, VMEM],
        out_specs=VMEM,
        compiler_params=params(),
        cost_estimate=cost(),
        name=f"climb{height}",
    )(me, own, other, skels, interps)


def climb_two_kernel(me, own, one, two, three, skels, interps, sibling, parent, *, height, row):
    node = me[0] >> height
    is_left = (node & 1) == 0
    left, right = ordered(own[...], one[...], is_left)
    mine = combine(left, right, skels[row], interps[row])
    left, right = ordered(two[...], three[...], is_left)
    other = combine(left, right, skels[row + 1], interps[row + 1])
    sibling[...] = other
    left, right = ordered(mine, other, (node & 2) == 0)
    parent[...] = combine(left, right, skels[row + 2], interps[row + 2])


def climb_two(me, own, others, skels, interps, height, row):
    node = jax.ShapeDtypeStruct((80, 128), bf16)
    return pl.pallas_call(
        functools.partial(climb_two_kernel, height=height, row=row),
        out_shape=(node, node),
        in_specs=[SMEM] + [VMEM] * 6,
        out_specs=(VMEM, VMEM),
        compiler_params=params(),
        cost_estimate=cost(),
        name=f"climb{height}",
    )(me, own, *others, skels, interps)


def top_kernel(*refs):
    parts, (rows, acc, cols, loads) = refs[:-4], refs[-4:]
    for t, part in enumerate(parts):
        node = part[0, :, :128] if len(part.shape) == 3 else part[...]
        cols[:, t * 128 : (t + 1) * 128] = source_matrix(node[:64], norm_row(node[:64]))
        loads[:, t * 128 : (t + 1) * 128] = jnp.concatenate([node[64:]] * 8, axis=0)
    lane = lax.broadcasted_iota(jnp.int32, (256, 128), 1) >> 4

    def two_leaves(i, carry):
        both = rows[pl.ds(2 * i, 2)].reshape(512, 128)
        value = jnp.exp(dot(both, cols[...])).astype(bf16)
        result = dot_nt(value, loads[...])
        group = lax.div(i, 4)
        place = (2 * i) & 7
        acc[group] += jnp.where(lane == place, result[:256], 0.0) + jnp.where(
            lane == place + 1, result[256:], 0.0
        )
        return carry

    acc[...] = jnp.zeros_like(acc)
    lax.fori_loop(0, rows.shape[0] // 2, two_leaves, 0, unroll=2)


def top(parts, rows):
    levels = len(parts)
    return pl.pallas_call(
        top_kernel,
        out_shape=jax.ShapeDtypeStruct((rows.shape[0] // 8, 256, 128), f32),
        grid=(1,),
        in_specs=[last_block(part) for part in parts] + [VMEM],
        out_specs=VMEM,
        scratch_shapes=[
            pltpu.VMEM((128, levels * 128), bf16),
            pltpu.VMEM((128, levels * 128), bf16),
        ],
        compiler_params=params(),
        cost_estimate=cost(),
        name="top",
    )(*parts, rows)


def last_kernel(*refs, n_far):
    fars = refs[:n_far]
    above, norms = refs[n_far : n_far + 2]
    received, out = refs[n_far + 2 : -1], refs[-1]
    groups = above.shape[0]
    for group in range(groups):
        local = above[group]
        for far in fars[group * n_far // groups : (group + 1) * n_far // groups]:
            local = local + far[...]
        local = jnp.transpose(local)
        total = received[0][group].astype(f32)
        for part in received[1:]:
            total = total + part[group].astype(f32)
        total = jnp.transpose(total)
        for j in range(8):
            leaf = group * 8 + j
            rows = slice(16 * j, 16 * j + 16)
            out[:, leaf * 256 : (leaf + 1) * 256] = local[rows] + total[rows] * jnp.exp(-norms[leaf])


def last(fars, above, norms, received):
    return pl.pallas_call(
        functools.partial(last_kernel, n_far=len(fars)),
        out_shape=jax.ShapeDtypeStruct((16, norms.shape[0] * 256), f32),
        in_specs=[VMEM] * (2 + len(fars) + len(received)),
        out_specs=VMEM,
        compiler_params=params(),
        cost_estimate=cost(),
        name="last_sum",
    )(*fars, above, norms, *received)


def swap(value, mask):
    pairs = [(d, d ^ mask) for d in range(lax.axis_size("leaf"))]
    return lax.ppermute(value, "leaf", pairs)


def after(value, *others):
    return lax.optimization_barrier((value,) + others)[0]


def shards(
    points,
    charges,
    leaf_order,
    near_owner,
    near_slot,
    far_list,
    far_count,
    leaf_interp,
    leaf_skel,
    inner_interp,
    inner_skel,
    top_interp,
    top_skel,
):
    device_count = lax.axis_size("leaf")
    bits = device_count.bit_length() - 1
    source_bits = tuple(b for b in range(bits) if b not in TARGET_BITS)
    outer_bits = source_bits[1:]
    device = lax.axis_index("leaf")
    leaves = near_owner.shape[0]
    me = device.reshape(1).astype(jnp.int32)
    mates = range(1, 2 ** len(TARGET_BITS))
    early_bits = outer_bits[:-1]
    late = 2 ** outer_bits[-1]

    def payload_codes(payload, first):
        near = payload[-2 * near_owner.shape[1] :, :leaves].astype(jnp.int32)
        return codes_of(near[: near_owner.shape[1]], near[near_owner.shape[1] :], first, leaves)

    owner, slot = near_owner.T, near_slot.T
    src, tgt, cols, loads, rows, norms, mine, interps, skels, codes = first_part(
        points, charges, leaf_order, owner, slot,
        leaf_interp, leaf_skel, inner_interp, inner_skel, top_interp, top_skel,
    )
    pieces = {0: src, late: swap(src, late)}
    for b in reversed(early_bits):
        pieces[2**b] = swap(src, 2**b)
    beside = swap(tgt, 2 ** TARGET_BITS[0])
    far_away = swap(tgt, 2 ** TARGET_BITS[1])
    pieces[1] = swap(mine, 1)

    def far(call, codes, token):
        return self_and_far(
            codes, after(far_list, token), far_count, cols, loads, rows, call, 2
        )

    far0, lists0 = far(0, [codes], norms)
    node = climb(me, after(mine, far0), pieces[1], skels, interps, 0, 0)
    siblings = [pieces[1], swap(node, 2)]
    far1, _ = far(1, [], node)
    node = climb(me, node, after(siblings[1], far1), skels, interps, 1, 1)
    last_targets = swap(after(far_away, far1), 2 ** TARGET_BITS[0])
    for n, b in enumerate(early_bits):
        for low in range(2**n):
            place = spread(low, early_bits[:n])
            if low:
                pieces[place | 2**b] = swap(pieces[place], 2**b)
    wanted = [spread(k, source_bits) for k in range(2 ** (len(source_bits) - 1))]
    targets = [tgt, beside, far_away, last_targets]
    lists = lists0
    height, row = 2, 2
    others = [swap(node, k * 2**height) for k in (1, 2, 3)]
    sums, *tables = near(
        0,
        [lists[0][0]],
        targets[:3],
        [pieces[k] for k in wanted if k == 1 or not k & 1],
        codes=[payload_codes(after(part, far1, node), 0) for part in (beside, far_away)],
    )
    others[0] = after(others[0], sums)
    while height + 1 < bits:
        if height > 2:
            others = [swap(node, k * 2**height) for k in (1, 2, 3)]
        sibling, node = climb_two(me, node, others, skels, interps, height, row)
        siblings += [others[0], sibling]
        height, row = height + 2, row + 3
    for k in wanted[2::2]:
        pieces[k | 1] = swap(after(pieces[k], node), 1)
    pieces[late] = after(pieces[late], node)
    for n, b in enumerate(early_bits):
        for low in range(2**n):
            place = spread(low, early_bits[:n]) | late
            pieces[place | 2**b] = swap(pieces[place], 2**b)
    pieces[late | 1] = swap(pieces[late], 1)
    if height < bits:
        siblings.append(swap(node, 2**height))
    sums, last_table, all_targets = near(
        1,
        [lists[0][1], tables[0], tables[2]],
        targets,
        [pieces[k] for k in wanted + [late, late | 1]],
        codes=[payload_codes(after(last_targets, node), 1)],
        before=sums,
    )
    for k in wanted[2::2]:
        pieces[k | late | 1] = swap(after(pieces[k | late], sums), 1)
    parts = near(
        2,
        [lists[0][2], tables[1], tables[3], last_table],
        [all_targets],
        [pieces[k | late] for k in wanted[2:]],
        before=sums,
    )
    siblings[-1] = after(siblings[-1], parts[0])
    received = [parts[0]] + [
        swap(after(parts[k], siblings[-1]), spread(k, TARGET_BITS)) for k in mates
    ]
    above = top(siblings, after(rows, parts[0]))
    return last((far0, far1), above, norms, received)


def solution(mesh):
    in_specs = (
        P(None, "leaf"),
        P(None, "leaf"),
        P("leaf"),
        P("leaf", None),
        P("leaf", None),
        P("leaf", None),
        P("leaf"),
        P("leaf", None, None),
        P("leaf", None),
        P("leaf", None, None),
        P("leaf", None),
        P(),
        P(),
    )
    out_specs = P(None, "leaf")
    return jax.shard_map(shards, mesh=mesh, in_specs=in_specs, out_specs=out_specs, check_vma=False)
```

```python
import functools

import jax
import jax.numpy as jnp
from jax import lax
from jax.experimental import pallas as pl
from jax.experimental.pallas import tpu as pltpu
from jax.sharding import PartitionSpec as P

TARGET_BITS = (1, 3)
STEPS = (8, 4, 2)
DUMMY = 1 << 30
PHASE_BIT = 24
CODE = (1 << PHASE_BIT) - 1
VMEM_LIMIT = 24 * 1024 * 1024
FIRST_LIMIT = 58 * 1024 * 1024
PHASES = 3
bf16 = jnp.bfloat16
f32 = jnp.float32

VMEM = pl.BlockSpec(memory_space=pltpu.VMEM)
SMEM = pl.BlockSpec(memory_space=pltpu.SMEM)
ANY = pl.BlockSpec(memory_space=pl.ANY)
HBM = pl.BlockSpec(memory_space=pltpu.HBM)


def params(limit=VMEM_LIMIT):
    return pltpu.CompilerParams(vmem_limit_bytes=limit)


def cost():
    return pl.CostEstimate(flops=1, bytes_accessed=1, transcendentals=0)


def dot(a, b):
    return lax.dot_general(a, b, (((1,), (0,)), ((), ())), preferred_element_type=f32)


def dot_nt(a, b):
    return lax.dot_general(a, b, (((1,), (1,)), ((), ())), preferred_element_type=f32)


def split3(value):
    hi = value.astype(bf16).astype(f32)
    rest = value - hi
    mid = rest.astype(bf16).astype(f32)
    return hi, mid, rest - mid


def norm_row(coords):
    wide = coords.astype(f32)
    return jnp.sum(wide * wide, axis=0, keepdims=True) * 0.125


def extra_rows(norms, first):
    hi, mid, lo = split3(-norms)
    row = lax.broadcasted_iota(jnp.int32, (16, norms.shape[1]), 0)
    one_at = 3 - first
    out = jnp.where((row >= one_at) & (row < one_at + 3), 1.0, 0.0)
    out = jnp.where(row == first, hi, out)
    out = jnp.where(row == first + 1, mid, out)
    return jnp.where(row == first + 2, lo, out)


def source_matrix(coords, norms):
    width = coords.shape[1]
    extra = extra_rows(norms, 0).astype(bf16)
    return jnp.concatenate([coords, extra, jnp.zeros((48, width), bf16)], axis=0)


def target_matrix(coords, norms):
    width = coords.shape[1]
    extra = extra_rows(norms, 3)
    wide = jnp.concatenate(
        [coords.astype(f32) * 0.25, extra, jnp.zeros((48, width), f32)], axis=0
    )
    return jnp.transpose(wide).astype(bf16)


def tiles_sum(count, exponent, weight):
    total = None
    value = None
    ahead = exponent(0)
    for u in range(count):
        now = ahead
        if u + 1 < count:
            ahead = exponent(u + 1)
        if value is not None:
            part = dot_nt(value, weight(u - 1))
            total = part if total is None else total + part
        value = jnp.exp(now).astype(bf16)
    part = dot_nt(value, weight(count - 1))
    return part if total is None else total + part


def placed(loads, place):
    zero = jnp.zeros_like(loads)
    return jnp.concatenate(
        [jnp.where(place == k, loads, zero) for k in range(8)], axis=0
    )


def onehot(picks, size):
    row = lax.broadcasted_iota(jnp.int32, (size, picks.shape[1]), 0)
    return jnp.where(row == picks, 1.0, 0.0).astype(bf16)


def combine(left, right, picks, interp):
    both = jnp.concatenate([left, right], axis=1)
    coords = dot(both[:64], onehot(picks, 256)).astype(bf16)
    load = dot(both[64:], interp).astype(bf16)
    return jnp.concatenate([coords, load], axis=0)


def spread(number, bits):
    return sum(((number >> k) & 1) << b for k, b in enumerate(bits))


def compress(number, bits):
    return sum(((number >> b) & 1) << k for k, b in enumerate(bits))


def codes_of(owner, slot, first, leaves):
    bits = lax.axis_size("leaf").bit_length() - 1
    source_bits = [b for b in range(bits) if b not in TARGET_BITS]
    other = owner ^ lax.axis_index("leaf")
    place = compress(other, source_bits) * leaves + slot
    here = jnp.where((other & sum(2**b for b in TARGET_BITS)) == 0, 1, 0)
    half = 2 ** (len(source_bits) - 1)
    is_late = place >= half * leaves
    place = place & (half * leaves - 1)
    is_last = is_late & (place >= 2 * leaves)
    piece = place >> (leaves.bit_length() - 1)
    is_first = jnp.logical_not(is_late) & ((piece < 2) | ((piece & 1) == 0))
    if first != 0:
        is_first = is_first & (piece < 0)
    phase = jnp.where(is_last, 2, jnp.where(is_first, 0, 1))
    first_place = place - (piece - jnp.where(piece < 2, piece, (piece >> 1) + 1)) * leaves
    place = jnp.where(
        is_last,
        place - 2 * leaves,
        jnp.where(is_late, half * leaves + place, jnp.where(is_first, first_place, place)),
    )
    target = lax.broadcasted_iota(jnp.int32, owner.shape, 1) & 7
    return (here << (phase + PHASE_BIT)) | (target << 16) | place


def first_kernel(
    order_in, points_in, charges_in, owner_in, slot_in,
    leaf_interp_in, leaf_skel_in, inner_interp_in, inner_skel_in, top_interp, top_skel,
    src_out, tgt_out, cols_out, loads_out, rows_out, norms_out, mine_out, interps_out, skels_out, codes_out,
    points, charges, owner, slot, unsorted, buffer0, buffer1, src, tgt, cols, loads, rows, norms,
    joined, root, interps, skels, codes, order, leaf_interp, leaf_skel, inner_interp, inner_skel, sems,
):
    count = points.shape[1]
    chunks = 4
    width = count // chunks
    begun = []

    def begin(a, b):
        copy = pltpu.make_async_copy(a, b, sems.at[len(begun)])
        copy.start()
        begun.append(copy)
        return copy

    parts = [begin(charges_in, charges)]
    for c in range(chunks):
        at = pl.ds(c * width, width)
        parts.append(begin(points_in.at[:, at], points.at[:, at]))
    order_copy = begin(order_in, order)
    near_lists = [begin(owner_in, owner), begin(slot_in, slot)]
    needed = [
        begin(leaf_skel_in, leaf_skel),
        begin(leaf_interp_in, leaf_interp),
        begin(inner_skel_in, inner_skel),
        begin(inner_interp_in, inner_interp),
    ]
    rest = []
    path = path_rows()
    on_path = []
    for k in range(interps_out.shape[0]):
        on_path.append(begin(top_interp.at[path[k]], interps.at[k]))
        on_path.append(begin(top_skel.at[pl.ds(path[k], 1)], skels.at[k]))

    parts[0].wait()
    for c in range(count // 128):
        at = slice(c * 128, (c + 1) * 128)
        if c * 128 % width == 0:
            parts[1 + c * 128 // width].wait()
        block = jnp.concatenate(
            [
                points[:, at].astype(f32),
                charges[:, at].astype(f32),
                jnp.zeros((48, 128), f32),
            ],
            axis=0,
        )
        unsorted[at, :] = jnp.transpose(block)

    leaves = src.shape[0]
    first_node = 2 * leaves
    lane = lax.broadcasted_iota(jnp.int32, (256, 128), 1)

    def finish(node, both):
        joined[node] = both
        cols[first_node + node] = source_matrix(both[:64], norm_row(both[:64]))
        loads[first_node + node] = both[64:]

    def copy_rows(pair, buffer):
        base = pl.multiple_of(pair * 512, 512)
        for u in range(512):
            buffer[u : u + 1, :] = unsorted[pl.ds(order[base + u], 1), :]

    def process(pair, buffer):
        even = buffer[:256]
        odd = buffer[256:]
        both = jnp.where(lane < 64, even, pltpu.roll(odd, 64, 1))
        tgt[pl.ds(pl.multiple_of(pair * 256, 256), 256), :] = (both * 0.25).astype(bf16)
        for k, mine in enumerate((even, odd)):
            i = 2 * pair + k
            both = jnp.transpose(mine)[:80].astype(bf16)
            src[i] = both
            coords, load = both[:64], both[64:]
            norm = norm_row(coords)
            norms[i] = norm
            rows[i] = target_matrix(coords, norm)
            matrix = source_matrix(coords, norm)
            for half in range(2):
                cols[2 * i + half] = matrix[:, half * 128 : half * 128 + 128]
                loads[2 * i + half] = load[:, half * 128 : half * 128 + 128]
            picked = dot(coords, onehot(leaf_skel[pl.ds(i, 1), :], 256)).astype(bf16)
            value = dot(load, leaf_interp[i]).astype(bf16)
            finish(i, jnp.concatenate([picked, value], axis=0))
        node = combine(
            joined[2 * pair],
            joined[2 * pair + 1],
            inner_skel[pl.ds(pair, 1), :],
            inner_interp[pair],
        )
        finish(leaves + pair, node)

    for copy in needed + [order_copy]:
        copy.wait()

    def two_pairs(i, carry):
        copy_rows(2 * i, buffer0)
        process(jnp.maximum(2 * i - 1, 0), buffer1)
        copy_rows(2 * i + 1, buffer1)
        process(2 * i, buffer0)
        return carry

    lax.fori_loop(0, leaves // 4, two_pairs, 0)
    process(leaves // 2 - 1, buffer1)
    for copy in near_lists + on_path:
        copy.wait()
    codes[...] = codes_of(owner[...], slot[...], 0, leaves)
    rest += [begin(interps, interps_out), begin(skels, skels_out), begin(codes, codes_out)]
    near = jnp.concatenate([owner[...].astype(f32), slot[...].astype(f32)], axis=0)
    blank = jnp.zeros((near.shape[0], 128 - near.shape[1]), f32)
    tgt[count // 2 :, :] = jnp.concatenate([near, blank], axis=1).astype(bf16)
    rest += [begin(src, src_out), begin(tgt, tgt_out), begin(src, mine_out.at[pl.ds(0, leaves)])]
    rest += [begin(rows, rows_out), begin(norms, norms_out)]
    tiles = pl.ds(0, 3 * leaves + leaves // 2)
    rest += [begin(cols.at[tiles], cols_out.at[tiles])]
    first, half = leaves, leaves // 4
    number, row = leaves + leaves // 2, leaves // 2
    while half > 0:
        for j in range(half):
            left = joined[first + 2 * j]
            right = joined[first + 2 * j + 1]
            finish(number, combine(left, right, inner_skel[row : row + 1, :], inner_interp[row]))
            number, row = number + 1, row + 1
        first = first + 2 * half
        half = half // 2
    node = joined[2 * leaves - 2]
    root[...] = jnp.concatenate([node, jnp.zeros_like(node)], axis=1)
    last = cols.shape[0] - 1
    cols[last] = jnp.zeros((128, 128), bf16)
    loads[last] = jnp.zeros((16, 128), bf16)
    inner_tiles = pl.ds(3 * leaves + leaves // 2, leaves // 2)
    rest += [begin(root, mine_out.at[leaves]), begin(loads, loads_out)]
    rest += [begin(cols.at[inner_tiles], cols_out.at[inner_tiles])]
    for copy in rest:
        copy.wait()


def path_rows():
    devices = lax.axis_size("leaf")
    device = lax.axis_index("leaf")
    bits = devices.bit_length() - 1

    def row_at(height, node):
        return devices - (devices >> (height - 1)) + node

    path = [row_at(1, device >> 1), row_at(2, device >> 2)]
    for height in range(2, bits - 1, 2):
        up = device >> (height + 1)
        path += [row_at(height + 1, up), row_at(height + 1, up ^ 1)]
        path.append(row_at(min(height + 2, bits - 1), up >> 1))
    return path


def first_part(points, charges, order, owner, slot, *tables):
    count = points.shape[1]
    leaves = count // 256
    tiles = 4 * leaves
    steps = len(path_rows())
    leaf_interp, leaf_skel, inner_interp, inner_skel = tables[:4]
    src = (leaves, 80, 256)
    tgt = (count // 2 + 2 * owner.shape[0], 128)
    cols = (tiles, 128, 128)
    loads = (tiles, 16, 128)
    rows = (leaves, 256, 128)
    norms = (leaves, 1, 256)
    shapes = [
        (src, bf16),
        (tgt, bf16),
        (cols, bf16),
        (loads, bf16),
        (rows, bf16),
        (norms, f32),
        ((leaves + 1, 80, 256), bf16),
        ((steps, 256, 128), bf16),
        ((steps, 1, 128), jnp.int32),
        (owner.shape, jnp.int32),
    ]
    held = [
        (points.shape, bf16),
        (charges.shape, bf16),
        (owner.shape, jnp.int32),
        (slot.shape, jnp.int32),
        ((count, 128), f32),
        ((512, 128), f32),
        ((512, 128), f32),
    ]
    held += shapes[:6]
    held += [((2 * leaves - 1, 80, 128), bf16), ((80, 256), bf16)]
    held += shapes[7:]
    n_before = len(held)
    held += [(table.shape, table.dtype) for table in tables[:4]]
    return pl.pallas_call(
        first_kernel,
        out_shape=tuple(jax.ShapeDtypeStruct(*shape) for shape in shapes),
        in_specs=[ANY] * 11,
        out_specs=(ANY,) * 10,
        scratch_shapes=[pltpu.VMEM(*shape) for shape in held[:n_before]]
        + [pltpu.SMEM(order.shape, jnp.int32)]
        + [pltpu.VMEM(*shape) for shape in held[n_before:]]
        + [pltpu.SemaphoreType.DMA((24 + 2 * steps,))],
        compiler_params=params(FIRST_LIMIT),
        cost_estimate=cost(),
        name="order_and_subtree",
    )(order, points, charges, owner, slot, *tables)


def far_kernel(*refs, first_leaf, n_leaves, n_ids):
    codes = refs[:n_ids]
    far_list, far_count, cols_in, loads_in, rows_in, acc = refs[n_ids : 6 + n_ids]
    lists = refs[6 + n_ids : -5]
    cols, loads, rows, tiles, sems = refs[-5:]
    leaves = rows.shape[0]
    width = far_list.shape[1]
    first_node = 2 * leaves
    empty = cols.shape[0] - 1
    mine = pl.ds(first_leaf, n_leaves)
    my_tiles = pl.ds(2 * first_leaf, 2 * n_leaves)
    nodes = pl.ds(first_node, cols.shape[0] - first_node)
    copies = [
        pltpu.make_async_copy(rows_in.at[mine], rows.at[mine], sems.at[0]),
        pltpu.make_async_copy(cols_in.at[my_tiles], cols.at[my_tiles], sems.at[1]),
        pltpu.make_async_copy(loads_in, loads, sems.at[2]),
        pltpu.make_async_copy(cols_in.at[nodes], cols.at[nodes], sems.at[3]),
    ]
    for copy in copies:
        copy.start()

    def list_leaf(k, count):
        i = first_leaf + k
        tiles[count] = (i << 16) | ((2 * i) << 8) | (2 * i + 1)
        count = count + 1
        used = far_count[i]
        for k in range(0, width, 2):
            first = far_list[i, k] + first_node
            second = jnp.where(k + 1 < used, far_list[i, k + 1] + first_node, empty)
            tiles[count] = (i << 16) | (first << 8) | second
            count = count + (k < used).astype(jnp.int32)
        return count

    count = lax.fori_loop(0, n_leaves, list_leaf, 0)
    tiles[count] = (empty << 8) | empty
    count = (count + 1) & ~1

    def step(start, size):
        values, weights = [], []
        for u in range(size):
            packed = tiles[start + u]
            leaf = packed >> 16
            first = (packed >> 8) & 255
            second = packed & 255
            matrix = jnp.concatenate([cols[first], cols[second]], axis=1)
            load = jnp.concatenate([loads[first], loads[second]], axis=1)
            values.append(jnp.exp(dot(rows[leaf], matrix)).astype(bf16))
            weights.append(placed(load, leaf & 7))
        acc[...] += dot_nt(jnp.concatenate(values, axis=1), jnp.concatenate(weights, axis=1))

    acc[...] = jnp.zeros_like(acc)
    for k in range(n_ids):
        list_pairs(codes[k], lists[PHASES * k : PHASES * k + PHASES])
    for copy in copies:
        copy.wait()
    largest = STEPS[0]
    whole = lax.div(count, largest)

    def full_step(i, carry):
        step(i * largest, largest)
        return carry

    lax.fori_loop(0, whole, full_step, 0)
    for size in STEPS[1:]:

        @pl.when((count & size) > 0)
        def _(size=size):
            step(count & ~(2 * size - 1), size)


def list_pairs(codes, tables):
    per_leaf, leaves = codes.shape
    for g in range(leaves // 8):
        counts = [jnp.int32(0)] * len(tables)
        for j in range(8):
            for u in range(per_leaf):
                value = codes[u, g * 8 + j]
                for p, table in enumerate(tables):
                    if table is None:
                        continue
                    table[g, 1 + counts[p]] = value & CODE
                    counts[p] = counts[p] + ((value >> (PHASE_BIT + p)) & 1)
        for p, table in enumerate(tables):
            if table is None:
                continue
            table[g, 1 + counts[p]] = DUMMY
            table[g, 0] = (counts[p] + 1) & ~1


def pair_table(leaves):
    return jax.ShapeDtypeStruct((leaves // 8, 128), jnp.int32)


def self_and_far(codes, far_list, far_count, cols, loads, rows, call, calls):
    leaves = rows.shape[0]
    width = far_list.shape[1]
    n_leaves = leaves // calls
    out = pl.pallas_call(
        functools.partial(
            far_kernel, first_leaf=call * n_leaves, n_leaves=n_leaves, n_ids=len(codes)
        ),
        out_shape=(jax.ShapeDtypeStruct((256, 128), f32),) + (pair_table(leaves),) * (PHASES * len(codes)),
        in_specs=[SMEM] * (2 + len(codes)) + [ANY] * 3,
        out_specs=(VMEM,) + (SMEM,) * (PHASES * len(codes)),
        scratch_shapes=[
            pltpu.VMEM(cols.shape, bf16),
            pltpu.VMEM(loads.shape, bf16),
            pltpu.VMEM(rows.shape, bf16),
            pltpu.SMEM((n_leaves * (1 + width // 2) + 2,), jnp.int32),
            pltpu.SemaphoreType.DMA((4,)),
        ],
        compiler_params=params(FIRST_LIMIT),
        cost_estimate=cost(),
        name=f"self_and_far{call}",
    )(*codes, far_list, far_count, cols, loads, rows)
    return out[0], [out[1 + PHASES * k : 1 + PHASES * k + PHASES] for k in range(len(codes))]


def near_kernel(*refs, n_sources, n_targets, n_lists, n_codes, phase):
    refs = list(refs)

    def take(n):
        taken = refs[:n]
        del refs[:n]
        return taken

    makes = phase < PHASES - 1
    codes = take(n_codes)
    lists = take(n_lists)
    target_parts = take(n_targets if makes else 1)
    source_parts = take(n_sources)
    before = take(phase > 0)
    outs = take(n_targets) if not makes else []
    (acc,) = take(1) if makes else (None,)
    tables = [take(PHASES - 1 - phase) for _ in range(n_codes)]
    if phase == 1:
        (targets,) = take(1)
    elif phase == 2:
        (targets,) = target_parts
        target_parts = []
    sources, sems, pairs, steps = take(4)
    if phase == 0:
        (targets,) = take(1)
    if not makes:
        (acc,) = take(1)
    leaves = source_parts[0].shape[0]
    size = leaves * 128
    copies = []

    def begin(part, place):
        copies.append(pltpu.make_async_copy(part, place, sems.at[len(copies)]))
        copies[-1].start()

    own_rows = acc.shape[0] // n_targets
    for k, part in enumerate(lists):
        begin(part, pairs.at[pl.ds(k * own_rows, own_rows)])
    for k, part in enumerate(target_parts):
        begin(part.at[pl.ds(0, size)], targets.at[pl.ds(k * size, size)])
    for k, part in enumerate(source_parts):
        begin(part.at[pl.ds(0, leaves)], sources.at[pl.ds(k * leaves, leaves)])
    acc[...] = jnp.zeros_like(acc)
    for k in range(n_codes):
        table = pairs.at[pl.ds((n_lists + k) * own_rows, own_rows)]
        list_pairs(codes[k], [None] * phase + [table] + tables[k])
    for copy in copies:
        copy.wait()

    counts = [jnp.int32(0)] * len(STEPS)
    for row in range(pairs.shape[0]):
        used = pairs[row, 0]
        whole = lax.div(used, STEPS[0])

        def note(i, count, row=row):
            steps[0, count + i] = row * 128 + 1 + i * STEPS[0]
            return count

        lax.fori_loop(0, whole, note, counts[0])
        counts[0] = counts[0] + whole
        for k, size in enumerate(STEPS[1:], 1):
            steps[k, counts[k]] = row * 128 + 1 + (used & ~(2 * size - 1))
            counts[k] = counts[k] + jnp.where((used & size) > 0, 1, 0)

    for k, size in enumerate(STEPS):

        def step(i, carry, k=k, size=size):
            group = steps[k, i] >> 7
            start = steps[k, i] & 127

            def exponent(u):
                packed = pairs[group, start + u]
                target = (packed >> 16) & 7
                coords = sources[packed & 65535, :64, :]
                odd = target & 1
                zero = jnp.zeros_like(coords)
                matrix = jnp.concatenate(
                    [jnp.where(odd == 0, coords, zero), jnp.where(odd == 1, coords, zero)],
                    axis=0,
                )
                at = pl.multiple_of(group * 1024 + (target >> 1) * 256, 256)
                return dot(targets[pl.ds(at, 256), :], matrix) - norm_row(coords)

            def weight(u):
                packed = pairs[group, start + u]
                place = jnp.where(packed < DUMMY, (packed >> 16) & 7, 8)
                return placed(sources[packed & 65535, 64:, :], place)

            acc[group] += tiles_sum(size, exponent, weight)
            return carry

        lax.fori_loop(0, counts[k], step, 0)

    if makes:
        for part in before:
            acc[: part.shape[0]] += part[...]
    for k, out in enumerate(outs):
        mine = slice(k * own_rows, (k + 1) * own_rows)
        out[...] = (acc[mine] + before[0][mine]).astype(bf16)


def near(phase, lists, targets, sources, codes=(), before=None):
    n_sources, n_codes = len(sources), len(codes)
    makes = phase < PHASES - 1
    n_targets = len(targets) if makes else len(lists)
    leaves = min(source.shape[0] for source in sources)
    sums = jax.ShapeDtypeStruct((n_targets * leaves // 8, 256, 128), f32)
    part = jax.ShapeDtypeStruct((leaves // 8, 256, 128), bf16)
    held_targets = jax.ShapeDtypeStruct((n_targets * leaves * 128, 128), bf16)
    args = list(codes) + list(lists) + list(targets) + list(sources)
    in_specs = [SMEM] * n_codes + [ANY] * (len(args) - n_codes)
    if not makes:
        in_specs[len(lists)] = VMEM
    if before is not None:
        args.append(before)
        in_specs.append(VMEM)
    if makes:
        n_tables = n_codes * (PHASES - 1 - phase)
        out_shape = (sums,) + (pair_table(leaves),) * n_tables
        out_specs = (VMEM,) + (SMEM,) * n_tables
        if phase == 1:
            out_shape, out_specs = out_shape + (held_targets,), out_specs + (VMEM,)
    else:
        out_shape, out_specs = (part,) * n_targets, (VMEM,) * n_targets
    scratch = [
        pltpu.VMEM((n_sources * leaves, 80, 256), bf16),
        pltpu.SemaphoreType.DMA((n_sources + n_targets + len(lists),)),
        pltpu.SMEM((n_targets * leaves // 8, 128), jnp.int32),
        pltpu.SMEM((len(STEPS), n_targets * leaves), jnp.int32),
    ]
    if phase == 0:
        scratch.append(pltpu.VMEM(held_targets.shape, bf16))
    if not makes:
        scratch.append(pltpu.VMEM(sums.shape, f32))
    return pl.pallas_call(
        functools.partial(
            near_kernel,
            n_sources=n_sources,
            n_targets=n_targets,
            n_lists=len(lists),
            n_codes=n_codes,
            phase=phase,
        ),
        out_shape=out_shape,
        in_specs=in_specs,
        out_specs=out_specs,
        scratch_shapes=scratch,
        compiler_params=params(),
        cost_estimate=cost(),
        name=f"near{phase}",
    )(*args)


def ordered(first, second, test):
    return jnp.where(test, first, second), jnp.where(test, second, first)


def climb_kernel(me, own, other, skels, interps, parent, *, height, row):
    sibling = other[0, :, :128] if len(other.shape) == 3 else other[...]
    left, right = ordered(own[0, :, :128] if len(own.shape) == 3 else own[...], sibling, ((me[0] >> height) & 1) == 0)
    parent[...] = combine(left, right, skels[row], interps[row])


def last_block(value):
    if value.ndim == 2:
        return VMEM
    blocks = value.shape[0]
    return pl.BlockSpec((1,) + value.shape[1:], lambda i: (blocks - 1, 0, 0))


def climb(me, own, other, skels, interps, height, row):
    return pl.pallas_call(
        functools.partial(climb_kernel, height=height, row=row),
        grid=(1,),
        out_shape=jax.ShapeDtypeStruct((80, 128), bf16),
        in_specs=[SMEM, last_block(own), last_block(other), VMEM, VMEM],
        out_specs=VMEM,
        compiler_params=params(),
        cost_estimate=cost(),
        name=f"climb{height}",
    )(me, own, other, skels, interps)


def climb_two_kernel(me, own, one, two, three, skels, interps, sibling, parent, *, height, row):
    node = me[0] >> height
    is_left = (node & 1) == 0
    left, right = ordered(own[...], one[...], is_left)
    mine = combine(left, right, skels[row], interps[row])
    left, right = ordered(two[...], three[...], is_left)
    other = combine(left, right, skels[row + 1], interps[row + 1])
    sibling[...] = other
    left, right = ordered(mine, other, (node & 2) == 0)
    parent[...] = combine(left, right, skels[row + 2], interps[row + 2])


def climb_two(me, own, others, skels, interps, height, row):
    node = jax.ShapeDtypeStruct((80, 128), bf16)
    return pl.pallas_call(
        functools.partial(climb_two_kernel, height=height, row=row),
        out_shape=(node, node),
        in_specs=[SMEM] + [VMEM] * 6,
        out_specs=(VMEM, VMEM),
        compiler_params=params(),
        cost_estimate=cost(),
        name=f"climb{height}",
    )(me, own, *others, skels, interps)


def top_kernel(*refs):
    parts, (rows, acc, cols, loads) = refs[:-4], refs[-4:]
    for t, part in enumerate(parts):
        node = part[0, :, :128] if len(part.shape) == 3 else part[...]
        cols[:, t * 128 : (t + 1) * 128] = source_matrix(node[:64], norm_row(node[:64]))
        loads[:, t * 128 : (t + 1) * 128] = jnp.concatenate([node[64:]] * 8, axis=0)
    lane = lax.broadcasted_iota(jnp.int32, (256, 128), 1) >> 4

    def two_leaves(i, carry):
        both = rows[pl.ds(2 * i, 2)].reshape(512, 128)
        value = jnp.exp(dot(both, cols[...])).astype(bf16)
        result = dot_nt(value, loads[...])
        group = lax.div(i, 4)
        place = (2 * i) & 7
        acc[group] += jnp.where(lane == place, result[:256], 0.0) + jnp.where(
            lane == place + 1, result[256:], 0.0
        )
        return carry

    acc[...] = jnp.zeros_like(acc)
    lax.fori_loop(0, rows.shape[0] // 2, two_leaves, 0, unroll=2)


def top(parts, rows):
    levels = len(parts)
    return pl.pallas_call(
        top_kernel,
        out_shape=jax.ShapeDtypeStruct((rows.shape[0] // 8, 256, 128), f32),
        grid=(1,),
        in_specs=[last_block(part) for part in parts] + [VMEM],
        out_specs=VMEM,
        scratch_shapes=[
            pltpu.VMEM((128, levels * 128), bf16),
            pltpu.VMEM((128, levels * 128), bf16),
        ],
        compiler_params=params(),
        cost_estimate=cost(),
        name="top",
    )(*parts, rows)


def last_kernel(*refs, n_far):
    fars = refs[:n_far]
    above, norms = refs[n_far : n_far + 2]
    received, out = refs[n_far + 2 : -1], refs[-1]
    groups = above.shape[0]
    for group in range(groups):
        local = above[group]
        for far in fars[group * n_far // groups : (group + 1) * n_far // groups]:
            local = local + far[...]
        local = jnp.transpose(local)
        total = received[0][group].astype(f32)
        for part in received[1:]:
            total = total + part[group].astype(f32)
        total = jnp.transpose(total)
        for j in range(8):
            leaf = group * 8 + j
            rows = slice(16 * j, 16 * j + 16)
            out[:, leaf * 256 : (leaf + 1) * 256] = local[rows] + total[rows] * jnp.exp(-norms[leaf])


def last(fars, above, norms, received):
    return pl.pallas_call(
        functools.partial(last_kernel, n_far=len(fars)),
        out_shape=jax.ShapeDtypeStruct((16, norms.shape[0] * 256), f32),
        in_specs=[VMEM] * (2 + len(fars) + len(received)),
        out_specs=VMEM,
        compiler_params=params(),
        cost_estimate=cost(),
        name="last_sum",
    )(*fars, above, norms, *received)


def swap(value, mask):
    pairs = [(d, d ^ mask) for d in range(lax.axis_size("leaf"))]
    return lax.ppermute(value, "leaf", pairs)


def after(value, *others):
    return lax.optimization_barrier((value,) + others)[0]


def shards(
    points,
    charges,
    leaf_order,
    near_owner,
    near_slot,
    far_list,
    far_count,
    leaf_interp,
    leaf_skel,
    inner_interp,
    inner_skel,
    top_interp,
    top_skel,
):
    device_count = lax.axis_size("leaf")
    bits = device_count.bit_length() - 1
    source_bits = tuple(b for b in range(bits) if b not in TARGET_BITS)
    outer_bits = source_bits[1:]
    device = lax.axis_index("leaf")
    leaves = near_owner.shape[0]
    me = device.reshape(1).astype(jnp.int32)
    mates = range(1, 2 ** len(TARGET_BITS))
    early_bits = outer_bits[:-1]
    late = 2 ** outer_bits[-1]

    def payload_codes(payload, first):
        near = payload[-2 * near_owner.shape[1] :, :leaves].astype(jnp.int32)
        return codes_of(near[: near_owner.shape[1]], near[near_owner.shape[1] :], first, leaves)

    owner, slot = near_owner.T, near_slot.T
    src, tgt, cols, loads, rows, norms, mine, interps, skels, codes = first_part(
        points, charges, leaf_order, owner, slot,
        leaf_interp, leaf_skel, inner_interp, inner_skel, top_interp, top_skel,
    )
    pieces = {0: src, late: swap(src, late)}
    for b in reversed(early_bits):
        pieces[2**b] = swap(src, 2**b)
    beside = swap(tgt, 2 ** TARGET_BITS[0])
    far_away = swap(tgt, 2 ** TARGET_BITS[1])
    pieces[1] = swap(mine, 1)

    def far(call, codes, token):
        return self_and_far(
            codes, after(far_list, token), far_count, cols, loads, rows, call, 2
        )

    far0, lists0 = far(0, [codes], norms)
    node = climb(me, after(mine, far0), pieces[1], skels, interps, 0, 0)
    siblings = [pieces[1], swap(node, 2)]
    far1, _ = far(1, [], node)
    for n, b in enumerate(early_bits):
        for low in range(2**n):
            place = spread(low, early_bits[:n])
            if low:
                pieces[place | 2**b] = swap(pieces[place], 2**b)
    wanted = [spread(k, source_bits) for k in range(2 ** (len(source_bits) - 1))]
    lists = lists0
    node = climb(me, node, after(siblings[1], far1), skels, interps, 1, 1)
    sums, *tables = near(
        0,
        [lists[0][0]],
        [tgt, beside],
        [pieces[k] for k in wanted if k == 1 or not k & 1],
        codes=[payload_codes(after(beside, far1, node), 0)],
    )
    last_targets = swap(after(far_away, sums), 2 ** TARGET_BITS[0])
    targets = [tgt, beside, far_away, last_targets]
    height, row = 2, 2
    others = [swap(node, k * 2**height) for k in (1, 2, 3)]
    while height + 1 < bits:
        if height > 2:
            others = [swap(node, k * 2**height) for k in (1, 2, 3)]
        sibling, node = climb_two(me, node, others, skels, interps, height, row)
        siblings += [others[0], sibling]
        height, row = height + 2, row + 3
    for k in wanted[2::2]:
        pieces[k | 1] = swap(after(pieces[k], node), 1)
    pieces[late] = after(pieces[late], node)
    for n, b in enumerate(early_bits):
        for low in range(2**n):
            place = spread(low, early_bits[:n]) | late
            pieces[place | 2**b] = swap(pieces[place], 2**b)
    pieces[late | 1] = swap(pieces[late], 1)
    if height < bits:
        siblings.append(swap(node, 2**height))
    sums, far_table, last_table, all_targets = near(
        1,
        [lists[0][1], tables[0]],
        targets,
        [pieces[k] for k in wanted + [late, late | 1]],
        codes=[payload_codes(after(part, node), 1) for part in targets[2:]],
        before=sums,
    )
    for k in wanted[2::2]:
        pieces[k | late | 1] = swap(after(pieces[k | late], sums), 1)
    parts = near(
        2,
        [lists[0][2], tables[1], far_table, last_table],
        [all_targets],
        [pieces[k | late] for k in wanted[2:]],
        before=sums,
    )
    siblings[-1] = after(siblings[-1], parts[0])
    received = [parts[0]] + [
        swap(after(parts[k], siblings[-1]), spread(k, TARGET_BITS)) for k in mates
    ]
    above = top(siblings, after(rows, parts[0]))
    return last((far0, far1), above, norms, received)


def solution(mesh):
    in_specs = (
        P(None, "leaf"),
        P(None, "leaf"),
        P("leaf"),
        P("leaf", None),
        P("leaf", None),
        P("leaf", None),
        P("leaf"),
        P("leaf", None, None),
        P("leaf", None),
        P("leaf", None, None),
        P("leaf", None),
        P(),
        P(),
    )
    out_specs = P(None, "leaf")
    return jax.shard_map(shards, mesh=mesh, in_specs=in_specs, out_specs=out_specs, check_vma=False)
```

```python
import functools

import jax
import jax.numpy as jnp
from jax import lax
from jax.experimental import pallas as pl
from jax.experimental.pallas import tpu as pltpu
from jax.sharding import PartitionSpec as P

TARGET_BITS = (1, 3)
STEPS = (8, 4, 2)
DUMMY = 1 << 30
PHASE_BIT = 24
CODE = (1 << PHASE_BIT) - 1
VMEM_LIMIT = 24 * 1024 * 1024
FIRST_LIMIT = 58 * 1024 * 1024
PHASES = 4
bf16 = jnp.bfloat16
f32 = jnp.float32

VMEM = pl.BlockSpec(memory_space=pltpu.VMEM)
SMEM = pl.BlockSpec(memory_space=pltpu.SMEM)
ANY = pl.BlockSpec(memory_space=pl.ANY)
HBM = pl.BlockSpec(memory_space=pltpu.HBM)


def params(limit=VMEM_LIMIT):
    return pltpu.CompilerParams(vmem_limit_bytes=limit)


def cost():
    return pl.CostEstimate(flops=1, bytes_accessed=1, transcendentals=0)


def dot(a, b):
    return lax.dot_general(a, b, (((1,), (0,)), ((), ())), preferred_element_type=f32)


def dot_nt(a, b):
    return lax.dot_general(a, b, (((1,), (1,)), ((), ())), preferred_element_type=f32)


def split3(value):
    hi = value.astype(bf16).astype(f32)
    rest = value - hi
    mid = rest.astype(bf16).astype(f32)
    return hi, mid, rest - mid


def norm_row(coords):
    wide = coords.astype(f32)
    return jnp.sum(wide * wide, axis=0, keepdims=True) * 0.125


def extra_rows(norms, first):
    hi, mid, lo = split3(-norms)
    row = lax.broadcasted_iota(jnp.int32, (16, norms.shape[1]), 0)
    one_at = 3 - first
    out = jnp.where((row >= one_at) & (row < one_at + 3), 1.0, 0.0)
    out = jnp.where(row == first, hi, out)
    out = jnp.where(row == first + 1, mid, out)
    return jnp.where(row == first + 2, lo, out)


def source_matrix(coords, norms):
    width = coords.shape[1]
    extra = extra_rows(norms, 0).astype(bf16)
    return jnp.concatenate([coords, extra, jnp.zeros((48, width), bf16)], axis=0)


def target_matrix(coords, norms):
    width = coords.shape[1]
    extra = extra_rows(norms, 3)
    wide = jnp.concatenate(
        [coords.astype(f32) * 0.25, extra, jnp.zeros((48, width), f32)], axis=0
    )
    return jnp.transpose(wide).astype(bf16)


def tiles_sum(count, exponent, weight):
    total = None
    value = None
    ahead = exponent(0)
    for u in range(count):
        now = ahead
        if u + 1 < count:
            ahead = exponent(u + 1)
        if value is not None:
            part = dot_nt(value, weight(u - 1))
            total = part if total is None else total + part
        value = jnp.exp(now).astype(bf16)
    part = dot_nt(value, weight(count - 1))
    return part if total is None else total + part


def placed(loads, place):
    zero = jnp.zeros_like(loads)
    return jnp.concatenate(
        [jnp.where(place == k, loads, zero) for k in range(8)], axis=0
    )


def onehot(picks, size):
    row = lax.broadcasted_iota(jnp.int32, (size, picks.shape[1]), 0)
    return jnp.where(row == picks, 1.0, 0.0).astype(bf16)


def combine(left, right, picks, interp):
    both = jnp.concatenate([left, right], axis=1)
    coords = dot(both[:64], onehot(picks, 256)).astype(bf16)
    load = dot(both[64:], interp).astype(bf16)
    return jnp.concatenate([coords, load], axis=0)


def spread(number, bits):
    return sum(((number >> k) & 1) << b for k, b in enumerate(bits))


def compress(number, bits):
    return sum(((number >> b) & 1) << k for k, b in enumerate(bits))


def codes_of(owner, slot, first, leaves):
    bits = lax.axis_size("leaf").bit_length() - 1
    source_bits = [b for b in range(bits) if b not in TARGET_BITS]
    other = owner ^ lax.axis_index("leaf")
    place = compress(other, source_bits) * leaves + slot
    here = jnp.where((other & sum(2**b for b in TARGET_BITS)) == 0, 1, 0)
    half = 2 ** (len(source_bits) - 1)
    is_late = place >= half * leaves
    place = place & (half * leaves - 1)
    is_last = is_late & (place >= 2 * leaves)
    piece = place >> (leaves.bit_length() - 1)
    is_first = jnp.logical_not(is_late) & ((piece < 2) | ((piece & 1) == 0))
    if first != 0:
        is_first = is_first & (piece < 0)
    phase = jnp.where(is_last, PHASES - 1, jnp.where(is_first, 0, max(first, 1)))
    first_place = place - (piece - jnp.where(piece < 2, piece, (piece >> 1) + 1)) * leaves
    place = jnp.where(
        is_last,
        place - 2 * leaves,
        jnp.where(is_late, half * leaves + place, jnp.where(is_first, first_place, place)),
    )
    target = lax.broadcasted_iota(jnp.int32, owner.shape, 1) & 7
    return (here << (phase + PHASE_BIT)) | (target << 16) | place


def first_kernel(
    order_in, points_in, charges_in, owner_in, slot_in,
    leaf_interp_in, leaf_skel_in, inner_interp_in, inner_skel_in, top_interp, top_skel,
    src_out, tgt_out, cols_out, loads_out, rows_out, norms_out, mine_out, interps_out, skels_out, codes_out,
    points, charges, owner, slot, unsorted, buffer0, buffer1, src, tgt, cols, loads, rows, norms,
    joined, root, interps, skels, codes, order, leaf_interp, leaf_skel, inner_interp, inner_skel, sems,
):
    count = points.shape[1]
    chunks = 4
    width = count // chunks
    begun = []

    def begin(a, b):
        copy = pltpu.make_async_copy(a, b, sems.at[len(begun)])
        copy.start()
        begun.append(copy)
        return copy

    parts = [begin(charges_in, charges)]
    for c in range(chunks):
        at = pl.ds(c * width, width)
        parts.append(begin(points_in.at[:, at], points.at[:, at]))
    order_copy = begin(order_in, order)
    near_lists = [begin(owner_in, owner), begin(slot_in, slot)]
    needed = [
        begin(leaf_skel_in, leaf_skel),
        begin(leaf_interp_in, leaf_interp),
        begin(inner_skel_in, inner_skel),
        begin(inner_interp_in, inner_interp),
    ]
    rest = []
    path = path_rows()
    on_path = []
    for k in range(interps_out.shape[0]):
        on_path.append(begin(top_interp.at[path[k]], interps.at[k]))
        on_path.append(begin(top_skel.at[pl.ds(path[k], 1)], skels.at[k]))

    parts[0].wait()
    for c in range(count // 128):
        at = slice(c * 128, (c + 1) * 128)
        if c * 128 % width == 0:
            parts[1 + c * 128 // width].wait()
        block = jnp.concatenate(
            [
                points[:, at].astype(f32),
                charges[:, at].astype(f32),
                jnp.zeros((48, 128), f32),
            ],
            axis=0,
        )
        unsorted[at, :] = jnp.transpose(block)

    leaves = src.shape[0]
    first_node = 2 * leaves
    lane = lax.broadcasted_iota(jnp.int32, (256, 128), 1)

    def finish(node, both):
        joined[node] = both
        cols[first_node + node] = source_matrix(both[:64], norm_row(both[:64]))
        loads[first_node + node] = both[64:]

    def copy_rows(pair, buffer):
        base = pl.multiple_of(pair * 512, 512)
        for u in range(512):
            buffer[u : u + 1, :] = unsorted[pl.ds(order[base + u], 1), :]

    def process(pair, buffer):
        even = buffer[:256]
        odd = buffer[256:]
        both = jnp.where(lane < 64, even, pltpu.roll(odd, 64, 1))
        tgt[pl.ds(pl.multiple_of(pair * 256, 256), 256), :] = (both * 0.25).astype(bf16)
        for k, mine in enumerate((even, odd)):
            i = 2 * pair + k
            both = jnp.transpose(mine)[:80].astype(bf16)
            src[i] = both
            coords, load = both[:64], both[64:]
            norm = norm_row(coords)
            norms[i] = norm
            rows[i] = target_matrix(coords, norm)
            matrix = source_matrix(coords, norm)
            for half in range(2):
                cols[2 * i + half] = matrix[:, half * 128 : half * 128 + 128]
                loads[2 * i + half] = load[:, half * 128 : half * 128 + 128]
            picked = dot(coords, onehot(leaf_skel[pl.ds(i, 1), :], 256)).astype(bf16)
            value = dot(load, leaf_interp[i]).astype(bf16)
            finish(i, jnp.concatenate([picked, value], axis=0))
        node = combine(
            joined[2 * pair],
            joined[2 * pair + 1],
            inner_skel[pl.ds(pair, 1), :],
            inner_interp[pair],
        )
        finish(leaves + pair, node)

    for copy in needed + [order_copy]:
        copy.wait()

    def two_pairs(i, carry):
        copy_rows(2 * i, buffer0)
        process(jnp.maximum(2 * i - 1, 0), buffer1)
        copy_rows(2 * i + 1, buffer1)
        process(2 * i, buffer0)
        return carry

    lax.fori_loop(0, leaves // 4, two_pairs, 0)
    process(leaves // 2 - 1, buffer1)
    for copy in near_lists + on_path:
        copy.wait()
    codes[...] = codes_of(owner[...], slot[...], 0, leaves)
    rest += [begin(interps, interps_out), begin(skels, skels_out), begin(codes, codes_out)]
    near = jnp.concatenate([owner[...].astype(f32), slot[...].astype(f32)], axis=0)
    blank = jnp.zeros((near.shape[0], 128 - near.shape[1]), f32)
    tgt[count // 2 :, :] = jnp.concatenate([near, blank], axis=1).astype(bf16)
    rest += [begin(src, src_out), begin(tgt, tgt_out), begin(src, mine_out.at[pl.ds(0, leaves)])]
    rest += [begin(rows, rows_out), begin(norms, norms_out)]
    tiles = pl.ds(0, 3 * leaves + leaves // 2)
    rest += [begin(cols.at[tiles], cols_out.at[tiles])]
    first, half = leaves, leaves // 4
    number, row = leaves + leaves // 2, leaves // 2
    while half > 0:
        for j in range(half):
            left = joined[first + 2 * j]
            right = joined[first + 2 * j + 1]
            finish(number, combine(left, right, inner_skel[row : row + 1, :], inner_interp[row]))
            number, row = number + 1, row + 1
        first = first + 2 * half
        half = half // 2
    node = joined[2 * leaves - 2]
    root[...] = jnp.concatenate([node, jnp.zeros_like(node)], axis=1)
    last = cols.shape[0] - 1
    cols[last] = jnp.zeros((128, 128), bf16)
    loads[last] = jnp.zeros((16, 128), bf16)
    inner_tiles = pl.ds(3 * leaves + leaves // 2, leaves // 2)
    rest += [begin(root, mine_out.at[leaves]), begin(loads, loads_out)]
    rest += [begin(cols.at[inner_tiles], cols_out.at[inner_tiles])]
    for copy in rest:
        copy.wait()


def path_rows():
    devices = lax.axis_size("leaf")
    device = lax.axis_index("leaf")
    bits = devices.bit_length() - 1

    def row_at(height, node):
        return devices - (devices >> (height - 1)) + node

    path = [row_at(1, device >> 1), row_at(2, device >> 2)]
    for height in range(2, bits - 1, 2):
        up = device >> (height + 1)
        path += [row_at(height + 1, up), row_at(height + 1, up ^ 1)]
        path.append(row_at(min(height + 2, bits - 1), up >> 1))
    return path


def first_part(points, charges, order, owner, slot, *tables):
    count = points.shape[1]
    leaves = count // 256
    tiles = 4 * leaves
    steps = len(path_rows())
    leaf_interp, leaf_skel, inner_interp, inner_skel = tables[:4]
    src = (leaves, 80, 256)
    tgt = (count // 2 + 2 * owner.shape[0], 128)
    cols = (tiles, 128, 128)
    loads = (tiles, 16, 128)
    rows = (leaves, 256, 128)
    norms = (leaves, 1, 256)
    shapes = [
        (src, bf16),
        (tgt, bf16),
        (cols, bf16),
        (loads, bf16),
        (rows, bf16),
        (norms, f32),
        ((leaves + 1, 80, 256), bf16),
        ((steps, 256, 128), bf16),
        ((steps, 1, 128), jnp.int32),
        (owner.shape, jnp.int32),
    ]
    held = [
        (points.shape, bf16),
        (charges.shape, bf16),
        (owner.shape, jnp.int32),
        (slot.shape, jnp.int32),
        ((count, 128), f32),
        ((512, 128), f32),
        ((512, 128), f32),
    ]
    held += shapes[:6]
    held += [((2 * leaves - 1, 80, 128), bf16), ((80, 256), bf16)]
    held += shapes[7:]
    n_before = len(held)
    held += [(table.shape, table.dtype) for table in tables[:4]]
    return pl.pallas_call(
        first_kernel,
        out_shape=tuple(jax.ShapeDtypeStruct(*shape) for shape in shapes),
        in_specs=[ANY] * 11,
        out_specs=(ANY,) * 10,
        scratch_shapes=[pltpu.VMEM(*shape) for shape in held[:n_before]]
        + [pltpu.SMEM(order.shape, jnp.int32)]
        + [pltpu.VMEM(*shape) for shape in held[n_before:]]
        + [pltpu.SemaphoreType.DMA((24 + 2 * steps,))],
        compiler_params=params(FIRST_LIMIT),
        cost_estimate=cost(),
        name="order_and_subtree",
    )(order, points, charges, owner, slot, *tables)


def far_kernel(*refs, first_leaf, n_leaves, n_ids):
    codes = refs[:n_ids]
    far_list, far_count, cols_in, loads_in, rows_in, acc = refs[n_ids : 6 + n_ids]
    lists = refs[6 + n_ids : -5]
    cols, loads, rows, tiles, sems = refs[-5:]
    leaves = rows.shape[0]
    width = far_list.shape[1]
    first_node = 2 * leaves
    empty = cols.shape[0] - 1
    mine = pl.ds(first_leaf, n_leaves)
    my_tiles = pl.ds(2 * first_leaf, 2 * n_leaves)
    nodes = pl.ds(first_node, cols.shape[0] - first_node)
    copies = [
        pltpu.make_async_copy(rows_in.at[mine], rows.at[mine], sems.at[0]),
        pltpu.make_async_copy(cols_in.at[my_tiles], cols.at[my_tiles], sems.at[1]),
        pltpu.make_async_copy(loads_in, loads, sems.at[2]),
        pltpu.make_async_copy(cols_in.at[nodes], cols.at[nodes], sems.at[3]),
    ]
    for copy in copies:
        copy.start()

    def list_leaf(k, count):
        i = first_leaf + k
        tiles[count] = (i << 16) | ((2 * i) << 8) | (2 * i + 1)
        count = count + 1
        used = far_count[i]
        for k in range(0, width, 2):
            first = far_list[i, k] + first_node
            second = jnp.where(k + 1 < used, far_list[i, k + 1] + first_node, empty)
            tiles[count] = (i << 16) | (first << 8) | second
            count = count + (k < used).astype(jnp.int32)
        return count

    count = lax.fori_loop(0, n_leaves, list_leaf, 0)
    tiles[count] = (empty << 8) | empty
    count = (count + 1) & ~1

    def step(start, size):
        values, weights = [], []
        for u in range(size):
            packed = tiles[start + u]
            leaf = packed >> 16
            first = (packed >> 8) & 255
            second = packed & 255
            matrix = jnp.concatenate([cols[first], cols[second]], axis=1)
            load = jnp.concatenate([loads[first], loads[second]], axis=1)
            values.append(jnp.exp(dot(rows[leaf], matrix)).astype(bf16))
            weights.append(placed(load, leaf & 7))
        acc[...] += dot_nt(jnp.concatenate(values, axis=1), jnp.concatenate(weights, axis=1))

    acc[...] = jnp.zeros_like(acc)
    for k in range(n_ids):
        list_pairs(codes[k], lists[PHASES * k : PHASES * k + PHASES])
    for copy in copies:
        copy.wait()
    largest = STEPS[0]
    whole = lax.div(count, largest)

    def full_step(i, carry):
        step(i * largest, largest)
        return carry

    lax.fori_loop(0, whole, full_step, 0)
    for size in STEPS[1:]:

        @pl.when((count & size) > 0)
        def _(size=size):
            step(count & ~(2 * size - 1), size)


def list_pairs(codes, tables):
    per_leaf, leaves = codes.shape
    for g in range(leaves // 8):
        counts = [jnp.int32(0)] * len(tables)
        for j in range(8):
            for u in range(per_leaf):
                value = codes[u, g * 8 + j]
                for p, table in enumerate(tables):
                    if table is None:
                        continue
                    table[g, 1 + counts[p]] = value & CODE
                    counts[p] = counts[p] + ((value >> (PHASE_BIT + p)) & 1)
        for p, table in enumerate(tables):
            if table is None:
                continue
            table[g, 1 + counts[p]] = DUMMY
            table[g, 0] = (counts[p] + 1) & ~1


def pair_table(leaves):
    return jax.ShapeDtypeStruct((leaves // 8, 128), jnp.int32)


def self_and_far(codes, far_list, far_count, cols, loads, rows, call, calls):
    leaves = rows.shape[0]
    width = far_list.shape[1]
    n_leaves = leaves // calls
    out = pl.pallas_call(
        functools.partial(
            far_kernel, first_leaf=call * n_leaves, n_leaves=n_leaves, n_ids=len(codes)
        ),
        out_shape=(jax.ShapeDtypeStruct((256, 128), f32),) + (pair_table(leaves),) * (PHASES * len(codes)),
        in_specs=[SMEM] * (2 + len(codes)) + [ANY] * 3,
        out_specs=(VMEM,) + (SMEM,) * (PHASES * len(codes)),
        scratch_shapes=[
            pltpu.VMEM(cols.shape, bf16),
            pltpu.VMEM(loads.shape, bf16),
            pltpu.VMEM(rows.shape, bf16),
            pltpu.SMEM((n_leaves * (1 + width // 2) + 2,), jnp.int32),
            pltpu.SemaphoreType.DMA((4,)),
        ],
        compiler_params=params(FIRST_LIMIT),
        cost_estimate=cost(),
        name=f"self_and_far{call}",
    )(*codes, far_list, far_count, cols, loads, rows)
    return out[0], [out[1 + PHASES * k : 1 + PHASES * k + PHASES] for k in range(len(codes))]


def near_kernel(*refs, n_sources, n_targets, n_lists, n_codes, n_before, phase):
    refs = list(refs)

    def take(n):
        taken = refs[:n]
        del refs[:n]
        return taken

    makes = phase < PHASES - 1
    codes = take(n_codes)
    lists = take(n_lists)
    target_parts = take(n_targets)
    source_parts = take(n_sources)
    before = take(n_before)
    outs = take(n_targets) if not makes else []
    (acc,) = take(1) if makes else (None,)
    tables = [take(PHASES - 1 - phase) for _ in range(n_codes)]
    sources, sems, pairs, steps, targets = take(5)
    if not makes:
        (acc,) = take(1)
    leaves = source_parts[0].shape[0]
    size = leaves * 128
    copies = []

    def begin(part, place):
        copies.append(pltpu.make_async_copy(part, place, sems.at[len(copies)]))
        copies[-1].start()

    own_rows = acc.shape[0] // n_targets
    for k, part in enumerate(lists):
        begin(part, pairs.at[pl.ds(k * own_rows, own_rows)])
    for k, part in enumerate(target_parts):
        begin(part.at[pl.ds(0, size)], targets.at[pl.ds(k * size, size)])
    for k, part in enumerate(source_parts):
        begin(part.at[pl.ds(0, leaves)], sources.at[pl.ds(k * leaves, leaves)])
    acc[...] = jnp.zeros_like(acc)
    for k in range(n_codes):
        table = pairs.at[pl.ds((n_lists + k) * own_rows, own_rows)]
        list_pairs(codes[k], [None] * phase + [table] + tables[k])
    for copy in copies:
        copy.wait()

    counts = [jnp.int32(0)] * len(STEPS)
    for row in range(pairs.shape[0]):
        used = pairs[row, 0]
        whole = lax.div(used, STEPS[0])

        def note(i, count, row=row):
            steps[0, count + i] = row * 128 + 1 + i * STEPS[0]
            return count

        lax.fori_loop(0, whole, note, counts[0])
        counts[0] = counts[0] + whole
        for k, size in enumerate(STEPS[1:], 1):
            steps[k, counts[k]] = row * 128 + 1 + (used & ~(2 * size - 1))
            counts[k] = counts[k] + jnp.where((used & size) > 0, 1, 0)

    for k, size in enumerate(STEPS):

        def step(i, carry, k=k, size=size):
            group = steps[k, i] >> 7
            start = steps[k, i] & 127

            def exponent(u):
                packed = pairs[group, start + u]
                target = (packed >> 16) & 7
                coords = sources[packed & 65535, :64, :]
                odd = target & 1
                zero = jnp.zeros_like(coords)
                matrix = jnp.concatenate(
                    [jnp.where(odd == 0, coords, zero), jnp.where(odd == 1, coords, zero)],
                    axis=0,
                )
                at = pl.multiple_of(group * 1024 + (target >> 1) * 256, 256)
                return dot(targets[pl.ds(at, 256), :], matrix) - norm_row(coords)

            def weight(u):
                packed = pairs[group, start + u]
                place = jnp.where(packed < DUMMY, (packed >> 16) & 7, 8)
                return placed(sources[packed & 65535, 64:, :], place)

            acc[group] += tiles_sum(size, exponent, weight)
            return carry

        lax.fori_loop(0, counts[k], step, 0)

    if makes:
        for part in before:
            acc[: part.shape[0]] += part[...]
    earlier = [(part, at) for part in before for at in range(0, part.shape[0], own_rows)]
    for k, out in enumerate(outs):
        mine = slice(k * own_rows, (k + 1) * own_rows)
        part, at = earlier[k]
        out[...] = (acc[mine] + part[at : at + own_rows]).astype(bf16)


def near(phase, lists, targets, sources, codes=(), before=()):
    n_sources, n_codes, n_targets = len(sources), len(codes), len(targets)
    makes = phase < PHASES - 1
    leaves = min(source.shape[0] for source in sources)
    sums = jax.ShapeDtypeStruct((n_targets * leaves // 8, 256, 128), f32)
    part = jax.ShapeDtypeStruct((leaves // 8, 256, 128), bf16)
    args = list(codes) + list(lists) + list(targets) + list(sources)
    in_specs = [SMEM] * n_codes + [ANY] * (len(args) - n_codes)
    args += list(before)
    in_specs += [VMEM] * len(before)
    if makes:
        n_tables = n_codes * (PHASES - 1 - phase)
        out_shape = (sums,) + (pair_table(leaves),) * n_tables
        out_specs = (VMEM,) + (SMEM,) * n_tables
    else:
        out_shape, out_specs = (part,) * n_targets, (VMEM,) * n_targets
    scratch = [
        pltpu.VMEM((n_sources * leaves, 80, 256), bf16),
        pltpu.SemaphoreType.DMA((n_sources + n_targets + len(lists),)),
        pltpu.SMEM((n_targets * leaves // 8, 128), jnp.int32),
        pltpu.SMEM((len(STEPS), n_targets * leaves), jnp.int32),
        pltpu.VMEM((n_targets * leaves * 128, 128), bf16),
    ]
    if not makes:
        scratch.append(pltpu.VMEM(sums.shape, f32))
    return pl.pallas_call(
        functools.partial(
            near_kernel,
            n_sources=n_sources,
            n_targets=n_targets,
            n_lists=len(lists),
            n_codes=n_codes,
            n_before=len(before),
            phase=phase,
        ),
        out_shape=out_shape,
        in_specs=in_specs,
        out_specs=out_specs,
        scratch_shapes=scratch,
        compiler_params=params(),
        cost_estimate=cost(),
        name=f"near{phase}",
    )(*args)


def ordered(first, second, test):
    return jnp.where(test, first, second), jnp.where(test, second, first)


def climb_kernel(me, own, other, skels, interps, parent, *, height, row):
    sibling = other[0, :, :128] if len(other.shape) == 3 else other[...]
    left, right = ordered(own[0, :, :128] if len(own.shape) == 3 else own[...], sibling, ((me[0] >> height) & 1) == 0)
    parent[...] = combine(left, right, skels[row], interps[row])


def last_block(value):
    if value.ndim == 2:
        return VMEM
    blocks = value.shape[0]
    return pl.BlockSpec((1,) + value.shape[1:], lambda i: (blocks - 1, 0, 0))


def climb(me, own, other, skels, interps, height, row):
    return pl.pallas_call(
        functools.partial(climb_kernel, height=height, row=row),
        grid=(1,),
        out_shape=jax.ShapeDtypeStruct((80, 128), bf16),
        in_specs=[SMEM, last_block(own), last_block(other), VMEM, VMEM],
        out_specs=VMEM,
        compiler_params=params(),
        cost_estimate=cost(),
        name=f"climb{height}",
    )(me, own, other, skels, interps)


def climb_two_kernel(me, own, one, two, three, skels, interps, sibling, parent, *, height, row):
    node = me[0] >> height
    is_left = (node & 1) == 0
    left, right = ordered(own[...], one[...], is_left)
    mine = combine(left, right, skels[row], interps[row])
    left, right = ordered(two[...], three[...], is_left)
    other = combine(left, right, skels[row + 1], interps[row + 1])
    sibling[...] = other
    left, right = ordered(mine, other, (node & 2) == 0)
    parent[...] = combine(left, right, skels[row + 2], interps[row + 2])


def climb_two(me, own, others, skels, interps, height, row):
    node = jax.ShapeDtypeStruct((80, 128), bf16)
    return pl.pallas_call(
        functools.partial(climb_two_kernel, height=height, row=row),
        out_shape=(node, node),
        in_specs=[SMEM] + [VMEM] * 6,
        out_specs=(VMEM, VMEM),
        compiler_params=params(),
        cost_estimate=cost(),
        name=f"climb{height}",
    )(me, own, *others, skels, interps)


def top_kernel(*refs):
    parts, (rows, acc, cols, loads) = refs[:-4], refs[-4:]
    for t, part in enumerate(parts):
        node = part[0, :, :128] if len(part.shape) == 3 else part[...]
        cols[:, t * 128 : (t + 1) * 128] = source_matrix(node[:64], norm_row(node[:64]))
        loads[:, t * 128 : (t + 1) * 128] = jnp.concatenate([node[64:]] * 8, axis=0)
    lane = lax.broadcasted_iota(jnp.int32, (256, 128), 1) >> 4

    def two_leaves(i, carry):
        both = rows[pl.ds(2 * i, 2)].reshape(512, 128)
        value = jnp.exp(dot(both, cols[...])).astype(bf16)
        result = dot_nt(value, loads[...])
        group = lax.div(i, 4)
        place = (2 * i) & 7
        acc[group] += jnp.where(lane == place, result[:256], 0.0) + jnp.where(
            lane == place + 1, result[256:], 0.0
        )
        return carry

    acc[...] = jnp.zeros_like(acc)
    lax.fori_loop(0, rows.shape[0] // 2, two_leaves, 0, unroll=2)


def top(parts, rows):
    levels = len(parts)
    return pl.pallas_call(
        top_kernel,
        out_shape=jax.ShapeDtypeStruct((rows.shape[0] // 8, 256, 128), f32),
        grid=(1,),
        in_specs=[last_block(part) for part in parts] + [VMEM],
        out_specs=VMEM,
        scratch_shapes=[
            pltpu.VMEM((128, levels * 128), bf16),
            pltpu.VMEM((128, levels * 128), bf16),
        ],
        compiler_params=params(),
        cost_estimate=cost(),
        name="top",
    )(*parts, rows)


def last_kernel(*refs, n_far):
    fars = refs[:n_far]
    above, norms = refs[n_far : n_far + 2]
    received, out = refs[n_far + 2 : -1], refs[-1]
    groups = above.shape[0]
    for group in range(groups):
        local = above[group]
        for far in fars[group * n_far // groups : (group + 1) * n_far // groups]:
            local = local + far[...]
        local = jnp.transpose(local)
        total = received[0][group].astype(f32)
        for part in received[1:]:
            total = total + part[group].astype(f32)
        total = jnp.transpose(total)
        for j in range(8):
            leaf = group * 8 + j
            rows = slice(16 * j, 16 * j + 16)
            out[:, leaf * 256 : (leaf + 1) * 256] = local[rows] + total[rows] * jnp.exp(-norms[leaf])


def last(fars, above, norms, received):
    return pl.pallas_call(
        functools.partial(last_kernel, n_far=len(fars)),
        out_shape=jax.ShapeDtypeStruct((16, norms.shape[0] * 256), f32),
        in_specs=[VMEM] * (2 + len(fars) + len(received)),
        out_specs=VMEM,
        compiler_params=params(),
        cost_estimate=cost(),
        name="last_sum",
    )(*fars, above, norms, *received)


def swap(value, mask):
    pairs = [(d, d ^ mask) for d in range(lax.axis_size("leaf"))]
    return lax.ppermute(value, "leaf", pairs)


def after(value, *others):
    return lax.optimization_barrier((value,) + others)[0]


def shards(
    points,
    charges,
    leaf_order,
    near_owner,
    near_slot,
    far_list,
    far_count,
    leaf_interp,
    leaf_skel,
    inner_interp,
    inner_skel,
    top_interp,
    top_skel,
):
    device_count = lax.axis_size("leaf")
    bits = device_count.bit_length() - 1
    source_bits = tuple(b for b in range(bits) if b not in TARGET_BITS)
    outer_bits = source_bits[1:]
    device = lax.axis_index("leaf")
    leaves = near_owner.shape[0]
    me = device.reshape(1).astype(jnp.int32)
    mates = range(1, 2 ** len(TARGET_BITS))
    early_bits = outer_bits[:-1]
    late = 2 ** outer_bits[-1]

    def payload_codes(payload, first):
        near = payload[-2 * near_owner.shape[1] :, :leaves].astype(jnp.int32)
        return codes_of(near[: near_owner.shape[1]], near[near_owner.shape[1] :], first, leaves)

    owner, slot = near_owner.T, near_slot.T
    src, tgt, cols, loads, rows, norms, mine, interps, skels, codes = first_part(
        points, charges, leaf_order, owner, slot,
        leaf_interp, leaf_skel, inner_interp, inner_skel, top_interp, top_skel,
    )
    pieces = {0: src, late: swap(src, late)}
    for b in reversed(early_bits):
        pieces[2**b] = swap(src, 2**b)
    beside = swap(tgt, 2 ** TARGET_BITS[0])
    far_away = swap(tgt, 2 ** TARGET_BITS[1])
    pieces[1] = swap(mine, 1)

    def far(call, codes, token):
        return self_and_far(
            codes, after(far_list, token), far_count, cols, loads, rows, call, 2
        )

    far0, lists0 = far(0, [codes], norms)
    node = climb(me, after(mine, far0), pieces[1], skels, interps, 0, 0)
    siblings = [pieces[1], swap(node, 2)]
    far1, _ = far(1, [], node)
    for n, b in enumerate(early_bits):
        for low in range(2**n):
            place = spread(low, early_bits[:n])
            if low:
                pieces[place | 2**b] = swap(pieces[place], 2**b)
    wanted = [spread(k, source_bits) for k in range(2 ** (len(source_bits) - 1))]
    lists = lists0
    node = climb(me, node, after(siblings[1], far1), skels, interps, 1, 1)
    sums, *tables = near(
        0,
        [lists[0][0]],
        [tgt, beside],
        [pieces[k] for k in wanted if k == 1 or not k & 1],
        codes=[payload_codes(after(beside, far1, node), 0)],
    )
    last_targets = swap(after(far_away, sums), 2 ** TARGET_BITS[0])
    for k in wanted[2::2]:
        pieces[k | 1] = swap(after(pieces[k], sums), 1)
    pieces[late] = after(pieces[late], sums)
    for n, b in enumerate(early_bits):
        for low in range(2**n):
            place = spread(low, early_bits[:n]) | late
            pieces[place | 2**b] = swap(pieces[place], 2**b)
    pieces[late | 1] = swap(pieces[late], 1)
    present = [pieces[k] for k in wanted + [late, late | 1]]
    sums, *far_tables = near(
        1,
        [lists[0][1], tables[0]],
        [tgt, beside, far_away],
        present,
        codes=[payload_codes(after(far_away, node, sums), 1)],
        before=[sums],
    )
    height, row = 2, 2
    node = after(node, sums)
    others = [swap(node, k * 2**height) for k in (1, 2, 3)]
    last_sums, last_table = near(
        2, [], [last_targets], present, codes=[payload_codes(after(last_targets, sums), 2)]
    )
    others[0] = after(others[0], last_sums)
    while height + 1 < bits:
        if height > 2:
            others = [swap(node, k * 2**height) for k in (1, 2, 3)]
        sibling, node = climb_two(me, node, others, skels, interps, height, row)
        siblings += [others[0], sibling]
        height, row = height + 2, row + 3
    if height < bits:
        siblings.append(swap(node, 2**height))
    for k in wanted[2::2]:
        pieces[k | late | 1] = swap(after(pieces[k | late], node), 1)
    parts = near(
        3,
        [lists[0][3], tables[2], far_tables[1], last_table],
        [tgt, beside, far_away, last_targets],
        [pieces[k | late] for k in wanted[2:]],
        before=[sums, last_sums],
    )
    siblings[-1] = after(siblings[-1], parts[0])
    received = [parts[0]] + [
        swap(after(parts[k], siblings[-1]), spread(k, TARGET_BITS)) for k in mates
    ]
    above = top(siblings, after(rows, parts[0]))
    return last((far0, far1), above, norms, received)


def solution(mesh):
    in_specs = (
        P(None, "leaf"),
        P(None, "leaf"),
        P("leaf"),
        P("leaf", None),
        P("leaf", None),
        P("leaf", None),
        P("leaf"),
        P("leaf", None, None),
        P("leaf", None),
        P("leaf", None, None),
        P("leaf", None),
        P(),
        P(),
    )
    out_specs = P(None, "leaf")
    return jax.shard_map(shards, mesh=mesh, in_specs=in_specs, out_specs=out_specs, check_vma=False)
```
